32 devices in a mesh: dp: 8 (over z, y), fsdp: 4 (over x, core).
Axes of the slice: x: 2, y: 2, z: 4, core: 2. Of those that a mesh axis runs over, the one named last changes fastest.
Arguments:
- points: float32 [3, 256, 1024], P(None, ('dp', 'fsdp')), may hold values from -6 to 6
- centers: int32 [256, 64], P(('dp', 'fsdp')), may hold values from 0 to 1023
- neighbours: int32 [256, 2048], P(('dp', 'fsdp')), may hold values from 0 to 1023
- mask: int32 [256, 64], P(('dp', 'fsdp')), may hold values from 0 to 1, as said below
- targets: int32 [256, 64], P(('dp', 'fsdp')), may hold values from 0 to 8191
- embed_in: float32 [2, 3, 128], P(None, None, 'fsdp'), may hold values from -3.5 to 3.5
- embed_in_m: float32 [2, 3, 128], P(None, None, 'fsdp'), may hold values from -1.4305115e-06 to 1.4305115e-06
- embed_in_v: float32 [2, 3, 128], P(None, None, 'fsdp'), may hold values from 2.5916072e-13 to 1.0366429e-12
- embed_out: float32 [2, 128, 384], P(None, 'fsdp'), may hold values from -0.5 to 0.5
- embed_out_m: float32 [2, 128, 384], P(None, 'fsdp'), may hold values from -1.4305115e-06 to 1.4305115e-06
- embed_out_v: float32 [2, 128, 384], P(None, 'fsdp'), may hold values from 2.5916072e-13 to 1.0366429e-12
- qkv_w: float32 [1, 384, 1152], P(None, 'fsdp'), may hold values from -0.3125 to 0.3125
- qkv_m: float32 [1, 384, 1152], P(None, 'fsdp'), may hold values from -1.4305115e-06 to 1.4305115e-06
- qkv_v: float32 [1, 384, 1152], P(None, 'fsdp'), may hold values from 2.5916072e-13 to 1.0366429e-12
- proj_w: float32 [1, 384, 384], P(None, 'fsdp'), may hold values from -2.5 to 2.5
- proj_m: float32 [1, 384, 384], P(None, 'fsdp'), may hold values from -1.4305115e-06 to 1.4305115e-06
- proj_v: float32 [1, 384, 384], P(None, 'fsdp'), may hold values from 2.5916072e-13 to 1.0366429e-12
- fc1_w: float32 [1, 384, 1536], P(None, 'fsdp'), may hold values from -0.3125 to 0.3125
- fc1_m: float32 [1, 384, 1536], P(None, 'fsdp'), may hold values from -1.4305115e-06 to 1.4305115e-06
- fc1_v: float32 [1, 384, 1536], P(None, 'fsdp'), may hold values from 2.5916072e-13 to 1.0366429e-12
- fc2_w: float32 [1, 1536, 384], P(None, 'fsdp'), may hold values from -0.15625 to 0.15625
- fc2_m: float32 [1, 1536, 384], P(None, 'fsdp'), may hold values from -1.4305115e-06 to 1.4305115e-06
- fc2_v: float32 [1, 1536, 384], P(None, 'fsdp'), may hold values from 2.5916072e-13 to 1.0366429e-12
- gains: float32 [3, 384], P(None, 'fsdp'), may hold values from 0.3 to 2.5
- gains_m: float32 [3, 384], P(None, 'fsdp'), may hold values from -5.722046e-06 to 5.722046e-06
- gains_v: float32 [3, 384], P(None, 'fsdp'), may hold values from 4.1864424e-12 to 1.674577e-11
- special: float32 [2, 384], P(None, 'fsdp'), may hold values from -6 to 6
- special_m: float32 [2, 384], P(None, 'fsdp'), may hold values from -5.722046e-06 to 5.722046e-06
- special_v: float32 [2, 384], P(None, 'fsdp'), may hold values from 4.1864424e-12 to 1.674577e-11
- head: float32 [384, 8192], P('fsdp'), may hold values from -0.3125 to 0.3125
- head_m: float32 [384, 8192], P('fsdp'), may hold values from -1.4305115e-06 to 1.4305115e-06
- head_v: float32 [384, 8192], P('fsdp'), may hold values from 2.5916072e-13 to 1.0366429e-12
Outputs:
- embed_in_m_new: float32 [2, 3, 128], P(None, None, 'fsdp')
- embed_in_v_new: float32 [2, 3, 128], P(None, None, 'fsdp')
- embed_in_new: float32 [2, 3, 128], P(None, None, 'fsdp')
- embed_out_m_new: float32 [2, 128, 384], P(None, 'fsdp')
- embed_out_v_new: float32 [2, 128, 384], P(None, 'fsdp')
- embed_out_new: float32 [2, 128, 384], P(None, 'fsdp')
- qkv_m_new: float32 [1, 384, 1152], P(None, 'fsdp')
- qkv_v_new: float32 [1, 384, 1152], P(None, 'fsdp')
- qkv_new: float32 [1, 384, 1152], P(None, 'fsdp')
- proj_m_new: float32 [1, 384, 384], P(None, 'fsdp')
- proj_v_new: float32 [1, 384, 384], P(None, 'fsdp')
- proj_new: float32 [1, 384, 384], P(None, 'fsdp')
- fc1_m_new: float32 [1, 384, 1536], P(None, 'fsdp')
- fc1_v_new: float32 [1, 384, 1536], P(None, 'fsdp')
- fc1_new: float32 [1, 384, 1536], P(None, 'fsdp')
- fc2_m_new: float32 [1, 1536, 384], P(None, 'fsdp')
- fc2_v_new: float32 [1, 1536, 384], P(None, 'fsdp')
- fc2_new: float32 [1, 1536, 384], P(None, 'fsdp')
- gains_m_new: float32 [3, 384], P(None, 'fsdp')
- gains_v_new: float32 [3, 384], P(None, 'fsdp')
- gains_new: float32 [3, 384], P(None, 'fsdp')
- special_m_new: float32 [2, 384], P(None, 'fsdp')
- special_v_new: float32 [2, 384], P(None, 'fsdp')
- special_new: float32 [2, 384], P(None, 'fsdp')
- head_m_new: float32 [384, 8192], P('fsdp')
- head_v_new: float32 [384, 8192], P('fsdp')
- head_new: float32 [384, 8192], P('fsdp')
- loss_sum: float32 [], replicated
- hidden_count: float32 [], replicated
- grad_norm: float32 [], replicated
The draws below stay inside these ranges and needn't reach their ends.
Inputs may be any that keep to these rules, and one draw needn't show every extreme that they name: Each cloud masks at least 8 and at most 36 of its patches; clouds of higher index mask more on average.
All inputs are finite; a program needn't handle non-finite values.
Results may differ from the reference program's by a relative error of at most 0.009.
Values may be sent and summed in bfloat16 or wider, within the bound.
No kernel may reach another device: no remote copies, remote signals or barrier semaphores. Data moves between devices by JAX's collectives and lax.ppermute only.
A program may use at most 256 MiB of HBM per device.

```python
import math
import jax
import jax.numpy as jnp
import numpy as np
from jax import lax

D = 384
HEADS = 6
HEAD_DIM = 64
FF = 1536
PE = 128
V = 8192
NB = 32
POINTS = 1024
PATCHES = 64
LAYERS = 1
STEP_NUMBER = 10
CLOUDS = 256
PARAMS = 5016192


def draw_mask(key, part):
    key = jax.random.fold_in(key, 11)
    order = jnp.arange(CLOUDS, dtype=jnp.int32)
    extra = jax.random.randint(jax.random.fold_in(key, 1), (CLOUDS,), 0, PATCHES // 16 + 2)
    hidden = PATCHES // 8 + order * (PATCHES * 3 // 8) // CLOUDS + extra
    ranks = jax.vmap(lambda sub: jax.random.permutation(sub, PATCHES))(jax.random.split(key, CLOUDS))
    return (ranks < hidden[:, None]).astype(jnp.int32)


def draw_gains(key, part):
    key = jax.random.fold_in(key, 23)
    column = jnp.arange(D, dtype=jnp.float32) / (D - 1)
    ramp = 0.6 + 1.2 * column
    noise = jax.random.uniform(key, (2 * LAYERS + 1, D), jnp.float32, 0.8, 1.25)
    return ramp * noise


def set_ends(result, own_key, least, largest):
    dims = result.shape
    spot = [jax.random.randint(jax.random.fold_in(own_key, axis), (), 0, dims[axis]) for axis in range(len(dims))]
    result = result.at[tuple(spot)].set(least)
    longest = dims.index(max(dims))
    spot[longest] = (spot[longest] + 1) % dims[longest]
    return result.at[tuple(spot)].set(largest)


def block_levels(own_key, extent, cuts, low, largest):
    def one(position, shards_of):
        steps = jax.random.uniform(jax.random.fold_in(jax.random.fold_in(own_key, 6), position), (shards_of,), jnp.float32, low / len(cuts), largest / len(cuts))
        return jnp.repeat(jnp.exp(steps), extent[position] // shards_of).reshape((-1,) + (1,) * (len(extent) - position - 1))

    level = one(*cuts[0])
    for cut in cuts[1:]:
        level = level * one(*cut)
    return level


def cumulative_ranks(count, slope):
    portions = [(1 << 20) // math.isqrt(rank ** slope) + 1 for rank in range(1, count + 1)]
    scale = 1 + sum(portions) // (1 << 30)
    return np.cumsum(np.array([max(1, weight // scale) for weight in portions]))


def ranked(own_key, extent, amount, slope):
    grid = cumulative_ranks(amount, slope)
    ticket = jax.random.randint(jax.random.fold_in(own_key, 1), extent, 0, int(grid[amount - 1]))
    rank = jnp.searchsorted(jnp.asarray(grid, jnp.int32), ticket, side="right")
    return jax.random.permutation(jax.random.fold_in(own_key, 2), amount)[rank].astype(jnp.int32)


def scatter_about(own_key, extent, spread, limit, cuts=(), held_as=jnp.bfloat16):
    loudness = block_levels(own_key, extent, cuts, -0.22, 0.18) if cuts else 1.0
    entries = jax.random.normal(own_key, extent, jnp.float32) * spread * loudness
    return jnp.minimum(jnp.maximum(entries, -limit), limit).astype(held_as)


def setup_inputs(seed: int = 0) -> dict:
    streams_of = jax.random.split(jax.random.key(seed), 33)
    return {
        "points": scatter_about(streams_of[0], (3, CLOUDS, POINTS), 1.0, 6.0, ((1, 32),), jnp.float32),
        "centers": set_ends(jax.random.randint(streams_of[1], (CLOUDS, PATCHES), 0, POINTS), jax.random.fold_in(streams_of[1], 1), 0, POINTS - 1).astype(jnp.int32),
        "neighbours": set_ends(jax.random.randint(streams_of[2], (CLOUDS, PATCHES * NB), 0, POINTS), jax.random.fold_in(streams_of[2], 1), 0, POINTS - 1).astype(jnp.int32),
        "mask": draw_mask(jax.random.fold_in(streams_of[32], 71), 0),
        "targets": set_ends(ranked(streams_of[4], (CLOUDS, PATCHES), V, 2), jax.random.fold_in(streams_of[4], 3), 0, V - 1).astype(jnp.int32),
        "embed_in": scatter_about(streams_of[5], (2, 3, PE), 3 ** -0.5, 3.5, ((2, 4),), jnp.float32),
        "embed_in_m": scatter_about(streams_of[6], (2, 3, PE), (0.00055 * PARAMS ** -0.5), 1.430511474609375e-06, ((2, 4),), jnp.float32),
        "embed_in_v": jnp.clip(jnp.exp(math.log(1.036642885247907e-12) - 1.3862944 * jax.random.uniform(streams_of[7], (2, 3, PE), jnp.float32) ** block_levels(streams_of[7], (2, 3, PE), ((2, 4),), -0.2, 0.2)), 2.5916072131197676e-13, 1.036642885247907e-12),
        "embed_out": scatter_about(streams_of[8], (2, PE, D), PE ** -0.5, 0.5, ((1, 4),), jnp.float32),
        "embed_out_m": scatter_about(streams_of[9], (2, PE, D), (0.00055 * PARAMS ** -0.5), 1.430511474609375e-06, ((1, 4),), jnp.float32),
        "embed_out_v": jnp.clip(jnp.exp(math.log(1.036642885247907e-12) - 1.3862944 * jax.random.uniform(streams_of[10], (2, PE, D), jnp.float32) ** block_levels(streams_of[10], (2, PE, D), ((1, 4),), -0.2, 0.2)), 2.5916072131197676e-13, 1.036642885247907e-12),
        "qkv_w": scatter_about(streams_of[11], (LAYERS, D, 3 * D), D ** -0.5, 0.3125, ((1, 4),), jnp.float32),
        "qkv_m": scatter_about(streams_of[12], (LAYERS, D, 3 * D), (0.00055 * PARAMS ** -0.5), 1.430511474609375e-06, ((1, 4),), jnp.float32),
        "qkv_v": jnp.clip(jnp.exp(math.log(1.036642885247907e-12) - 1.3862944 * jax.random.uniform(streams_of[13], (LAYERS, D, 3 * D), jnp.float32) ** block_levels(streams_of[13], (LAYERS, D, 3 * D), ((1, 4),), -0.2, 0.2)), 2.5916072131197676e-13, 1.036642885247907e-12),
        "proj_w": scatter_about(streams_of[14], (LAYERS, D, D), (max(D // 64, 1)) ** -0.5, 2.5, ((1, 4),), jnp.float32),
        "proj_m": scatter_about(streams_of[15], (LAYERS, D, D), (0.00055 * PARAMS ** -0.5), 1.430511474609375e-06, ((1, 4),), jnp.float32),
        "proj_v": jnp.clip(jnp.exp(math.log(1.036642885247907e-12) - 1.3862944 * jax.random.uniform(streams_of[16], (LAYERS, D, D), jnp.float32) ** block_levels(streams_of[16], (LAYERS, D, D), ((1, 4),), -0.2, 0.2)), 2.5916072131197676e-13, 1.036642885247907e-12),
        "fc1_w": scatter_about(streams_of[17], (LAYERS, D, FF), D ** -0.5, 0.3125, ((1, 4),), jnp.float32),
        "fc1_m": scatter_about(streams_of[18], (LAYERS, D, FF), (0.00055 * PARAMS ** -0.5), 1.430511474609375e-06, ((1, 4),), jnp.float32),
        "fc1_v": jnp.clip(jnp.exp(math.log(1.036642885247907e-12) - 1.3862944 * jax.random.uniform(streams_of[19], (LAYERS, D, FF), jnp.float32) ** block_levels(streams_of[19], (LAYERS, D, FF), ((1, 4),), -0.2, 0.2)), 2.5916072131197676e-13, 1.036642885247907e-12),
        "fc2_w": scatter_about(streams_of[20], (LAYERS, FF, D), FF ** -0.5, 0.15625, ((1, 4),), jnp.float32),
        "fc2_m": scatter_about(streams_of[21], (LAYERS, FF, D), (0.00055 * PARAMS ** -0.5), 1.430511474609375e-06, ((1, 4),), jnp.float32),
        "fc2_v": jnp.clip(jnp.exp(math.log(1.036642885247907e-12) - 1.3862944 * jax.random.uniform(streams_of[22], (LAYERS, FF, D), jnp.float32) ** block_levels(streams_of[22], (LAYERS, FF, D), ((1, 4),), -0.2, 0.2)), 2.5916072131197676e-13, 1.036642885247907e-12),
        "gains": draw_gains(jax.random.fold_in(streams_of[32], 71), 0),
        "gains_m": scatter_about(streams_of[24], (2 * LAYERS + 1, D), (0.0022 * PARAMS ** -0.5), 5.7220458984375e-06, ((1, 4),), jnp.float32),
        "gains_v": jnp.clip(jnp.exp(math.log(1.6745769701453916e-11) - 1.3862944 * jax.random.uniform(streams_of[25], (2 * LAYERS + 1, D), jnp.float32) ** block_levels(streams_of[25], (2 * LAYERS + 1, D), ((1, 4),), -0.2, 0.2)), 4.186442425363479e-12, 1.6745769701453916e-11),
        "special": scatter_about(streams_of[26], (2, D), 1.0, 6.0, ((1, 4),), jnp.float32),
        "special_m": scatter_about(streams_of[27], (2, D), (0.0022 * PARAMS ** -0.5), 5.7220458984375e-06, ((1, 4),), jnp.float32),
        "special_v": jnp.clip(jnp.exp(math.log(1.6745769701453916e-11) - 1.3862944 * jax.random.uniform(streams_of[28], (2, D), jnp.float32) ** block_levels(streams_of[28], (2, D), ((1, 4),), -0.2, 0.2)), 4.186442425363479e-12, 1.6745769701453916e-11),
        "head": scatter_about(streams_of[29], (D, V), D ** -0.5, 0.3125, ((0, 4),), jnp.float32),
        "head_m": scatter_about(streams_of[30], (D, V), (0.00055 * PARAMS ** -0.5), 1.430511474609375e-06, ((0, 4),), jnp.float32),
        "head_v": jnp.clip(jnp.exp(math.log(1.036642885247907e-12) - 1.3862944 * jax.random.uniform(streams_of[31], (D, V), jnp.float32) ** block_levels(streams_of[31], (D, V), ((0, 4),), -0.2, 0.2)), 2.5916072131197676e-13, 1.036642885247907e-12),
    }


@jax.custom_vjp
def low(v):
    return lax.optimization_barrier(v.astype(jnp.bfloat16)).astype(jnp.float32)

@jax.custom_vjp
def low_back(v):
    return v

def low_keep(v):
    return (low(v), None)

def low_pass(kept, grad):
    return (grad,)

def back_keep(v):
    return (v, None)

def back_low(kept, grad):
    return (low(grad),)
low.defvjp(low_keep, low_pass)
low_back.defvjp(back_keep, back_low)
HIGHEST = lax.Precision.HIGHEST
BETA_ONE = 0.9
BETA_TWO = 0.95
EPSILON = 1e-08
DECAY = 0.05
RATE_MATRIX = 0.1
RATE_VECTOR = 0.5
CLIP = 0.005

def matmul(left, right):
    return low_back(jnp.matmul(low(left), low(right), precision=HIGHEST))

def layer_norm(stream, gain):
    centred = stream - lax.optimization_barrier(jnp.mean(stream, -1, keepdims=True))
    return centred * lax.rsqrt(lax.optimization_barrier(jnp.mean(centred * centred, -1, keepdims=True)) + 1e-06) * gain

def pick_points(points, index):
    return jnp.stack([jnp.take_along_axis(points[comp], index, axis=1) for comp in range(3)], -1)

def block(stream, w_qkv, w_proj, w_fc1, w_fc2, gain_attn, gain_ffn):
    clouds, length = (stream.shape[0], stream.shape[1])
    packed = matmul(layer_norm(stream, gain_attn), w_qkv).reshape(clouds, length, 3, HEADS, HEAD_DIM)
    queries = low(packed[:, :, 0])
    key_rows = low(packed[:, :, 1])
    value_rows = low(packed[:, :, 2])
    scores = low_back(jnp.einsum('cqhd,ckhd->chqk', queries, key_rows, precision=HIGHEST)) * HEAD_DIM ** (-0.5)
    attend = jax.nn.softmax(scores, -1)
    mixed = low_back(jnp.einsum('chqk,ckhd->cqhd', low(attend), value_rows, precision=HIGHEST))
    middle = stream + matmul(mixed.reshape(clouds, length, D), w_proj)
    return middle + matmul(jax.nn.gelu(matmul(layer_norm(middle, gain_ffn), w_fc1)), w_fc2)

def forward(params, points, centers, neighbours, mask, targets):
    embed_in, embed_out, qkv_w, proj_w, fc1_w, fc2_w, gains, special, head = params
    gains = low(gains)
    special = low(special)
    clouds = mask.shape[0]
    centre = pick_points(points, centers)
    relative = pick_points(points, neighbours).reshape(clouds, PATCHES, NB, 3) - centre[:, :, None, :]
    inner = jax.nn.gelu(matmul(relative, embed_in[0]))
    patch = lax.optimization_barrier(jnp.mean(jax.nn.gelu(matmul(inner, embed_out[0])), 2))
    place = matmul(jax.nn.gelu(matmul(centre, embed_in[1])), embed_out[1])
    tokens = jnp.where(mask[:, :, None] > 0, special[1], patch) + place
    stream = jnp.concatenate([jnp.broadcast_to(special[0], (clouds, 1, D)), tokens], 1)
    for layer in range(LAYERS):
        stream = block(stream, qkv_w[layer], proj_w[layer], fc1_w[layer], fc2_w[layer], gains[2 * layer], gains[2 * layer + 1])
    logits = matmul(layer_norm(stream[:, 1:], gains[2 * LAYERS]), head)
    total = jax.nn.logsumexp(logits, -1)
    chosen = jnp.take_along_axis(logits, targets[:, :, None], axis=2)[:, :, 0]
    return jnp.sum((total - chosen) * mask.astype(jnp.float32))

def reference(points, centers, neighbours, mask, targets, embed_in, embed_in_m, embed_in_v, embed_out, embed_out_m, embed_out_v, qkv_w, qkv_m, qkv_v, proj_w, proj_m, proj_v, fc1_w, fc1_m, fc1_v, fc2_w, fc2_m, fc2_v, gains, gains_m, gains_v, special, special_m, special_v, head, head_m, head_v):
    masters = (embed_in, embed_out, qkv_w, proj_w, fc1_w, fc2_w, gains, special, head)
    firsts = (embed_in_m, embed_out_m, qkv_m, proj_m, fc1_m, fc2_m, gains_m, special_m, head_m)
    seconds = (embed_in_v, embed_out_v, qkv_v, proj_v, fc1_v, fc2_v, gains_v, special_v, head_v)
    count = jnp.sum(mask).astype(jnp.float32)
    group = math.gcd(CLOUDS, 64)
    rounds = CLOUDS // group
    pieces = (points.reshape(3, rounds, group, POINTS).transpose(1, 0, 2, 3), centers.reshape(rounds, group, PATCHES), neighbours.reshape(rounds, group, PATCHES * NB), mask.reshape(rounds, group, PATCHES), targets.reshape(rounds, group, PATCHES))

    def one_group(carry, piece):
        loss, pull = jax.vjp(lambda *params: forward(params, *piece), *masters)
        grads = pull(1.0 / count)
        return ((carry[0] + loss, tuple((acc + new for acc, new in zip(carry[1], grads)))), None)
    start = (jnp.zeros((), jnp.float32), tuple((jnp.zeros_like(weight) for weight in masters)))
    (loss_sum, grads), _ = lax.scan(one_group, start, pieces)
    norm = jnp.sqrt(sum((jnp.sum(grad * grad) for grad in grads)))
    factor = jnp.minimum(1.0, CLIP / norm)
    results = []
    for index in range(9):
        vector = index in (6, 7)
        rate = RATE_VECTOR if vector else RATE_MATRIX
        decay = 0.0 if vector else DECAY
        clipped = grads[index] * factor
        first = BETA_ONE * firsts[index] + (1 - BETA_ONE) * clipped
        second = BETA_TWO * seconds[index] + (1 - BETA_TWO) * clipped * clipped
        update = first / (1 - BETA_ONE ** STEP_NUMBER) / (jnp.sqrt(second / (1 - BETA_TWO ** STEP_NUMBER)) + EPSILON)
        results += [first, second, masters[index] - rate * (update + decay * masters[index])]
    return (results[0], results[1], results[2], results[3], results[4], results[5], results[6], results[7], results[8], results[9], results[10], results[11], results[12], results[13], results[14], results[15], results[16], results[17], results[18], results[19], results[20], results[21], results[22], results[23], results[24], results[25], results[26], loss_sum, count, norm)
```

```python
import functools

import jax
import jax.numpy as jnp
from jax import lax
from jax.experimental import pallas as pl
from jax.experimental.pallas import tpu as pltpu
from jax.sharding import PartitionSpec as P

BF = jnp.bfloat16
F32 = jnp.float32
I32 = jnp.int32
D = 384
HEAD_DIM = 64
FF = 1536
PE = 128
NB = 32
PATCHES = 64
STEP_NUMBER = 10
MOST_MASKED = 36

BETA_ONE = 0.9
BETA_TWO = 0.95
EPSILON = 1e-08
DECAY = 0.05
RATE_MATRIX = 0.1
RATE_VECTOR = 0.5
CLIP = 0.005

TOP = 512
ROWS = 528
CAP = 288
CAPL = 384
VQ = 2048
SPLIT = 8
L_WIDE = 4608
L_ROWS = 3456
L_PIECE = L_ROWS // SPLIT
H_PIECE = 192
E_ROWS = 224
E_GRAD = 216
CH = 256

GA = 0.7978845608028654
GB = GA * 0.044715


def dot(left, right, dims=((1,), (0,))):
    return lax.dot_general(left, right, (dims, ((), ())), preferred_element_type=F32)


def gelu_pair(x):
    square = x * x
    half = 0.5 * jnp.tanh(x * (GA + GB * square)) + 0.5
    value = x * half
    slope = half + (value * (1.0 - half)) * (2.0 * GA + (6.0 * GB) * square)
    return value, slope


def iota(shape, axis):
    return lax.broadcasted_iota(I32, shape, axis)


def params(mib=48):
    return pltpu.CompilerParams(vmem_limit_bytes=mib << 20)


VM = pl.BlockSpec(memory_space=pltpu.VMEM)
SM = pl.BlockSpec(memory_space=pltpu.SMEM)
HB = pl.BlockSpec(memory_space=pl.ANY)


def shape(dims, dtype=F32):
    return jax.ShapeDtypeStruct(dims, dtype)


def cost(flops, moved, trans=0):
    return pl.CostEstimate(flops=int(flops), bytes_accessed=int(moved), transcendentals=int(trans))


def pack_kernel(ein, eout, qkv, proj, fc1, fc2, gains, special, mask, targets, e_out, l_out, scr):
    for i in range(2):
        for j in range(3):
            e_out[(i * 3 + j) * 32 : (i * 3 + j + 1) * 32, :] = eout[
                i, :, j * 128 : (j + 1) * 128
            ].astype(BF)
    scr[...] = jnp.zeros_like(scr)
    scr[0:3, 0:32] = ein[0]
    scr[3:6, 0:32] = ein[1]
    scr[6:9, 0:96] = gains[...]
    scr[9:11, 0:96] = special[...]
    hidden = mask[...].astype(F32)
    codes = targets[...]
    high = (codes >> 7).astype(F32)
    low = (codes & 127).astype(F32)
    for part, rows in enumerate((hidden, high, low)):
        for c in range(8):
            at = 16 + part * 4 + c // 2
            scr[at : at + 1, (c % 2) * 64 : (c % 2) * 64 + 64] = rows[c : c + 1, :]
    e_out[192:224, :] = scr[...].astype(BF)
    l_out[:, 0:1152] = qkv[0].astype(BF)
    l_out[:, 1152:1536] = proj[0].astype(BF)
    l_out[:, 1536:3072] = fc1[0].astype(BF)
    for q in range(4):
        l_out[:, 3072 + q * 384 : 3456 + q * 384] = fc2[0, q * 96 : (q + 1) * 96, :].astype(BF)


def pack(*arrays):
    return pl.pallas_call(
        pack_kernel,
        out_shape=(shape((E_ROWS, 128), BF), shape((96, L_WIDE), BF)),
        in_specs=[VM] * 10,
        out_specs=(VM, VM),
        scratch_shapes=[pltpu.VMEM((32, 128), F32)],
        compiler_params=params(),
        name="pack_layer",
    )(*arrays)


def pack_head_kernel(where, head, own, core, far):
    for pos in range(4):
        quarter = pos ^ where[0]
        piece = head[:, pl.ds(pl.multiple_of(quarter * VQ, VQ), VQ)].astype(BF)
        if pos == 0:
            own[...] = piece
        elif pos == 1:
            core[...] = piece
        else:
            far[pos - 2] = piece


def pack_head(where, head):
    return pl.pallas_call(
        pack_head_kernel,
        out_shape=(shape((96, VQ), BF), shape((96, VQ), BF), shape((2, 96, VQ), BF)),
        in_specs=[SM, VM],
        out_specs=(VM, VM, VM),
        compiler_params=params(),
        name="pack_head",
    )(where, head)


def choose_kernel(where, e_ref, code_ref, pick_ref, small_ref):
    upper = (iota((TOP, TOP), 0) <= iota((TOP, TOP), 1)).astype(F32).astype(BF)
    flags, codes = [], []
    for pos in range(4):
        rows = e_ref[pos ^ where[0], 208:224, :].astype(F32)
        flags.append(jnp.concatenate([rows[u : u + 1] for u in range(4)], 1))
        high = jnp.concatenate([rows[4 + u : 5 + u] for u in range(4)], 1)
        low = jnp.concatenate([rows[8 + u : 9 + u] for u in range(4)], 1)
        codes.append(high * 128.0 + low)
    stack = jnp.concatenate(flags + [jnp.zeros((4, TOP), F32)], 0).astype(BF)
    ranks = dot(stack, upper)
    for pos in range(4):
        rank = ranks[pos : pos + 1]
        chosen = (rank == (iota((CAP, TOP), 0) + 1).astype(F32)) & (flags[pos] > 0.0)
        picked = jnp.where(chosen, 1.0, 0.0)
        code = jnp.sum(picked * codes[pos], 1, keepdims=True)
        real = jnp.sum(picked, 1, keepdims=True) > 0.0
        column = jnp.where(real, code, -1.0).astype(I32)
        code_ref[pos] = jnp.broadcast_to(column, (CAP, 128))
        if pos == 0:
            pick_ref[...] = picked.astype(BF)
    for r in range(4):
        small_ref[:, r * 96 : (r + 1) * 96] = e_ref[r, 192:208, :].astype(F32)[:, 0:96]


def choose(where, e_all):
    return pl.pallas_call(
        choose_kernel,
        out_shape=(shape((4, CAP, 128), I32), shape((CAP, TOP), BF), shape((16, D))),
        in_specs=[SM, VM],
        out_specs=(VM, VM, VM),
        compiler_params=params(),
        name="choose_rows",
    )(where, e_all)


def point_forward_kernel(
    points, centers, neighbours, mask, e_ref,
    x_ref, slope_ref, inner_ref, slope_in_ref, rel_ref, cen_ref, up_ref, slope_up_ref, hid_ref,
    turned, cloud_pts, cloud_cen, cloud_flag, w_in, w_out, mark,
):
    c = pl.program_id(0)

    @pl.when(c == 0)
    def _():
        lane = iota((8, 128), 1)
        patch = lane & 63
        for q in range(16):
            spot = (patch & 3) * 32 + 2 * q + (lane >> 6)
            found = jnp.zeros((8, 128), I32)
            for v in range(16):
                part = jnp.take_along_axis(
                    neighbours[:, v * 128 : (v + 1) * 128], spot, axis=1, mode="promise_in_bounds"
                )
                found = jnp.where((patch >> 2) == v, part, found)
            for cloud in range(8):
                turned[cloud, 0:1, q * 128 : (q + 1) * 128] = found[cloud : cloud + 1]
        merged = jnp.zeros((16, 128), F32)
        for r in range(4):
            rows = e_ref[r, 192:208, :].astype(F32)
            merged = merged + jnp.where(
                iota((16, 128), 1) >> 5 == r, pltpu.roll(rows, r * 32, 1), 0.0
            )
            mark[:, r * 96 : (r + 1) * 96] = rows[:, 0:96]
            for i in range(2):
                for j in range(3):
                    w_out[i, r * 32 : (r + 1) * 32, j * 128 : (j + 1) * 128] = e_ref[
                        r, (i * 3 + j) * 32 : (i * 3 + j + 1) * 32, :
                    ]
        w_in[...] = jnp.zeros_like(w_in)
        w_in[0, 0:3, :] = merged[0:3]
        w_in[1, 0:3, :] = merged[3:6]
        cloud_pts[...] = jnp.zeros_like(cloud_pts)
        flags = mask[...].astype(F32)
        for cloud in range(8):
            row = slice(cloud, cloud + 1)
            for k in range(3):
                cloud_pts[cloud, k : k + 1, :] = points[k, row, :]
            cloud_cen[cloud, 0:1, 0:64] = centers[row, :]
            cloud_cen[cloud, 0:1, 64:128] = centers[row, :]
            cloud_flag[cloud, 0:1, 0:64] = flags[row, :]

    def look_up(index):
        index = jnp.broadcast_to(index, (8, 128))
        low = index & 127
        high = index >> 7
        found = jnp.zeros((8, 128), F32)
        for k in range(8):
            part = jnp.take_along_axis(
                cloud_pts[c, :, k * 128 : (k + 1) * 128], low, axis=1, mode="promise_in_bounds"
            )
            found = jnp.where(high == k, part, found)
        return found

    centre = look_up(cloud_cen[c, 0:1, :])
    in_point = w_in[0].astype(BF)
    in_centre = w_in[1].astype(BF)
    total = jnp.zeros((PATCHES, D), F32)
    for step in range(PATCHES * NB // CH):
        halves = []
        for q in range(step * CH // 128, (step + 1) * CH // 128):
            near = look_up(turned[c, 0:1, q * 128 : (q + 1) * 128])
            halves.append(near - centre)
        relative = jnp.concatenate(halves, 1).astype(BF)
        at = slice(step * CH, (step + 1) * CH)
        rel_ref[0, :, at] = relative
        value, slope = gelu_pair(dot(relative, in_point, ((0,), (0,))))
        inner = value.astype(BF)
        inner_ref[0, at, :] = inner
        slope_in_ref[0, at, :] = slope.astype(BF)
        value, slope = gelu_pair(dot(inner, w_out[0]))
        slope_ref[0, at, :] = slope.astype(BF)
        total = total + jnp.sum(value.reshape(CH // PATCHES, PATCHES, D), 0)
    centre_b = centre.astype(BF)
    cen_ref[0] = centre_b
    value, slope = gelu_pair(dot(centre_b, in_centre, ((0,), (0,)))[0:PATCHES])
    up = value.astype(BF)
    up_ref[0] = up
    slope_up_ref[0] = slope
    place = dot(up, w_out[1])
    diagonal = iota((PATCHES, PATCHES), 0) == iota((PATCHES, PATCHES), 1)
    flags = jnp.broadcast_to(cloud_flag[c, 0:1, 0:64], (PATCHES, PATCHES))
    hidden = jnp.sum(jnp.where(diagonal, flags, 0.0), 1, keepdims=True)
    hid_ref[...] = jnp.broadcast_to(hidden, (PATCHES, 128))
    x_ref[...] = jnp.where(hidden > 0.0, mark[10:11, :], total * (1.0 / NB)) + place


def point_forward(points, centers, neighbours, mask, e_all):
    clouds = mask.shape[0]
    tokens = PATCHES * NB

    def whole(array):
        return pl.BlockSpec(array.shape, lambda c: (0,) * array.ndim)

    def per(*dims):
        return pl.BlockSpec((1,) + dims, lambda c: (c, 0, 0))

    inputs = (points, centers, neighbours, mask, e_all)
    return pl.pallas_call(
        point_forward_kernel,
        grid=(clouds,),
        out_shape=(
            shape((TOP, D)),
            shape((clouds, tokens, D), BF),
            shape((clouds, tokens, PE), BF),
            shape((clouds, tokens, PE), BF),
            shape((clouds, 8, tokens), BF),
            shape((clouds, 8, 128), BF),
            shape((clouds, PATCHES, PE), BF),
            shape((clouds, PATCHES, PE)),
            shape((TOP, 128)),
        ),
        in_specs=[whole(array) for array in inputs],
        out_specs=(
            pl.BlockSpec((PATCHES, D), lambda c: (c, 0)),
            per(tokens, D),
            per(tokens, PE),
            per(tokens, PE),
            per(8, tokens),
            per(8, 128),
            per(PATCHES, PE),
            per(PATCHES, PE),
            pl.BlockSpec((PATCHES, 128), lambda c: (c, 0)),
        ),
        scratch_shapes=[
            pltpu.VMEM((8, 8, tokens), I32),
            pltpu.VMEM((8, 8, 1024), F32),
            pltpu.VMEM((8, 8, 128), I32),
            pltpu.VMEM((8, 8, 128), F32),
            pltpu.VMEM((2, 8, PE), F32),
            pltpu.VMEM((2, PE, D), BF),
            pltpu.VMEM((16, D), F32),
        ],
        compiler_params=params(),
        cost_estimate=cost(3e9, 20e6, 8e6),
        name="point_forward",
    )(*inputs)


def layer_copies(where, shards, w_main, w_two, sems):
    copies = []
    for pos, shard in enumerate(shards):
        rank = pos ^ where[0]
        rows = pl.ds(pl.multiple_of(rank * 96, 96), 96)
        copies.append(
            pltpu.make_async_copy(shard.at[:, 0:3072], w_main.at[rows, :], sems.at[pos, 4])
        )
        for q in range(4):
            rows = pl.ds(pl.multiple_of(rank * 384 + q * 96, 96), 96)
            copies.append(
                pltpu.make_async_copy(
                    shard.at[:, 3072 + q * 384 : 3456 + q * 384], w_two.at[rows, :], sems.at[pos, q]
                )
            )
    return copies


LAYER_SCRATCH = [
    pltpu.VMEM((D, 3072), BF),
    pltpu.VMEM((FF, D), BF),
    pltpu.SemaphoreType.DMA((4, 5)),
]


def norm(x):
    centred = x - jnp.mean(x, -1, keepdims=True)
    scale = lax.rsqrt(jnp.mean(centred * centred, -1, keepdims=True) + 1e-06)
    return centred * scale, scale


def norm_back(grad, x, gain):
    hat, scale = norm(x)
    d_gain = jnp.sum(grad * hat, 0, keepdims=True)
    inner = grad * gain
    d_x = scale * (
        inner - jnp.mean(inner, -1, keepdims=True) - hat * jnp.mean(inner * hat, -1, keepdims=True)
    )
    return d_x, d_gain


def cloud_rows(ref, start, lanes):
    return jnp.concatenate([ref[pl.ds(start, 64), lanes], ref[TOP:ROWS, lanes]], 0)


def lane_masks():
    first = (iota((1, 128), 1) < HEAD_DIM).astype(F32)
    return first.astype(BF), (1.0 - first).astype(BF)


def layer_forward_kernel(
    where, xp, small, pick, s0, s1, s2, s3,
    m_ref, xo_ref, y_ref, qkv_ref, a_ref, o_ref, z_ref, act_ref, slope_ref, f_ref,
    w_main, w_two, sems, x_all, o_cls,
):
    copies = layer_copies(where, (s0, s1, s2, s3), w_main, w_two, sems)
    for copy in copies:
        copy.start()
    x_all[0:TOP, :] = xp[...]
    opening = jnp.broadcast_to(small[9:10, :], (16, D))
    x_all[TOP:ROWS, :] = jnp.where(iota((16, D), 0) < 8, opening, 0.0)
    hat, _ = norm(x_all[...])
    y_ref[...] = (hat * small[6:7, :]).astype(BF)
    for copy in copies:
        copy.wait()
    qkv_ref[...] = dot(y_ref[...], w_main[:, 0:1152]).astype(BF)
    o_cls[...] = jnp.zeros_like(o_cls)
    mask0, mask1 = lane_masks()

    def one_cloud(c, carry):
        start = pl.multiple_of(c * 64, 64)
        column = iota((160, 80), 1)
        allowed = (column < 64) | (column == c + 64)
        for p in range(3):
            q = cloud_rows(qkv_ref, start, slice(p * 128, p * 128 + 128))
            k = cloud_rows(qkv_ref, start, slice(384 + p * 128, 512 + p * 128))
            v = cloud_rows(qkv_ref, start, slice(768 + p * 128, 896 + p * 128))
            both = jnp.concatenate([q * mask0, q * mask1], 0)
            scores = dot(both, k, ((1,), (1,))) * HEAD_DIM**-0.5
            scores = jnp.where(allowed, scores, -1e30)
            top = jnp.max(scores, -1, keepdims=True)
            e = jnp.exp(scores - top)
            a = (e / jnp.sum(e, -1, keepdims=True)).astype(BF)
            a_ref[c * 3 + p] = a
            o = dot(a, v)
            pair = jnp.where(iota((80, 128), 1) < HEAD_DIM, o[0:80], o[80:160])
            lanes = slice(p * 128, p * 128 + 128)
            o_ref[pl.ds(start, 64), lanes] = pair[0:64].astype(BF)
            o_cls[:, lanes] += jnp.where(iota((16, 128), 0) == c, pair[64:80], 0.0)
        return carry

    lax.fori_loop(0, 8, one_cloud, 0)
    o_ref[TOP:ROWS, :] = o_cls[...].astype(BF)
    m_ref[...] = x_all[...] + dot(o_ref[...], w_main[:, 1152:1536])
    hat, _ = norm(m_ref[...])
    z_ref[...] = (hat * small[7:8, :]).astype(BF)
    for part in range(3):
        lanes = slice(part * 512, part * 512 + 512)
        hidden = dot(z_ref[...], w_main[:, 1536 + part * 512 : 2048 + part * 512])
        value, slope = gelu_pair(hidden)
        act_ref[:, lanes] = value.astype(BF)
        slope_ref[:, lanes] = slope.astype(BF)
    xo = m_ref[0:TOP, :] + dot(act_ref[0:TOP, :], w_two[...])
    xo_ref[...] = xo
    hat, _ = norm(xo)
    f_ref[...] = dot(pick[...], (hat * small[8:9, :]).astype(BF)).astype(BF)


def layer_forward(where, xp, small, pick, shards):
    return pl.pallas_call(
        layer_forward_kernel,
        out_shape=(
            shape((ROWS, D)),
            shape((TOP, D)),
            shape((ROWS, D), BF),
            shape((ROWS, 1152), BF),
            shape((24, 160, 80), BF),
            shape((ROWS, D), BF),
            shape((ROWS, D), BF),
            shape((ROWS, FF), BF),
            shape((ROWS, FF), BF),
            shape((CAP, D), BF),
        ),
        in_specs=[SM, VM, VM, VM] + [HB] * 4,
        out_specs=(VM,) * 10,
        scratch_shapes=LAYER_SCRATCH + [pltpu.VMEM((ROWS, D), F32), pltpu.VMEM((16, D), F32)],
        compiler_params=params(),
        cost_estimate=cost(3e9, 12e6, 2e6),
        name="layer_forward",
    )(where, xp, small, pick, *shards)


def head_copies(where, pieces, table, sems):
    copies = []
    for pos, piece in enumerate(pieces):
        rows = pl.ds(pl.multiple_of((pos ^ where[0]) * 96, 96), 96)
        copies.append(pltpu.make_async_copy(piece, table.at[rows, :], sems.at[pos]))
    return copies


def head_scores_kernel(
    where, f0, f1, f2, f3, h0, h1, h2, h3, codes, e_ref, stat_ref, table, scores, sems
):
    copies = head_copies(where, (h0, h1, h2.at[0], h3), table, sems)
    for copy in copies:
        copy.start()
    for copy in copies:
        copy.wait()
    base = where[0] * VQ
    for pos, rows in enumerate((f0, f1, f2, f3)):
        best = jnp.full((CAP, 128), -jnp.inf, F32)
        for t in range(4):
            part = dot(rows[...], table[:, t * 512 : t * 512 + 512])
            scores[:, t * 512 : t * 512 + 512] = part
            for u in range(4):
                best = jnp.maximum(best, part[:, u * 128 : u * 128 + 128])
        top = jnp.max(best, -1, keepdims=True)
        code = codes[pos] - base
        total = jnp.zeros((CAP, 128), F32)
        aimed = jnp.zeros((CAP, 128), F32)
        for u in range(16):
            lanes = slice(u * 128, u * 128 + 128)
            part = scores[:, lanes]
            e = jnp.exp(part - top)
            e_ref[pos, :, lanes] = e.astype(BF)
            total = total + e
            aimed = aimed + jnp.where(iota((CAP, 128), 1) + u * 128 == code, part, 0.0)
        lane = iota((CAP, 128), 1)
        both = jnp.where(
            lane == 0,
            top,
            jnp.where(
                lane == 1,
                jnp.sum(total, -1, keepdims=True),
                jnp.where(lane == 2, jnp.sum(aimed, -1, keepdims=True), 0.0),
            ),
        )
        both = jnp.concatenate([both, jnp.zeros((CAPL - CAP, 128), F32)], 0)
        stat_ref[pos] = jnp.transpose(both)[0:8, :]


def head_scores(where, rows, pieces, codes):
    return pl.pallas_call(
        head_scores_kernel,
        out_shape=(shape((4, CAP, VQ), BF), shape((4, 8, CAPL))),
        in_specs=[SM] + [VM] * 4 + [HB] * 4 + [VM],
        out_specs=(VM, VM),
        scratch_shapes=[
            pltpu.VMEM((D, VQ), BF),
            pltpu.VMEM((CAP, VQ), F32),
            pltpu.SemaphoreType.DMA((4,)),
        ],
        compiler_params=params(),
        cost_estimate=cost(2e9, 8e6, 3e6),
        name="head_scores",
    )(where, *rows, *pieces, codes)


def head_back_kernel(
    where, e_ref, t0, t1, t2, t3, codes, h0, h1, h2, h3,
    d_ref, keep_ref, send_ref, loss_ref, table, sems,
):
    copies = head_copies(where, (h0, h1, h2.at[0], h3), table, sems)
    for copy in copies:
        copy.start()
    stats = (t0, t1, t2, t3)
    columns, aims = [], []
    for pos in range(4):
        tops = [stats[q][pos ^ q, 0:1, :] for q in range(4)]
        sums = [stats[q][pos ^ q, 1:2, :] for q in range(4)]
        top = jnp.maximum(jnp.maximum(tops[0], tops[1]), jnp.maximum(tops[2], tops[3]))
        total = jnp.zeros((1, CAPL), F32)
        for q in range(4):
            total = total + sums[q] * jnp.exp(tops[q] - top)
        scale = jnp.exp(tops[0] - top) / total
        columns.append(scale)
        aims.append(jnp.exp(t0[pos, 2:3, :] - top) / total - 1.0)
        if pos == 0:
            aimed = t0[0, 2:3, :] + t1[1, 2:3, :] + t2[2, 2:3, :] + t3[3, 2:3, :]
            losses = top + jnp.log(total) - aimed
    block = jnp.concatenate(columns + aims + [losses, jnp.zeros((119, CAPL), F32)], 0)
    turned = jnp.transpose(block)[0:CAP, :]
    real = codes[0] >= 0
    loss = jnp.where(real[:, 0:1], turned[:, 8:9], 0.0)
    loss_ref[...] = jnp.broadcast_to(jnp.sum(loss, 0, keepdims=True), (8, 128))
    base = where[0] * VQ
    for copy in copies:
        copy.wait()
    for pos in range(4):
        scale = jnp.where(codes[pos][:, 0:1] >= 0, turned[:, pos : pos + 1], 0.0)
        aim = turned[:, 4 + pos : 5 + pos]
        code = codes[pos] - base
        for u in range(16):
            lanes = slice(u * 128, u * 128 + 128)
            hit = iota((CAP, 128), 1) + u * 128 == code
            grad = jnp.where(hit, aim, e_ref[pos, :, lanes].astype(F32) * scale)
            d_ref[pos, :, lanes] = grad.astype(BF)
        back = dot(d_ref[pos], table[...], ((1,), (1,)))
        if pos % 2 == 0:
            keep_ref[pos // 2] = back
        else:
            send_ref[pos // 2] = back.astype(BF)


def head_back(where, e, stats, codes, pieces):
    return pl.pallas_call(
        head_back_kernel,
        out_shape=(
            shape((4, CAP, VQ), BF),
            shape((2, CAP, D)),
            shape((2, CAP, D), BF),
            shape((8, 128)),
        ),
        in_specs=[SM] + [VM] * 6 + [HB] * 4,
        out_specs=(VM,) * 4,
        scratch_shapes=[pltpu.VMEM((D, VQ), BF), pltpu.SemaphoreType.DMA((4,))],
        compiler_params=params(),
        cost_estimate=cost(2e9, 12e6),
        name="head_back",
    )(where, e, *stats, codes, *pieces)


def place_piece(where, piece):
    rel = piece ^ where[1]
    return rel & 1, ((rel >> 1) & 1) * 2 + ((rel >> 2) & 1)


def head_grad_kernel(where, f0, f1, f2, f3, d_ref, g_ref, joined):
    for pos, rows in enumerate((f0, f1, f2, f3)):
        joined[:, pos * CAP : (pos + 1) * CAP] = jnp.transpose(rows[...].astype(F32)).astype(BF)

    for piece in range(SPLIT):
        first, index = place_piece(where, piece)
        lanes = slice(piece * 256, piece * 256 + 256)
        cols = jnp.concatenate([d_ref[pos, :, lanes] for pos in range(4)], 0)
        grad = dot(joined[...], cols)
        for r in range(4):
            for j in range(2):
                g_ref[first, index, r ^ where[0], j * 96 : j * 96 + 96, :] = grad[
                    r * 96 : r * 96 + 96, j * 128 : j * 128 + 128
                ].astype(BF)


def head_grad(where, rows, d):
    return pl.pallas_call(
        head_grad_kernel,
        out_shape=shape((2, 4, 4, H_PIECE, 128), BF),
        in_specs=[SM] + [VM] * 5,
        out_specs=VM,
        scratch_shapes=[pltpu.VMEM((D, 4 * CAP), BF)],
        compiler_params=params(),
        cost_estimate=cost(2e9, 8e6),
        name="head_grad",
    )(where, *rows, d)


def store_layer_grad(where, g_ref, block, grad):
    for r in range(4):
        pos = r ^ where[0]
        core, far = pos & 1, pos >> 1
        for unit in range(2):
            row = block * 96 + unit * 48
            first, index = place_piece(where, row // L_PIECE)
            at = row % L_PIECE
            g_ref[core, far, first, index, at : at + 48, :] = grad[
                r * 96 + unit * 48 : r * 96 + unit * 48 + 48, :
            ].astype(BF)


def layer_backward_kernel(
    where, keep, rc, rx, pick, xo, m_ref, xp, small, y_ref, qkv_ref, a_ref, o_ref, z_ref, act_ref,
    slope_ref, hid, s0, s1, s2, s3,
    g_ref, dx_ref, sg_ref,
    w_main, w_two, sems, x_all, d_o, d_qkv, d_cls, d_hid,
):
    copies = layer_copies(where, (s0, s1, s2, s3), w_main, w_two, sems)
    for copy in copies:
        copy.start()
    x_all[0:TOP, :] = xp[...]
    opening = jnp.broadcast_to(small[9:10, :], (16, D))
    x_all[TOP:ROWS, :] = jnp.where(iota((16, D), 0) < 8, opening, 0.0)
    compact = keep[0] + rc[0].astype(F32) + rx[...].astype(F32)
    high = compact.astype(BF)
    low = (compact - high.astype(F32)).astype(BF)
    d_rows = dot(pick[...], high, ((0,), (0,))) + dot(pick[...], low, ((0,), (0,)))
    d_out, d_gain = norm_back(d_rows, xo[...], small[8:9, :])
    sg_ref[...] = jnp.zeros_like(sg_ref)
    sg_ref[8:9, :] = d_gain
    grad_b = d_out.astype(BF)
    for copy in copies:
        copy.wait()
    for part in range(3):
        lanes = slice(part * 512, part * 512 + 512)
        back = dot(grad_b, w_two[lanes, :], ((1,), (1,)))
        d_hid[:, lanes] = (back * slope_ref[0:TOP, lanes].astype(F32)).astype(BF)
    d_fc2 = dot(act_ref[0:TOP, :], grad_b, ((0,), (0,)))
    for q in range(4):
        for j in range(3):
            parts = [d_fc2[r * 384 + q * 96 : r * 384 + q * 96 + 96, j * 128 : j * 128 + 128] for r in range(4)]
            store_layer_grad(where, g_ref, 24 + q * 3 + j, jnp.concatenate(parts, 0))
    for j in range(12):
        grad = dot(z_ref[0:TOP, :], d_hid[:, j * 128 : j * 128 + 128], ((0,), (0,)))
        store_layer_grad(where, g_ref, 12 + j, grad)
    d_z = dot(d_hid[...], w_main[:, 1536:3072], ((1,), (1,)))
    d_m, d_gain = norm_back(d_z, m_ref[0:TOP, :], small[7:8, :])
    sg_ref[7:8, :] = d_gain
    d_m = d_m + d_out
    dx_ref[0:TOP, :] = d_m
    dx_ref[TOP:ROWS, :] = jnp.zeros((16, D), F32)
    m_b = d_m.astype(BF)
    for j in range(3):
        grad = dot(o_ref[0:TOP, :], m_b[:, j * 128 : j * 128 + 128], ((0,), (0,)))
        store_layer_grad(where, g_ref, 9 + j, grad)
    d_o[...] = dot(m_b, w_main[:, 1152:1536], ((1,), (1,))).astype(BF)
    d_cls[...] = jnp.zeros_like(d_cls)
    mask0, mask1 = lane_masks()

    def one_cloud(c, carry):
        start = pl.multiple_of(c * 64, 64)
        for p in range(3):
            lanes = slice(p * 128, p * 128 + 128)
            q = qkv_ref[pl.ds(start, 64), lanes]
            k = cloud_rows(qkv_ref, start, slice(384 + p * 128, 512 + p * 128))
            v = cloud_rows(qkv_ref, start, slice(768 + p * 128, 896 + p * 128))
            d = d_o[pl.ds(start, 64), lanes]
            q2 = jnp.concatenate([q * mask0, q * mask1], 0)
            d2 = jnp.concatenate([d * mask0, d * mask1], 0)
            a = jnp.concatenate([a_ref[c * 3 + p, 0:64, :], a_ref[c * 3 + p, 80:144, :]], 0)
            d_a = dot(d2, v, ((1,), (1,)))
            full = a.astype(F32)
            d_s = full * (d_a - jnp.sum(d_a * full, -1, keepdims=True)) * HEAD_DIM**-0.5
            d_s = d_s.astype(BF)
            d_q = dot(d_s, k)
            d_q = jnp.where(iota((64, 128), 1) < HEAD_DIM, d_q[0:64], d_q[64:128])
            d_k = dot(d_s, q2, ((0,), (0,)))
            d_v = dot(a, d2, ((0,), (0,)))
            d_qkv[pl.ds(start, 64), p * 128 : p * 128 + 128] = d_q.astype(BF)
            d_qkv[pl.ds(start, 64), 384 + p * 128 : 512 + p * 128] = d_k[0:64].astype(BF)
            d_qkv[pl.ds(start, 64), 768 + p * 128 : 896 + p * 128] = d_v[0:64].astype(BF)
            d_cls[:, 384 + p * 128 : 512 + p * 128] += d_k[64:80]
            d_cls[:, 768 + p * 128 : 896 + p * 128] += d_v[64:80]
        return carry

    lax.fori_loop(0, 8, one_cloud, 0)
    d_qkv[TOP:ROWS, :] = d_cls[...].astype(BF)
    for j in range(9):
        grad = dot(y_ref[...], d_qkv[:, j * 128 : j * 128 + 128], ((0,), (0,)))
        store_layer_grad(where, g_ref, j, grad)
    d_y = dot(d_qkv[...], w_main[:, 0:1152], ((1,), (1,)))
    d_x, d_gain = norm_back(d_y, x_all[...], small[6:7, :])
    sg_ref[6:7, :] = d_gain
    d_x = d_x + dx_ref[...]
    dx_ref[...] = d_x
    sg_ref[9:10, :] = jnp.sum(d_x[TOP:ROWS], 0, keepdims=True)
    sg_ref[10:11, :] = jnp.sum(
        jnp.where(hid[:, 0:1] > 0.0, d_x[0:TOP], 0.0), 0, keepdims=True
    )


def layer_backward(where, keep, rc, rx, pick, kept, xp, small, hid, shards):
    m, xo, y, qkv, a, o, z, act, slope = kept
    return pl.pallas_call(
        layer_backward_kernel,
        out_shape=(
            shape((2, 2, 2, 4, L_PIECE, 128), BF),
            shape((ROWS, D)),
            shape((16, D)),
        ),
        in_specs=[SM] + [VM] * 16 + [HB] * 4,
        out_specs=(VM,) * 3,
        scratch_shapes=LAYER_SCRATCH
        + [
            pltpu.VMEM((ROWS, D), F32),
            pltpu.VMEM((TOP, D), BF),
            pltpu.VMEM((ROWS, 1152), BF),
            pltpu.VMEM((16, 1152), F32),
            pltpu.VMEM((TOP, FF), BF),
        ],
        compiler_params=params(),
        cost_estimate=cost(5e9, 20e6),
        name="layer_backward",
    )(where, keep, rc, rx, pick, xo, m, xp, small, y, qkv, a, o, z, act, slope, hid, *shards)


def point_backward_kernel(
    where, dx_ref, hid, slope_ref, inner_ref, slope_in_ref, rel_ref, cen_ref, up_ref, slope_up_ref,
    e_ref, sg_ref, loss_ref, mask, g_ref, w_out, d_out, d_in,
):
    c = pl.program_id(0)

    @pl.when(c == 0)
    def _():
        for r in range(4):
            for i in range(2):
                for j in range(3):
                    w_out[i, r * 32 : (r + 1) * 32, j * 128 : (j + 1) * 128] = e_ref[
                        r, (i * 3 + j) * 32 : (i * 3 + j + 1) * 32, :
                    ]
        d_out[...] = jnp.zeros_like(d_out)
        d_in[...] = jnp.zeros_like(d_in)

    rows = dx_ref[...]
    place = rows.astype(BF)
    d_out[1] += dot(up_ref[0], place, ((0,), (0,)))
    d_up = (dot(place, w_out[1], ((1,), (1,))) * slope_up_ref[0]).astype(BF)
    d_in[1] += dot(cen_ref[0, :, 0:PATCHES], d_up)
    d_patch = jnp.where(hid[:, 0:1] > 0.0, 0.0, rows) * (1.0 / NB)
    tiled = jnp.concatenate([d_patch] * (CH // PATCHES), 0)
    for step in range(PATCHES * NB // CH):
        at = slice(step * CH, (step + 1) * CH)
        d_spread = (tiled * slope_ref[0, at, :].astype(F32)).astype(BF)
        d_out[0] += dot(inner_ref[0, at, :], d_spread, ((0,), (0,)))
        back = dot(d_spread, w_out[0], ((1,), (1,)))
        d_lift = (back * slope_in_ref[0, at, :].astype(F32)).astype(BF)
        d_in[0] += dot(rel_ref[0, :, at], d_lift)

    @pl.when(c == pl.num_programs(0) - 1)
    def _():
        lane = iota((8, 128), 1)
        for r in range(4):
            pos = r ^ where[0]
            core, far = pos & 1, pos >> 1
            for i in range(2):
                for j in range(3):
                    g_ref[core, far, (i * 3 + j) * 32 : (i * 3 + j + 1) * 32, :] = d_out[
                        i, r * 32 : (r + 1) * 32, j * 128 : (j + 1) * 128
                    ]
            g_ref[core, far, 192:216, :] = jnp.zeros((24, 128), F32)
            turn = (128 - r * 32) % 128
            for i in range(2):
                rolled = d_in[i] if turn == 0 else pltpu.roll(d_in[i], turn, 1)
                rolled = jnp.where(lane < 32, rolled, 0.0)
                g_ref[core, far, 192 + i * 3 : 195 + i * 3, :] = rolled[0:3]
            g_ref[core, far, 198:203, 0:96] = sg_ref[6:11, r * 96 : (r + 1) * 96]
            g_ref[core, far, 208:209, :] = loss_ref[0:1, :]
            seen = jnp.sum(jnp.sum(mask[...].astype(F32), 1, keepdims=True), 0, keepdims=True)
            g_ref[core, far, 209:210, :] = jnp.broadcast_to(seen, (1, 128))


def point_backward(where, dx, kept, e_all, sg, loss, mask):
    slope, inner, slope_in, rel, cen, up, slope_up, hid = kept
    clouds = mask.shape[0]
    tokens = PATCHES * NB

    def whole(array):
        return pl.BlockSpec(array.shape, lambda c: (0,) * array.ndim)

    def per(*dims):
        return pl.BlockSpec((1,) + dims, lambda c: (c, 0, 0))

    return pl.pallas_call(
        point_backward_kernel,
        grid=(clouds,),
        out_shape=shape((2, 2, E_GRAD, 128)),
        in_specs=[
            SM,
            pl.BlockSpec((PATCHES, D), lambda c: (c, 0)),
            pl.BlockSpec((PATCHES, 128), lambda c: (c, 0)),
            per(tokens, D),
            per(tokens, PE),
            per(tokens, PE),
            per(8, tokens),
            per(8, 128),
            per(PATCHES, PE),
            per(PATCHES, PE),
            whole(e_all),
            whole(sg),
            whole(loss),
            whole(mask),
        ],
        out_specs=pl.BlockSpec((2, 2, E_GRAD, 128), lambda c: (0, 0, 0, 0)),
        scratch_shapes=[
            pltpu.VMEM((2, PE, D), BF),
            pltpu.VMEM((2, PE, D), F32),
            pltpu.VMEM((2, 8, PE), F32),
        ],
        compiler_params=params(),
        cost_estimate=cost(4e9, 22e6),
        name="point_backward",
    )(where, dx, hid, slope, inner, slope_in, rel, cen, up, slope_up, e_all, sg, loss, mask)


def squares_kernel(h0, h1, l0, l1, e_ref, out_ref):
    total = jnp.zeros((16, 128), F32)
    for ref in (h0, h1):
        for i in range(4):
            for q in range(4):
                part = ref[i, q].astype(F32)
                total = total + jnp.sum((part * part).reshape(H_PIECE // 16, 16, 128), 0)
    for ref in (l0, l1):
        for i in range(4):
            part = ref[i].astype(F32)
            total = total + jnp.sum((part * part).reshape(L_PIECE // 16, 16, 128), 0)
    part = e_ref[0:208, :]
    total = total + jnp.sum((part * part).reshape(13, 16, 128), 0)
    total = jnp.sum(jnp.sum(total, 1, keepdims=True), 0, keepdims=True)
    out_ref[...] = jnp.broadcast_to(total, (8, 128))


def squares(hs, ls, e):
    return pl.pallas_call(
        squares_kernel,
        out_shape=shape((8, 128)),
        in_specs=[VM] * 5,
        out_specs=VM,
        compiler_params=params(),
        name="squares",
    )(*hs, *ls, e)


def adam(grad, first, second, weight, factor, vector):
    rate = RATE_VECTOR if vector else RATE_MATRIX
    clipped = grad * factor
    first = BETA_ONE * first + (1 - BETA_ONE) * clipped
    second = BETA_TWO * second + (1 - BETA_TWO) * (clipped * clipped)
    root = jnp.sqrt(second * (1.0 / (1 - BETA_TWO**STEP_NUMBER))) + EPSILON
    update = (first * (rate / (1 - BETA_ONE**STEP_NUMBER))) / root
    if vector:
        return first, second, weight - update
    return first, second, weight * (1.0 - rate * DECAY) - update


def clip_factor(s0, s1, e_ref):
    count = e_ref[209:210, :]
    length = jnp.sqrt(s0[0:1, :] + s1[0:1, :]) / count
    return jnp.minimum(1.0, CLIP / length) / count, length


def step_head_kernel(where, s0, s1, e_ref, g0, g1, w, m, v, m_out, v_out, w_out):
    factor, _ = clip_factor(s0, s1, e_ref)
    step = pl.program_id(0)
    quarter = (step >> 1) ^ where[0]
    for p in range(4):
        first, index = place_piece(where, (step & 1) * 4 + p)

        def do(ref):
            for j in range(2):
                lanes = slice(p * 256 + j * 128, p * 256 + j * 128 + 128)
                grad = ref[index, quarter, j * 96 : j * 96 + 96, :].astype(F32)
                out = adam(grad, m[:, lanes], v[:, lanes], w[:, lanes], factor, False)
                m_out[:, lanes], v_out[:, lanes], w_out[:, lanes] = out

        pl.when(first == 0)(functools.partial(do, g0))
        pl.when(first == 1)(functools.partial(do, g1))


def step_head(where, sums, e, grads, w, m, v):
    tile = pl.BlockSpec((96, 1024), lambda i: (0, i))

    def whole(array):
        return pl.BlockSpec(array.shape, lambda i: (0,) * array.ndim)

    return pl.pallas_call(
        step_head_kernel,
        grid=(8,),
        out_shape=(shape(w.shape),) * 3,
        in_specs=[SM] + [whole(array) for array in (*sums, e, *grads)] + [tile] * 3,
        out_specs=(tile,) * 3,
        compiler_params=params(),
        cost_estimate=cost(2e7, 2e7),
        name="step_head",
    )(where, *sums, e, *grads, w, m, v)


def step_rest_kernel(where, s0, s1, e_ref, g0, g1, *refs):
    ins, outs, joined = refs[:24], refs[24:-1], refs[-1]
    factor, length = clip_factor(s0, s1, e_ref)
    for piece in range(SPLIT):
        first, index = place_piece(where, piece)
        rows = slice(piece * L_PIECE, (piece + 1) * L_PIECE)

        def copy(ref, rows=rows, index=index):
            joined[rows, :] = ref[index]

        pl.when(first == 0)(functools.partial(copy, g0))
        pl.when(first == 1)(functools.partial(copy, g1))

    def update(which, at, grad, vector=False):
        w, m, v = (ins[which * 3 + k] for k in range(3))
        out = adam(grad, m[at], v[at], w[at], factor[:, 0 : grad.shape[-1]], vector)
        for k in range(3):
            outs[which * 3 + k][at] = out[k]

    for i in range(2):
        update(0, (i,), e_ref[192 + i * 3 : 195 + i * 3, 0:32])
        for j in range(3):
            block = i * 3 + j
            update(1, (i, slice(None), slice(j * 128, j * 128 + 128)), e_ref[block * 32 : block * 32 + 32, :])
    for block in range(36):
        grad = joined[block * 96 : block * 96 + 96, :].astype(F32)
        if block < 9:
            update(2, (0, slice(None), slice(block * 128, block * 128 + 128)), grad)
        elif block < 12:
            j = block - 9
            update(3, (0, slice(None), slice(j * 128, j * 128 + 128)), grad)
        elif block < 24:
            j = block - 12
            update(4, (0, slice(None), slice(j * 128, j * 128 + 128)), grad)
        else:
            q, j = divmod(block - 24, 3)
            update(5, (0, slice(q * 96, q * 96 + 96), slice(j * 128, j * 128 + 128)), grad)
    update(6, (slice(0, 3),), e_ref[198:201, 0:96], True)
    update(7, (slice(0, 2),), e_ref[201:203, 0:96], True)
    outs[24][0:1, :] = e_ref[208:209, :]
    outs[24][1:2, :] = e_ref[209:210, :]
    outs[24][2:3, :] = length


def step_rest(where, sums, e, grads, states):
    outs = tuple(shape(array.shape) for array in states) + (shape((8, 128)),)
    return pl.pallas_call(
        step_rest_kernel,
        out_shape=outs,
        in_specs=[SM] + [VM] * (5 + len(states)),
        out_specs=(VM,) * len(outs),
        scratch_shapes=[pltpu.VMEM((L_ROWS, 128), BF)],
        compiler_params=params(),
        cost_estimate=cost(2e7, 1.2e7),
        name="step_rest",
    )(where, *sums, e, *grads, *states)


def add(*parts):
    total = parts[0].astype(F32)
    for part in parts[1:]:
        total = total + part.astype(F32)
    return total.astype(BF)


def body(dp, fsdp, *args):
    (
        points, centers, neighbours, mask, targets,
        embed_in, embed_in_m, embed_in_v, embed_out, embed_out_m, embed_out_v,
        qkv_w, qkv_m, qkv_v, proj_w, proj_m, proj_v, fc1_w, fc1_m, fc1_v, fc2_w, fc2_m, fc2_v,
        gains, gains_m, gains_v, special, special_m, special_v, head, head_m, head_v,
    ) = args
    rank = lax.axis_index("fsdp").astype(I32)
    group = lax.axis_index("dp").astype(I32)
    where = jnp.stack([rank, group % SPLIT])

    def swap(x, axis, bit):
        size = dp if axis == "dp" else fsdp
        return lax.ppermute(x, axis, [(i, i ^ bit) for i in range(size)])

    def halve(keep, send):
        got = swap(send, "dp", 1)
        upper = add(keep[2:], got[2:])
        got_upper = swap(upper, "dp", 2)
        lower = add(keep[:2], got[:2])
        last = add(lower[1], got_upper[1])
        got_last = swap(last, "dp", 4)
        total = add(lower[0], got_upper[0], got_last)
        bit = SPLIT
        while bit < dp:
            total = add(total, swap(total, "dp", bit))
            bit *= 2
        return total

    def double(piece):
        both = jnp.stack([piece, swap(piece, "dp", 4)])
        both = jnp.concatenate([both, swap(both, "dp", 2)], 0)
        return both, swap(both, "dp", 1)

    e_own, l_own = pack(
        embed_in, embed_out, qkv_w, proj_w, fc1_w, fc2_w, gains, special, mask, targets
    )
    e_all = lax.all_gather(e_own, "fsdp", axis=0)
    l_far = swap(l_own, "fsdp", 2)
    h_own, h_core, h_far = pack_head(where, head)
    h_got = swap(h_far, "fsdp", 2)
    l_near = swap(l_own, "fsdp", 1)
    codes, pick, small = choose(where, e_all)
    xp, *points_kept = point_forward(points, centers, neighbours, mask, e_all)
    l_last = swap(l_far, "fsdp", 1)
    h_near = swap(h_core, "fsdp", 1)
    shards = (l_own, l_near, l_far, l_last)
    *kept, f_own = layer_forward(where, xp, small, pick, shards)
    hid = points_kept[-1]
    h_last = swap(h_got[1], "fsdp", 1)
    pieces = (h_own, h_near, h_got, h_last)
    f_far = swap(f_own, "fsdp", 2)
    f_near = swap(f_own, "fsdp", 1)
    f_last = swap(f_far, "fsdp", 1)
    rows = (f_own, f_near, f_far, f_last)
    e, stat = head_scores(where, rows, pieces, codes)
    stat_far = swap(stat, "fsdp", 2)
    stat_near = swap(stat, "fsdp", 1)
    stat_last = swap(stat_far, "fsdp", 1)
    d, keep, send, loss = head_back(where, e, (stat, stat_near, stat_far, stat_last), codes, pieces)
    got = swap(send, "fsdp", 1)
    got_far = swap(add(keep[1], got[1]), "fsdp", 2)
    h_grad = head_grad(where, rows, d)
    h_sum = halve(h_grad[0], h_grad[1])
    l_grad, dx, sg = layer_backward(
        where, keep, got, got_far, pick, kept, xp, small, hid, shards
    )
    h_cross = swap(h_sum[2:], "fsdp", 2)
    h_inner = swap(jnp.stack([h_sum[1], h_cross[1]]), "fsdp", 1)
    h_mine = jnp.stack([h_sum[0], h_inner[0], h_cross[0], h_inner[1]])
    h_full = double(h_mine)

    l_got = swap(l_grad[1], "fsdp", 1)
    l_got_far = swap(add(l_grad[0, 1], l_got[1]), "fsdp", 2)
    l_sum = halve(
        add(l_grad[0, 0, 0], l_got[0, 0], l_got_far[0]),
        add(l_grad[0, 0, 1], l_got[0, 1], l_got_far[1]),
    )
    l_full = double(l_sum)

    e_grad = point_backward(where, dx, points_kept, e_all, sg, loss, mask)
    e_got = swap(e_grad[1], "fsdp", 1)
    e_got_far = swap(e_grad[0, 1] + e_got[1], "fsdp", 2)
    e_sum = e_grad[0, 0] + e_got[0] + e_got_far
    bit = 1
    while bit < dp:
        e_sum = e_sum + swap(e_sum, "dp", bit)
        bit *= 2

    sums = squares(h_full, l_full, e_sum)
    sums = sums + swap(sums, "fsdp", 1)
    sums = (sums, swap(sums, "fsdp", 2))
    head_m_new, head_v_new, head_new = step_head(where, sums, e_sum, h_full, head, head_m, head_v)
    *rest, scalars = step_rest(
        where, sums, e_sum, l_full,
        (
            embed_in, embed_in_m, embed_in_v, embed_out, embed_out_m, embed_out_v,
            qkv_w, qkv_m, qkv_v, proj_w, proj_m, proj_v, fc1_w, fc1_m, fc1_v, fc2_w, fc2_m, fc2_v,
            gains, gains_m, gains_v, special, special_m, special_v,
        ),
    )
    return (
        *rest, head_m_new, head_v_new, head_new, scalars[0, 0], scalars[1, 0], scalars[2, 0]
    )


def solution(mesh):
    in_specs = (
        P(None, ("dp", "fsdp"), None),
        *[P(("dp", "fsdp"), None)] * 4,
        *[P(None, None, "fsdp")] * 3,
        *[P(None, "fsdp", None)] * 15,
        *[P(None, "fsdp")] * 6,
        *[P("fsdp", None)] * 3,
    )
    out_specs = in_specs[5:] + (P(), P(), P())
    step = functools.partial(body, mesh.shape["dp"], mesh.shape["fsdp"])
    return jax.shard_map(
        step, mesh=mesh, in_specs=in_specs, out_specs=out_specs, check_vma=False
    )
```

```python
import functools

import jax
import jax.numpy as jnp
from jax import lax
from jax.experimental import pallas as pl
from jax.experimental.pallas import tpu as pltpu
from jax.sharding import PartitionSpec as P

BF = jnp.bfloat16
F32 = jnp.float32
I32 = jnp.int32
D = 384
HEAD_DIM = 64
FF = 1536
PE = 128
NB = 32
PATCHES = 64
STEP_NUMBER = 10
MOST_MASKED = 36

BETA_ONE = 0.9
BETA_TWO = 0.95
EPSILON = 1e-08
DECAY = 0.05
RATE_MATRIX = 0.1
RATE_VECTOR = 0.5
CLIP = 0.005

TOP = 512
ROWS = 528
CAP = 288
CAPL = 384
VQ = 2048
SPLIT = 8
L_WIDE = 4608
F_ROWS = 2304
F_PIECE = F_ROWS // SPLIT
T_ROWS = 1152
T_PIECE = T_ROWS // SPLIT
H_PIECE = 192
E_ROWS = 224
E_GRAD = 216
CH = 256

GA = 0.7978845608028654
GB = GA * 0.044715


def dot(left, right, dims=((1,), (0,))):
    return lax.dot_general(left, right, (dims, ((), ())), preferred_element_type=F32)


def gelu_pair(x):
    square = x * x
    half = 0.5 * jnp.tanh(x * (GA + GB * square)) + 0.5
    value = x * half
    slope = half + (value * (1.0 - half)) * (2.0 * GA + (6.0 * GB) * square)
    return value, slope


def iota(shape, axis):
    return lax.broadcasted_iota(I32, shape, axis)


def params(mib=48):
    return pltpu.CompilerParams(vmem_limit_bytes=mib << 20)


VM = pl.BlockSpec(memory_space=pltpu.VMEM)
SM = pl.BlockSpec(memory_space=pltpu.SMEM)
HB = pl.BlockSpec(memory_space=pltpu.HBM)


def shape(dims, dtype=F32):
    return jax.ShapeDtypeStruct(dims, dtype)


def cost(flops, moved, trans=0):
    return pl.CostEstimate(flops=int(flops), bytes_accessed=int(moved), transcendentals=int(trans))


def pack_kernel(*refs):
    sources, (e_out, l_out), local, scr, sems = refs[:10], refs[10:12], refs[12:22], refs[22], refs[23]
    copies = [
        pltpu.make_async_copy(source, target, sems.at[i])
        for i, (source, target) in enumerate(zip(sources, local))
    ]
    for copy in copies:
        copy.start()
    for copy in copies[:6]:
        copy.wait()
    ein, eout, gains, special, mask, targets, qkv, proj, fc1, fc2 = local
    for i in range(2):
        for j in range(3):
            e_out[(i * 3 + j) * 32 : (i * 3 + j + 1) * 32, :] = eout[
                i, :, j * 128 : (j + 1) * 128
            ].astype(BF)
    scr[...] = jnp.zeros_like(scr)
    for k in range(3):
        for i in range(2):
            scr[i * 3 + k : i * 3 + k + 1, 0:32] = ein[k, i : i + 1, :]
    scr[6:9, 0:96] = gains[...]
    scr[9:11, 0:96] = special[...]
    hidden = mask[...].astype(F32)
    codes = targets[...]
    high = (codes >> 7).astype(F32)
    low = (codes & 127).astype(F32)
    for part, rows in enumerate((hidden, high, low)):
        for c in range(8):
            at = 16 + part * 4 + c // 2
            scr[at : at + 1, (c % 2) * 64 : (c % 2) * 64 + 64] = rows[c : c + 1, :]
    e_out[192:224, :] = scr[...].astype(BF)
    for copy in copies[6:]:
        copy.wait()
    l_out[:, 0:1152] = qkv[0].astype(BF)
    l_out[:, 1152:1536] = proj[0].astype(BF)
    l_out[:, 1536:3072] = fc1[0].astype(BF)
    for q in range(4):
        l_out[:, 3072 + q * 384 : 3456 + q * 384] = fc2[0, q * 96 : (q + 1) * 96, :].astype(BF)


def pack(*arrays):
    return pl.pallas_call(
        pack_kernel,
        out_shape=(shape((E_ROWS, 128), BF), shape((96, L_WIDE), BF)),
        in_specs=[HB] * 10,
        out_specs=(VM, VM),
        scratch_shapes=[pltpu.VMEM(array.shape, array.dtype) for array in arrays]
        + [pltpu.VMEM((32, 128), F32), pltpu.SemaphoreType.DMA((10,))],
        compiler_params=params(60),
        name="pack_weights",
    )(*arrays)


def pack_head_kernel(where, head, own, core, far):
    for pos in range(4):
        quarter = pos ^ where[0]
        piece = head[:, pl.ds(pl.multiple_of(quarter * VQ, VQ), VQ)].astype(BF)
        if pos == 0:
            own[...] = piece
        elif pos == 1:
            core[...] = piece
        else:
            far[pos - 2] = piece


def pack_head(where, head):
    return pl.pallas_call(
        pack_head_kernel,
        out_shape=(shape((96, VQ), BF), shape((96, VQ), BF), shape((2, 96, VQ), BF)),
        in_specs=[SM, VM],
        out_specs=(VM, VM, VM),
        compiler_params=params(),
        name="pack_head",
    )(where, head)


def choose_kernel(where, e_ref, code_ref, pick_ref, small_ref):
    upper = (iota((TOP, TOP), 0) <= iota((TOP, TOP), 1)).astype(F32).astype(BF)
    flags, codes = [], []
    for pos in range(4):
        rows = e_ref[pos, 208:224, :].astype(F32)
        flags.append(jnp.concatenate([rows[u : u + 1] for u in range(4)], 1))
        high = jnp.concatenate([rows[4 + u : 5 + u] for u in range(4)], 1)
        low = jnp.concatenate([rows[8 + u : 9 + u] for u in range(4)], 1)
        codes.append(high * 128.0 + low)
    stack = jnp.concatenate(flags + [jnp.zeros((4, TOP), F32)], 0).astype(BF)
    ranks = dot(stack, upper)
    for pos in range(4):
        rank = ranks[pos : pos + 1]
        chosen = (rank == (iota((CAP, TOP), 0) + 1).astype(F32)) & (flags[pos] > 0.0)
        picked = jnp.where(chosen, 1.0, 0.0)
        code = jnp.sum(picked * codes[pos], 1, keepdims=True)
        real = jnp.sum(picked, 1, keepdims=True) > 0.0
        column = jnp.where(real, code, -1.0).astype(I32)
        code_ref[pos] = jnp.broadcast_to(column, (CAP, 128))
        if pos == 0:
            pick_ref[...] = picked.astype(BF)
    for r in range(4):
        small_ref[:, r * 96 : (r + 1) * 96] = e_ref[r ^ where[0], 192:208, :].astype(F32)[:, 0:96]


def choose(where, e_all):
    return pl.pallas_call(
        choose_kernel,
        out_shape=(shape((4, CAP, 128), I32), shape((CAP, TOP), BF), shape((16, D))),
        in_specs=[SM, VM],
        out_specs=(VM, VM, VM),
        compiler_params=params(),
        cost_estimate=cost(1e4, 1e3),
        name="choose_rows",
    )(where, e_all)


def point_forward_kernel(
    where, points, centers, neighbours, mask, e_ref,
    x_ref, slope_ref, inner_ref, slope_in_ref, rel_ref, cen_ref, up_ref, slope_up_ref, hid_ref,
    turned, cloud_pts, cloud_cen, cloud_flag, w_in, w_out, w_place, mark,
):
    c = pl.program_id(0)

    @pl.when(c == 0)
    def _():
        lane = iota((8, 128), 1)
        patch = lane & 63
        for q in range(16):
            spot = (patch & 3) * 32 + 2 * q + (lane >> 6)
            found = jnp.zeros((8, 128), I32)
            for v in range(16):
                part = jnp.take_along_axis(
                    neighbours[:, v * 128 : (v + 1) * 128], spot, axis=1, mode="promise_in_bounds"
                )
                found = jnp.where((patch >> 2) == v, part, found)
            for cloud in range(8):
                turned[cloud, 0:1, q * 128 : (q + 1) * 128] = found[cloud : cloud + 1]
        merged = jnp.zeros((16, 128), F32)
        for r in range(4):
            rank = r ^ where[0]
            rows = e_ref[rank, 192:208, :].astype(F32)
            merged = merged + jnp.where(
                iota((16, 128), 1) >> 5 == r, pltpu.roll(rows, r * 32, 1), 0.0
            )
            mark[:, r * 96 : (r + 1) * 96] = rows[:, 0:96]
            for j in range(3):
                lanes = slice(j * 128, j * 128 + 128)
                w_out[r * 32 : (r + 1) * 32, lanes] = e_ref[
                    rank, j * 32 : (j + 1) * 32, :
                ].astype(F32)
                w_place[r * 32 : (r + 1) * 32, lanes] = e_ref[
                    rank, (3 + j) * 32 : (4 + j) * 32, :
                ]
        for i in range(2):
            rows = jnp.concatenate([merged[i * 3 : i * 3 + 3], jnp.zeros((125, 128), F32)], 0)
            w_in[i] = jnp.transpose(rows)
        cloud_pts[...] = jnp.zeros_like(cloud_pts)
        flags = mask[...].astype(F32)
        for cloud in range(8):
            row = slice(cloud, cloud + 1)
            for k in range(3):
                cloud_pts[cloud, k : k + 1, :] = points[k, row, :]
            cloud_cen[cloud, 0:1, 0:64] = centers[row, :]
            cloud_cen[cloud, 0:1, 64:128] = centers[row, :]
            cloud_flag[cloud, 0:1, 0:64] = flags[row, :]

    def look_up(index):
        index = jnp.broadcast_to(index, (8, 128))
        low = index & 127
        high = index >> 7
        found = jnp.zeros((8, 128), F32)
        for k in range(8):
            part = jnp.take_along_axis(
                cloud_pts[c, :, k * 128 : (k + 1) * 128], low, axis=1, mode="promise_in_bounds"
            )
            found = jnp.where(high == k, part, found)
        return found

    centre = look_up(cloud_cen[c, 0:1, :])
    in_point = w_in[0, :, 0:8].astype(BF)
    in_centre = w_in[1, :, 0:8].astype(BF)
    out_point = jnp.transpose(w_out[...]).astype(BF)
    total = jnp.zeros((D, 128), F32)
    for step in range(PATCHES * NB // CH):
        tiles = []
        for q in range(step * CH // 128, (step + 1) * CH // 128):
            near = look_up(turned[c, 0:1, q * 128 : (q + 1) * 128])
            tiles.append(near - centre)
        relative = jnp.concatenate(tiles, 1).astype(BF)
        at = slice(step * CH, (step + 1) * CH)
        rel_ref[0, :, at] = relative
        value, slope = gelu_pair(dot(in_point, relative))
        inner = value.astype(BF)
        inner_ref[0, :, at] = inner
        slope_in_ref[0, :, at] = slope.astype(BF)
        value, slope = gelu_pair(dot(out_point, inner).astype(BF))
        slope_ref[0, :, at] = slope
        for q in range(CH // 128):
            total = total + value[:, q * 128 : (q + 1) * 128].astype(F32)
    centre_b = centre.astype(BF)
    cen_ref[0] = centre_b
    value, slope = gelu_pair(dot(in_centre, centre_b))
    up = value.astype(BF)
    up_ref[0] = up
    slope_up_ref[0] = slope
    place = dot(up, w_place[...], ((0,), (0,)))[0:PATCHES]
    both = jnp.transpose(total)
    diagonal = iota((PATCHES, PATCHES), 0) == iota((PATCHES, PATCHES), 1)
    flags = jnp.broadcast_to(cloud_flag[c, 0:1, 0:64], (PATCHES, PATCHES))
    hidden = jnp.sum(jnp.where(diagonal, flags, 0.0), 1, keepdims=True)
    hid_ref[...] = jnp.broadcast_to(hidden, (PATCHES, 128))
    patch = (both[0:PATCHES] + both[PATCHES:128]) * (1.0 / NB)
    x_ref[...] = jnp.where(hidden > 0.0, mark[10:11, :], patch) + place


def point_forward(where, points, centers, neighbours, mask, e_all):
    clouds = mask.shape[0]
    tokens = PATCHES * NB

    def whole(array):
        return pl.BlockSpec(array.shape, lambda c: (0,) * array.ndim)

    def per(*dims):
        return pl.BlockSpec((1,) + dims, lambda c: (c, 0, 0))

    inputs = (points, centers, neighbours, mask, e_all)
    return pl.pallas_call(
        point_forward_kernel,
        grid=(clouds,),
        out_shape=(
            shape((TOP, D)),
            shape((clouds, D, tokens), BF),
            shape((clouds, PE, tokens), BF),
            shape((clouds, PE, tokens), BF),
            shape((clouds, 8, tokens), BF),
            shape((clouds, 8, 128), BF),
            shape((clouds, PE, 128), BF),
            shape((clouds, PE, 128)),
            shape((TOP, 128)),
        ),
        in_specs=[SM] + [whole(array) for array in inputs],
        out_specs=(
            pl.BlockSpec((PATCHES, D), lambda c: (c, 0)),
            per(D, tokens),
            per(PE, tokens),
            per(PE, tokens),
            per(8, tokens),
            per(8, 128),
            per(PE, 128),
            per(PE, 128),
            pl.BlockSpec((PATCHES, 128), lambda c: (c, 0)),
        ),
        scratch_shapes=[
            pltpu.VMEM((8, 8, tokens), I32),
            pltpu.VMEM((8, 8, 1024), F32),
            pltpu.VMEM((8, 8, 128), I32),
            pltpu.VMEM((8, 8, 128), F32),
            pltpu.VMEM((2, 128, PE), F32),
            pltpu.VMEM((PE, D), F32),
            pltpu.VMEM((PE, D), BF),
            pltpu.VMEM((16, D), F32),
        ],
        compiler_params=params(),
        cost_estimate=cost(30e9, 20e6, 8e6),
        name="point_forward",
    )(where, *inputs)


def layer_weights(where, shards, low, high, w_main, w_two):
    for pos, shard in enumerate(shards):
        rank = pos ^ where[0]
        w_main[pl.ds(pl.multiple_of(rank * 96, 96), 96), :] = shard[:, low:high]
        if w_two is None:
            continue
        for q in range(4):
            rows = pl.ds(pl.multiple_of(rank * 384 + q * 96, 96), 96)
            w_two[rows, :] = shard[:, 3072 + q * 384 : 3456 + q * 384]


def norm(x):
    centred = x - jnp.mean(x, -1, keepdims=True)
    scale = lax.rsqrt(jnp.mean(centred * centred, -1, keepdims=True) + 1e-06)
    return centred * scale, scale


def norm_back(grad, x, gain):
    hat, scale = norm(x)
    d_gain = jnp.sum(grad * hat, 0, keepdims=True)
    inner = grad * gain
    d_x = scale * (
        inner - jnp.mean(inner, -1, keepdims=True) - hat * jnp.mean(inner * hat, -1, keepdims=True)
    )
    return d_x, d_gain


def cloud_rows(ref, start, lanes):
    return jnp.concatenate([ref[pl.ds(start, 64), lanes], ref[TOP:ROWS, lanes]], 0)


def lane_masks():
    first = (iota((1, 128), 1) < HEAD_DIM).astype(F32)
    return first.astype(BF), (1.0 - first).astype(BF)


def layer_forward_kernel(
    where, xp, small, pick, s0, s1, s2, s3,
    m_ref, xo_ref, y_ref, qkv_ref, a_ref, o_ref, z_ref, act_ref, slope_ref, f_ref,
    w_main, w_two, x_all, o_cls,
):
    layer_weights(where, (s0, s1, s2, s3), 0, 3072, w_main, w_two)
    x_all[0:TOP, :] = xp[...]
    opening = jnp.broadcast_to(small[9:10, :], (16, D))
    x_all[TOP:ROWS, :] = jnp.where(iota((16, D), 0) < 8, opening, 0.0)
    hat, _ = norm(x_all[...])
    y_ref[...] = (hat * small[6:7, :]).astype(BF)
    qkv_ref[...] = dot(y_ref[...], w_main[:, 0:1152]).astype(BF)
    o_cls[...] = jnp.zeros_like(o_cls)
    mask0, mask1 = lane_masks()

    def one_cloud(c, carry):
        start = pl.multiple_of(c * 64, 64)
        column = iota((160, 80), 1)
        allowed = (column < 64) | (column == c + 64)
        for p in range(3):
            q = cloud_rows(qkv_ref, start, slice(p * 128, p * 128 + 128))
            k = cloud_rows(qkv_ref, start, slice(384 + p * 128, 512 + p * 128))
            v = cloud_rows(qkv_ref, start, slice(768 + p * 128, 896 + p * 128))
            both = jnp.concatenate([q * mask0, q * mask1], 0)
            scores = dot(both, k, ((1,), (1,))) * HEAD_DIM**-0.5
            scores = jnp.where(allowed, scores, -1e30)
            top = jnp.max(scores, -1, keepdims=True)
            e = jnp.exp(scores - top)
            a = (e / jnp.sum(e, -1, keepdims=True)).astype(BF)
            a_ref[c * 3 + p] = a
            o = dot(a, v)
            pair = jnp.where(iota((80, 128), 1) < HEAD_DIM, o[0:80], o[80:160])
            lanes = slice(p * 128, p * 128 + 128)
            o_ref[pl.ds(start, 64), lanes] = pair[0:64].astype(BF)
            o_cls[:, lanes] += jnp.where(iota((16, 128), 0) == c, pair[64:80], 0.0)
        return carry

    lax.fori_loop(0, 8, one_cloud, 0, unroll=4)
    o_ref[TOP:ROWS, :] = o_cls[...].astype(BF)
    m_ref[...] = x_all[...] + dot(o_ref[...], w_main[:, 1152:1536])
    hat, _ = norm(m_ref[...])
    z_ref[...] = (hat * small[7:8, :]).astype(BF)
    for part in range(3):
        lanes = slice(part * 512, part * 512 + 512)
        hidden = dot(z_ref[...], w_main[:, 1536 + part * 512 : 2048 + part * 512])
        value, slope = gelu_pair(hidden)
        act_ref[:, lanes] = value.astype(BF)
        slope_ref[:, lanes] = slope.astype(BF)
    xo = m_ref[0:TOP, :] + dot(act_ref[0:TOP, :], w_two[...])
    xo_ref[...] = xo
    hat, _ = norm(xo)
    f_ref[...] = dot(pick[...], (hat * small[8:9, :]).astype(BF)).astype(BF)


def layer_forward(where, xp, small, pick, shards):
    return pl.pallas_call(
        layer_forward_kernel,
        out_shape=(
            shape((ROWS, D)),
            shape((TOP, D)),
            shape((ROWS, D), BF),
            shape((ROWS, 1152), BF),
            shape((24, 160, 80), BF),
            shape((ROWS, D), BF),
            shape((ROWS, D), BF),
            shape((ROWS, FF), BF),
            shape((ROWS, FF), BF),
            shape((CAP, D), BF),
        ),
        in_specs=[SM] + [VM] * 7,
        out_specs=(VM,) * 10,
        scratch_shapes=[
            pltpu.VMEM((D, 3072), BF),
            pltpu.VMEM((FF, D), BF),
            pltpu.VMEM((ROWS, D), F32),
            pltpu.VMEM((16, D), F32),
        ],
        compiler_params=params(),
        cost_estimate=cost(1e4, 1e3),
        name="layer_forward",
    )(where, xp, small, pick, *shards)


def head_table(where, pieces, table):
    for pos, piece in enumerate(pieces):
        rows = pl.ds(pl.multiple_of((pos ^ where[0]) * 96, 96), 96)
        table[rows, :] = piece[...] if len(piece.shape) == 2 else piece[0]


def head_scores_kernel(
    where, f0, f1, f2, f3, h0, h1, h2, h3, codes, e_ref, stat_ref, table, scores
):
    head_table(where, (h0, h1, h2, h3), table)
    base = where[0] * VQ
    for pos, rows in enumerate((f0, f1, f2, f3)):
        best = jnp.full((CAP, 128), -jnp.inf, F32)
        for t in range(4):
            part = dot(rows[...], table[:, t * 512 : t * 512 + 512])
            scores[:, t * 512 : t * 512 + 512] = part
            for u in range(4):
                best = jnp.maximum(best, part[:, u * 128 : u * 128 + 128])
        top = jnp.max(best, -1, keepdims=True)
        code = codes[pos] - base
        total = jnp.zeros((CAP, 128), F32)
        aimed = jnp.zeros((CAP, 128), F32)
        for u in range(16):
            lanes = slice(u * 128, u * 128 + 128)
            part = scores[:, lanes]
            e = jnp.exp(part - top)
            e_ref[pos, :, lanes] = e.astype(BF)
            total = total + e
            aimed = aimed + jnp.where(iota((CAP, 128), 1) + u * 128 == code, part, 0.0)
        lane = iota((CAP, 128), 1)
        both = jnp.where(
            lane == 0,
            top,
            jnp.where(
                lane == 1,
                jnp.sum(total, -1, keepdims=True),
                jnp.where(lane == 2, jnp.sum(aimed, -1, keepdims=True), 0.0),
            ),
        )
        both = jnp.concatenate([both, jnp.zeros((CAPL - CAP, 128), F32)], 0)
        stat_ref[pos] = jnp.transpose(both)[0:8, :]


def head_scores(where, rows, pieces, codes):
    return pl.pallas_call(
        head_scores_kernel,
        out_shape=(shape((4, CAP, VQ), BF), shape((4, 8, CAPL))),
        in_specs=[SM] + [VM] * 9,
        out_specs=(VM, VM),
        scratch_shapes=[
            pltpu.VMEM((D, VQ), BF),
            pltpu.VMEM((CAP, VQ), F32),
        ],
        compiler_params=params(),
        cost_estimate=cost(2e9, 8e6, 3e6),
        name="head_scores",
    )(where, *rows, *pieces, codes)


def head_back_kernel(
    where, e_ref, t0, t1, t2, t3, codes, h0, h1, h2, h3,
    d_ref, keep_ref, send_ref, loss_ref, table,
):
    head_table(where, (h0, h1, h2, h3), table)
    stats = (t0, t1, t2, t3)
    columns, aims = [], []
    for pos in range(4):
        tops = [stats[q][pos ^ q, 0:1, :] for q in range(4)]
        sums = [stats[q][pos ^ q, 1:2, :] for q in range(4)]
        top = jnp.maximum(jnp.maximum(tops[0], tops[1]), jnp.maximum(tops[2], tops[3]))
        total = jnp.zeros((1, CAPL), F32)
        for q in range(4):
            total = total + sums[q] * jnp.exp(tops[q] - top)
        scale = jnp.exp(tops[0] - top) / total
        columns.append(scale)
        aims.append(jnp.exp(t0[pos, 2:3, :] - top) / total - 1.0)
        if pos == 0:
            aimed = t0[0, 2:3, :] + t1[1, 2:3, :] + t2[2, 2:3, :] + t3[3, 2:3, :]
            losses = top + jnp.log(total) - aimed
    block = jnp.concatenate(columns + aims + [losses, jnp.zeros((119, CAPL), F32)], 0)
    turned = jnp.transpose(block)[0:CAP, :]
    real = codes[0] >= 0
    loss = jnp.where(real[:, 0:1], turned[:, 8:9], 0.0)
    loss_ref[...] = jnp.broadcast_to(jnp.sum(loss, 0, keepdims=True), (8, 128))
    base = where[0] * VQ
    for pos in range(4):
        scale = jnp.where(codes[pos][:, 0:1] >= 0, turned[:, pos : pos + 1], 0.0)
        aim = turned[:, 4 + pos : 5 + pos]
        code = codes[pos] - base
        for u in range(16):
            lanes = slice(u * 128, u * 128 + 128)
            hit = iota((CAP, 128), 1) + u * 128 == code
            grad = jnp.where(hit, aim, e_ref[pos, :, lanes].astype(F32) * scale)
            d_ref[pos, :, lanes] = grad.astype(BF)
        back = dot(d_ref[pos], table[...], ((1,), (1,)))
        if pos % 2 == 0:
            keep_ref[pos // 2] = back
        else:
            send_ref[pos // 2] = back.astype(BF)


def head_back(where, e, stats, codes, pieces):
    return pl.pallas_call(
        head_back_kernel,
        out_shape=(
            shape((4, CAP, VQ), BF),
            shape((2, CAP, D)),
            shape((2, CAP, D), BF),
            shape((8, 128)),
        ),
        in_specs=[SM] + [VM] * 10,
        out_specs=(VM,) * 4,
        scratch_shapes=[pltpu.VMEM((D, VQ), BF)],
        compiler_params=params(),
        cost_estimate=cost(2e9, 12e6),
        name="head_back",
    )(where, e, *stats, codes, *pieces)


def place_y(rel):
    return rel & 1, ((rel >> 1) & 1) * 2 + ((rel >> 2) & 1)


def place_z(rel):
    return (rel >> 1) & 1, ((rel >> 2) & 1) * 2 + (rel & 1)


def head_grad_kernel(where, f0, f1, f2, f3, d_ref, a_keep, a_send, b_keep, b_send, joined, held):
    for pos, rows in enumerate((f0, f1, f2, f3)):
        joined[:, pos * CAP : (pos + 1) * CAP] = jnp.transpose(rows[...].astype(F32)).astype(BF)
    for rel in range(SPLIT):
        lanes = pl.ds(pl.multiple_of((rel ^ where[1]) * 256, 256), 256)
        cols = jnp.concatenate([d_ref[pos, :, lanes] for pos in range(4)], 0)
        held[rel % 2] = dot(joined[...], cols).astype(BF)
        first_a, index_a = place_y(rel)
        first_b, index_b = place_z(rel)
        for pos in range(4):
            rows = held[rel % 2, pl.ds(pl.multiple_of((pos ^ where[0]) * 96, 96), 96), :]
            if pos < 2:
                ref, index = (a_send if first_a else a_keep), index_a
            else:
                ref, index = (b_send if first_b else b_keep), index_b
            for j in range(2):
                ref[index, pos & 1, j * 96 : j * 96 + 96, :] = rows[:, j * 128 : j * 128 + 128]


def head_grad(where, rows, d):
    return pl.pallas_call(
        head_grad_kernel,
        out_shape=(shape((4, 2, H_PIECE, 128), BF),) * 4,
        in_specs=[SM] + [VM] * 5,
        out_specs=(VM,) * 4,
        scratch_shapes=[pltpu.VMEM((D, 4 * CAP), BF), pltpu.VMEM((2, D, 256), BF)],
        compiler_params=params(),
        cost_estimate=cost(4e9, 8e6),
        name="head_grad",
    )(where, *rows, d)


def hold_grad(held, block, grad):
    for r in range(4):
        held[r, block * 96 : block * 96 + 96, :] = grad[r * 96 : r * 96 + 96, :].astype(BF)


def spread_grad(where, held, keep, send, piece_rows, far_first):
    for pos in range(4):
        ref, far = (send if pos & 1 else keep), pos >> 1
        for rel in range(SPLIT):
            first, index = place_y(rel)
            start = pl.multiple_of((rel ^ where[1]) * piece_rows, 16)
            rows = held[pos ^ where[0], pl.ds(start, piece_rows), :]
            if far_first:
                ref[far, first, index] = rows
            else:
                ref[first, far, index] = rows


def ffn_backward_kernel(
    where, keep, rc, rx, pick, xo, m_ref, small, z_ref, act_ref, slope_ref, s0, s1, s2, s3,
    keep_ref, send_ref, dm_ref, sg_ref,
    w_main, w_two, d_hid, held,
):
    layer_weights(where, (s0, s1, s2, s3), 1536, 3072, w_main, w_two)
    compact = keep[0] + rc[0].astype(F32) + rx[...].astype(F32)
    high = compact.astype(BF)
    low = (compact - high.astype(F32)).astype(BF)
    d_rows = dot(pick[...], high, ((0,), (0,))) + dot(pick[...], low, ((0,), (0,)))
    d_out, d_gain = norm_back(d_rows, xo[...], small[8:9, :])
    sg_ref[...] = jnp.zeros_like(sg_ref)
    sg_ref[1:2, :] = d_gain
    grad_b = d_out.astype(BF)
    for part in range(3):
        lanes = slice(part * 512, part * 512 + 512)
        back = dot(grad_b, w_two[lanes, :], ((1,), (1,)))
        d_hid[:, lanes] = (back * slope_ref[0:TOP, lanes].astype(F32)).astype(BF)
    d_fc2 = dot(jnp.transpose(d_out).astype(BF), act_ref[0:TOP, :])
    for j in range(3):
        for q in range(4):
            parts = [
                d_fc2[q * 96 : q * 96 + 96, r * 384 + j * 128 : r * 384 + j * 128 + 128]
                for r in range(4)
            ]
            hold_grad(held, 12 + j * 4 + q, jnp.concatenate(parts, 0))
    turned = jnp.transpose(z_ref[0:TOP, :].astype(F32)).astype(BF)
    for part in range(3):
        grad = dot(turned, d_hid[:, part * 512 : part * 512 + 512])
        for j in range(4):
            hold_grad(held, part * 4 + j, grad[:, j * 128 : j * 128 + 128])
    spread_grad(where, held, keep_ref, send_ref, F_PIECE, True)
    d_z = dot(d_hid[...], w_main[...], ((1,), (1,)))
    d_m, d_gain = norm_back(d_z, m_ref[0:TOP, :], small[7:8, :])
    sg_ref[0:1, :] = d_gain
    dm_ref[...] = d_m + d_out


def ffn_backward(where, keep, rc, rx, pick, xo, m, small, z, act, slope, shards):
    return pl.pallas_call(
        ffn_backward_kernel,
        out_shape=(
            shape((2, 2, 4, F_PIECE, 128), BF),
            shape((2, 2, 4, F_PIECE, 128), BF),
            shape((TOP, D)),
            shape((8, D)),
        ),
        in_specs=[SM] + [VM] * 14,
        out_specs=(VM,) * 4,
        scratch_shapes=[
            pltpu.VMEM((D, FF), BF),
            pltpu.VMEM((FF, D), BF),
            pltpu.VMEM((TOP, FF), BF),
            pltpu.VMEM((4, F_ROWS, 128), BF),
        ],
        compiler_params=params(),
        cost_estimate=cost(10e9, 10e6),
        name="ffn_backward",
    )(where, keep, rc, rx, pick, xo, m, small, z, act, slope, *shards)


def attention_backward_kernel(
    where, dm_ref, sgf, xp, small, y_ref, qkv_ref, a_ref, o_ref, hid, s0, s1, s2, s3,
    keep_ref, send_ref, dx_ref, sg_ref,
    w_main, x_all, d_o, d_qkv, d_cls, held,
):
    layer_weights(where, (s0, s1, s2, s3), 0, 1536, w_main, None)
    x_all[0:TOP, :] = xp[...]
    opening = jnp.broadcast_to(small[9:10, :], (16, D))
    x_all[TOP:ROWS, :] = jnp.where(iota((16, D), 0) < 8, opening, 0.0)
    m_b = dm_ref[...].astype(BF)
    d_o[...] = dot(m_b, w_main[:, 1152:1536], ((1,), (1,))).astype(BF)
    d_cls[...] = jnp.zeros_like(d_cls)
    mask0, mask1 = lane_masks()

    def one_cloud(c, carry):
        start = pl.multiple_of(c * 64, 64)
        for p in range(3):
            lanes = slice(p * 128, p * 128 + 128)
            q = qkv_ref[pl.ds(start, 64), lanes]
            k = cloud_rows(qkv_ref, start, slice(384 + p * 128, 512 + p * 128))
            v = cloud_rows(qkv_ref, start, slice(768 + p * 128, 896 + p * 128))
            d = d_o[pl.ds(start, 64), lanes]
            q2 = jnp.concatenate([q * mask0, q * mask1], 0)
            d2 = jnp.concatenate([d * mask0, d * mask1], 0)
            a = jnp.concatenate([a_ref[c * 3 + p, 0:64, :], a_ref[c * 3 + p, 80:144, :]], 0)
            d_a = dot(d2, v, ((1,), (1,)))
            full = a.astype(F32)
            d_s = full * (d_a - jnp.sum(d_a * full, -1, keepdims=True)) * HEAD_DIM**-0.5
            d_s = d_s.astype(BF)
            d_q = dot(d_s, k)
            d_q = jnp.where(iota((64, 128), 1) < HEAD_DIM, d_q[0:64], d_q[64:128])
            d_k = dot(d_s, q2, ((0,), (0,)))
            d_v = dot(a, d2, ((0,), (0,)))
            d_qkv[pl.ds(start, 64), p * 128 : p * 128 + 128] = d_q.astype(BF)
            d_qkv[pl.ds(start, 64), 384 + p * 128 : 512 + p * 128] = d_k[0:64].astype(BF)
            d_qkv[pl.ds(start, 64), 768 + p * 128 : 896 + p * 128] = d_v[0:64].astype(BF)
            d_cls[:, 384 + p * 128 : 512 + p * 128] += d_k[64:80]
            d_cls[:, 768 + p * 128 : 896 + p * 128] += d_v[64:80]
        return carry

    lax.fori_loop(0, 8, one_cloud, 0, unroll=4)
    d_qkv[TOP:ROWS, :] = d_cls[...].astype(BF)
    turned = jnp.transpose(o_ref[0:TOP, :].astype(F32)).astype(BF)
    grad = dot(turned, m_b)
    for j in range(3):
        hold_grad(held, 9 + j, grad[:, j * 128 : j * 128 + 128])
    turned = jnp.transpose(y_ref[...].astype(F32)).astype(BF)
    for part in range(3):
        grad = dot(turned, d_qkv[:, part * 384 : part * 384 + 384])
        for j in range(3):
            hold_grad(held, part * 3 + j, grad[:, j * 128 : j * 128 + 128])
    spread_grad(where, held, keep_ref, send_ref, T_PIECE, False)
    d_y = dot(d_qkv[...], w_main[:, 0:1152], ((1,), (1,)))
    d_x, d_gain = norm_back(d_y, x_all[...], small[6:7, :])
    d_x = d_x + jnp.concatenate([dm_ref[...], jnp.zeros((16, D), F32)], 0)
    dx_ref[...] = d_x
    sg_ref[...] = jnp.zeros_like(sg_ref)
    sg_ref[6:7, :] = d_gain
    sg_ref[7:9, :] = sgf[0:2, :]
    sg_ref[9:10, :] = jnp.sum(d_x[TOP:ROWS], 0, keepdims=True)
    sg_ref[10:11, :] = jnp.sum(
        jnp.where(hid[:, 0:1] > 0.0, d_x[0:TOP], 0.0), 0, keepdims=True
    )


def attention_backward(where, dm, sgf, xp, small, y, qkv, a, o, hid, shards):
    return pl.pallas_call(
        attention_backward_kernel,
        out_shape=(
            shape((2, 2, 4, T_PIECE, 128), BF),
            shape((2, 2, 4, T_PIECE, 128), BF),
            shape((ROWS, D)),
            shape((16, D)),
        ),
        in_specs=[SM] + [VM] * 13,
        out_specs=(VM,) * 4,
        scratch_shapes=[
            pltpu.VMEM((D, FF), BF),
            pltpu.VMEM((ROWS, D), F32),
            pltpu.VMEM((TOP, D), BF),
            pltpu.VMEM((ROWS, 1152), BF),
            pltpu.VMEM((16, 1152), F32),
            pltpu.VMEM((4, T_ROWS, 128), BF),
        ],
        compiler_params=params(),
        cost_estimate=cost(10e9, 10e6),
        name="attention_backward",
    )(where, dm, sgf, xp, small, y, qkv, a, o, hid, *shards)


def point_backward_kernel(
    where, dx_ref, hid, slope_ref, inner_ref, slope_in_ref, rel_ref, cen_ref, up_ref, slope_up_ref,
    e_ref, *rest,
):
    c = pl.program_id(0)
    first, last = len(rest) == 5, len(rest) == 11
    w_out, spread, lift = rest[-3:]
    if first:
        d_out, d_in = rest[:2]
    elif last:
        start_out, start_in, sg_ref, loss_ref, mask, g_ref, d_out, d_in = rest[:8]
    else:
        start_out, start_in, d_out, d_in = rest[:4]

    @pl.when(c == 0)
    def _():
        for r in range(4):
            for i in range(2):
                for j in range(3):
                    w_out[i, r * 32 : (r + 1) * 32, j * 128 : (j + 1) * 128] = e_ref[
                        r ^ where[0], (i * 3 + j) * 32 : (i * 3 + j + 1) * 32, :
                    ]
        if first:
            d_out[...] = jnp.zeros_like(d_out)
            d_in[...] = jnp.zeros_like(d_in)
        else:
            d_out[...] = start_out[...]
            d_in[...] = start_in[...]

    across = ((1,), (1,))
    rows = dx_ref[...]
    place = rows.astype(BF)
    d_out[1] += dot(up_ref[0, :, 0:PATCHES], place)
    d_up = (dot(w_out[1], place, across) * slope_up_ref[0, :, 0:PATCHES]).astype(BF)
    d_in[1] += dot(d_up, cen_ref[0, :, 0:PATCHES], across)
    d_patch = jnp.where(hid[:, 0:1] > 0.0, 0.0, rows) * (1.0 / NB)
    turned = jnp.transpose(jnp.concatenate([d_patch, d_patch], 0))
    for step in range(PATCHES * NB // CH):
        at = slice(step * CH, (step + 1) * CH)
        for q in range(step * CH // 128, (step + 1) * CH // 128):
            lanes = slice(q * 128, q * 128 + 128)
            spread[:, lanes] = (turned * slope_ref[0, :, lanes].astype(F32)).astype(BF)
        back = dot(w_out[0], spread[:, at])
        lift[:, at] = (back * slope_in_ref[0, :, at].astype(F32)).astype(BF)
    d_out[0] += dot(inner_ref[0], spread[...], across)
    d_in[0] += dot(lift[...], rel_ref[0], across)
    if not last:
        return

    @pl.when(c == pl.num_programs(0) - 1)
    def _():
        lane = iota((8, 128), 1)
        seen = jnp.sum(jnp.sum(mask[...].astype(F32), 1, keepdims=True), 0, keepdims=True)
        ins = [
            jnp.transpose(jnp.concatenate([d_in[i], jnp.zeros((PE, 120), F32)], 1))[0:8]
            for i in range(2)
        ]
        for r in range(4):
            pos = r ^ where[0]
            core, far = pos & 1, pos >> 1
            for i in range(2):
                for j in range(3):
                    g_ref[core, far, (i * 3 + j) * 32 : (i * 3 + j + 1) * 32, :] = d_out[
                        i, r * 32 : (r + 1) * 32, j * 128 : (j + 1) * 128
                    ]
            g_ref[core, far, 192:216, :] = jnp.zeros((24, 128), F32)
            turn = (128 - r * 32) % 128
            for i in range(2):
                rolled = ins[i] if turn == 0 else pltpu.roll(ins[i], turn, 1)
                rolled = jnp.where(lane < 32, rolled, 0.0)
                g_ref[core, far, 192 + i * 3 : 195 + i * 3, :] = rolled[0:3]
            g_ref[core, far, 198:203, 0:96] = sg_ref[6:11, r * 96 : (r + 1) * 96]
            g_ref[core, far, 208:209, :] = loss_ref[0:1, :]
            g_ref[core, far, 209:210, :] = jnp.broadcast_to(seen, (1, 128))


def point_backward(where, dx, kept, e_all, part, parts, start=(), last=()):
    slope, inner, slope_in, rel, cen, up, slope_up, hid = kept
    half = slope.shape[0] // parts
    tokens = PATCHES * NB

    def whole(array):
        return pl.BlockSpec(array.shape, lambda c: (0,) * len(array.shape))

    def per(*dims):
        return pl.BlockSpec((1,) + dims, lambda c: (c + part * half, 0, 0))

    sums = (shape((2, PE, D)), shape((2, PE, 8)))
    more = (*start, *last)
    packed = shape((2, 2, E_GRAD, 128))
    return pl.pallas_call(
        point_backward_kernel,
        grid=(half,),
        out_shape=packed if last else sums,
        in_specs=[
            SM,
            pl.BlockSpec((PATCHES, D), lambda c: (c + part * half, 0)),
            pl.BlockSpec((PATCHES, 128), lambda c: (c + part * half, 0)),
            per(D, tokens),
            per(PE, tokens),
            per(PE, tokens),
            per(8, tokens),
            per(8, 128),
            per(PE, 128),
            per(PE, 128),
            whole(e_all),
            *[whole(array) for array in more],
        ],
        out_specs=whole(packed) if last else tuple(whole(array) for array in sums),
        scratch_shapes=([pltpu.VMEM(array.shape, F32) for array in sums] if last else [])
        + [
            pltpu.VMEM((2, PE, D), BF),
            pltpu.VMEM((D, tokens), BF),
            pltpu.VMEM((PE, tokens), BF),
        ],
        compiler_params=params(),
        cost_estimate=cost(6e9, 6e6),
        name="point_backward",
    )(where, dx, hid, slope, inner, slope_in, rel, cen, up, slope_up, e_all, *more)


def squares_kernel(*refs):
    total = jnp.zeros((16, 128), F32)
    for ref in refs[:-2]:
        rows = ref.shape[-2]
        for lead in range(ref.shape[0] * (ref.shape[1] if len(ref.shape) == 4 else 1)):
            part = ref[divmod(lead, ref.shape[1])] if len(ref.shape) == 4 else ref[lead]
            part = part.astype(F32)
            total = total + jnp.sum((part * part).reshape(rows // 16, 16, 128), 0)
    part = refs[-2][0:208, :]
    total = total + jnp.sum((part * part).reshape(13, 16, 128), 0)
    total = jnp.sum(jnp.sum(total, 1, keepdims=True), 0, keepdims=True)
    refs[-1][...] = jnp.broadcast_to(total, (8, 128))


def squares(*arrays):
    return pl.pallas_call(
        squares_kernel,
        out_shape=shape((8, 128)),
        in_specs=[VM] * len(arrays),
        out_specs=VM,
        compiler_params=params(),
        name="squares",
    )(*arrays)


def adam(grad, first, second, weight, factor, vector):
    rate = RATE_VECTOR if vector else RATE_MATRIX
    clipped = grad * factor
    first = BETA_ONE * first + (1 - BETA_ONE) * clipped
    second = BETA_TWO * second + (1 - BETA_TWO) * (clipped * clipped)
    level = second * (1.0 / (1 - BETA_TWO**STEP_NUMBER))
    root = level * lax.rsqrt(level) + EPSILON
    update = (first * (rate / (1 - BETA_ONE**STEP_NUMBER))) * pl.reciprocal(root)
    if vector:
        return first, second, weight - update
    return first, second, weight * (1.0 - rate * DECAY) - update


def clip_factor(s0, s1, e_ref):
    count = e_ref[209:210, :]
    length = jnp.sqrt(s0[0:1, :] + s1[0:1, :]) / count
    return jnp.minimum(1.0, CLIP / length) / count, length


def step_kernel(where, s0, s1, e_ref, f0, f1, t0, t1, a0, a1, b0, b1, *refs):
    ins, outs, scalars = refs[:27], refs[27:54], refs[54]
    done, joined, turned, sems = refs[55:82], refs[82], refs[83], refs[84]
    factor, length = clip_factor(s0, s1, e_ref)
    copies = []

    def send(which, at=None):
        for k in range(3):
            i = which * 3 + k
            source = done[i] if at is None else done[i].at[at]
            target = outs[i] if at is None else outs[i].at[at]
            copy = pltpu.make_async_copy(source, target, sems.at[len(copies)])
            copy.start()
            copies.append(copy)

    def update(which, at, grad, vector=False):
        w, m, v = (ins[which * 3 + k] for k in range(3))
        out = adam(grad, m[at], v[at], w[at], factor[:, 0 : grad.shape[-1]], vector)
        for k in range(3):
            done[which * 3 + k][at] = out[k]

    for piece in range(SPLIT):
        first, index = place_y(piece ^ where[1])
        rows = slice(T_ROWS + piece * F_PIECE, T_ROWS + (piece + 1) * F_PIECE)
        joined[rows, :] = jnp.where(first == 0, f0[index], f1[index])
        first, index = place_z(piece ^ where[1])
        rows = slice(piece * T_PIECE, (piece + 1) * T_PIECE)
        joined[rows, :] = jnp.where(first == 0, t0[index], t1[index])

    starts = {0: (2, 0), 9: (3, 9), 12: (4, 12)}
    which = base = 0
    for block in range(36):
        grad = joined[block * 96 : block * 96 + 96, :].astype(F32)
        if block >= 24:
            j, q = divmod(block - 24, 4)
            turned[q * 96 : q * 96 + 96, j * 128 : j * 128 + 128] = grad
            continue
        if block in starts:
            which, base = starts[block]
        j = block - base
        update(which, (0, slice(None), slice(j * 128, j * 128 + 128)), grad)
        if block in (8, 11, 23):
            send(which)
    grad = jnp.transpose(turned[...])
    for j in range(3):
        lanes = slice(j * 128, j * 128 + 128)
        update(5, (0, slice(None), lanes), grad[:, lanes])
    send(5)
    for i in range(2):
        for k in range(3):
            at = 192 + i * 3 + k
            update(0, (k, slice(i, i + 1)), e_ref[at : at + 1, 0:32])
        for j in range(3):
            block = i * 3 + j
            grad = e_ref[block * 32 : block * 32 + 32, :]
            update(1, (i, slice(None), slice(j * 128, j * 128 + 128)), grad)
    update(6, (slice(0, 3),), e_ref[198:201, 0:96], True)
    update(7, (slice(0, 2),), e_ref[201:203, 0:96], True)
    for which in (0, 1, 6, 7):
        send(which)
    scalars[0:1, :] = e_ref[208:209, :]
    scalars[1:2, :] = e_ref[209:210, :]
    scalars[2:3, :] = length
    for piece in range(32):
        quarter = (piece // SPLIT) ^ where[0]
        first_a, index_a = place_y((piece % SPLIT) ^ where[1])
        first_b, index_b = place_z((piece % SPLIT) ^ where[1])
        for j in range(2):
            lanes = slice(piece * 256 + j * 128, piece * 256 + j * 128 + 128)
            rows = slice(j * 96, j * 96 + 96)
            near = quarter & 1
            grad = jnp.where(
                quarter < 2,
                jnp.where(first_a == 0, a0[index_a, near, rows, :], a1[index_a, near, rows, :]),
                jnp.where(first_b == 0, b0[index_b, near, rows, :], b1[index_b, near, rows, :]),
            )
            update(8, (slice(None), lanes), grad.astype(F32))
        if piece % 4 == 3:
            send(8, (slice(None), slice((piece - 3) * 256, (piece + 1) * 256)))
    for copy in copies:
        copy.wait()


def step_all(where, sums, e, grads, states):
    outs = tuple(shape(array.shape) for array in states)
    return pl.pallas_call(
        step_kernel,
        out_shape=outs + (shape((8, 128)),),
        in_specs=[SM] + [VM] * (11 + len(states)),
        out_specs=(HB,) * len(outs) + (VM,),
        scratch_shapes=[pltpu.VMEM(array.shape, F32) for array in states]
        + [
            pltpu.VMEM((T_ROWS + F_ROWS, 128), BF),
            pltpu.VMEM((D, D), F32),
            pltpu.SemaphoreType.DMA((48,)),
        ],
        compiler_params=params(24),
        cost_estimate=cost(4e7, 3e7),
        name="step_all",
    )(where, *sums, e, *grads, *states)


def add(*parts):
    total = parts[0].astype(F32)
    for part in parts[1:]:
        total = total + part.astype(F32)
    return total.astype(BF)


def after(*arrays):
    return lax.optimization_barrier(arrays)


def body(dp, fsdp, *args):
    (
        points, centers, neighbours, mask, targets,
        embed_in, embed_in_m, embed_in_v, embed_out, embed_out_m, embed_out_v,
        qkv_w, qkv_m, qkv_v, proj_w, proj_m, proj_v, fc1_w, fc1_m, fc1_v, fc2_w, fc2_m, fc2_v,
        gains, gains_m, gains_v, special, special_m, special_v, head, head_m, head_v,
    ) = args
    rank = lax.axis_index("fsdp").astype(I32)
    group = lax.axis_index("dp").astype(I32)
    where = jnp.stack([rank, group % SPLIT])

    def swap(x, axis, bit):
        size = dp if axis == "dp" else fsdp
        return lax.ppermute(x, axis, [(i, i ^ bit) for i in range(size)])

    def higher(total):
        bit = SPLIT
        while bit < dp:
            total = add(total, swap(total, "dp", bit))
            bit *= 2
        return total

    embed_in, embed_in_m, embed_in_v = (
        jnp.transpose(array, (1, 0, 2)) for array in (embed_in, embed_in_m, embed_in_v)
    )
    e_own, l_own = pack(
        embed_in, embed_out, gains, special, mask, targets, qkv_w, proj_w, fc1_w, fc2_w
    )
    e_far = swap(e_own, "fsdp", 2)
    e_all = jnp.stack([e_own, swap(e_own, "fsdp", 1), e_far, swap(e_far, "fsdp", 1)])
    l_ready, head_ready, e_all = after(l_own, head, e_all)
    l_far = swap(l_ready, "fsdp", 2)
    h_own, h_core, h_far = pack_head(where, head_ready)
    h_got = swap(h_far, "fsdp", 2)
    e_all, h_own = after(e_all, h_own)
    xp, *points_kept = point_forward(where, points, centers, neighbours, mask, e_all)
    l_far, xp, e_late = after(l_far, xp, e_all)
    l_near = swap(l_ready, "fsdp", 1)
    l_last = swap(l_far, "fsdp", 1)
    h_near = swap(h_core, "fsdp", 1)
    codes, pick, small = choose(where, e_late)
    shards = (l_own, l_near, l_far, l_last)
    *kept, f_own = layer_forward(where, xp, small, pick, shards)
    m, xo, y, qkv, a, o, z, act, slope = kept
    hid = points_kept[-1]
    f_far = swap(f_own, "fsdp", 2)
    f_near = swap(f_own, "fsdp", 1)
    h_got, f_far = after(h_got, f_far)
    h_last = swap(h_got[1], "fsdp", 1)
    pieces = (h_own, h_near, h_got, h_last)
    f_last = swap(f_far, "fsdp", 1)
    rows = (f_own, f_near, f_far, f_last)
    e, stat = head_scores(where, rows, pieces, codes)
    stat_far = swap(stat, "fsdp", 2)
    stat_near = swap(stat, "fsdp", 1)
    stat_last = swap(stat_far, "fsdp", 1)
    d, keep, send, loss = head_back(where, e, (stat, stat_near, stat_far, stat_last), codes, pieces)
    got = swap(send, "fsdp", 1)
    passed, d = after(add(keep[1], got[1]), d)
    got_far = swap(passed, "fsdp", 2)
    a_keep, a_send, b_keep, b_send = head_grad(where, rows, d)

    a_send, b_send, got_far = after(a_send, b_send, got_far)
    a_1 = swap(a_send, "dp", 1)
    b_1 = swap(b_send, "dp", 2)
    f_keep, f_send, dm, sgf = ffn_backward(
        where, keep, got, got_far, pick, xo, m, small, z, act, slope, shards
    )
    a_1, b_1, f_send, dm = after(a_1, b_1, f_send, dm)
    a_2 = swap(add(a_keep[2:], a_1[2:]), "dp", 2)
    b_2 = swap(add(b_keep[2:], b_1[2:]), "dp", 4)
    f_core = swap(f_send, "fsdp", 1)
    t_keep, t_send, dx, sg = attention_backward(
        where, dm, sgf, xp, small, y, qkv, a, o, hid, shards
    )
    a_2, b_2, f_core, t_send, dx = after(a_2, b_2, f_core, t_send, dx)
    a_low = add(a_keep[:2], a_1[:2])
    b_low = add(b_keep[:2], b_1[:2])
    a_3 = swap(add(a_low[1], a_2[1]), "dp", 4)
    b_3 = swap(add(b_low[1], b_2[1]), "dp", 1)
    f_x = swap(add(f_keep[1], f_core[1]), "fsdp", 2)
    t_core = swap(t_send, "fsdp", 1)
    part = point_backward(where, dx, points_kept, e_all, 0, 4)
    a_3, b_3, t_core, part = after(a_3, b_3, t_core, part)
    a_sum = higher(add(a_low[0], a_2[0], a_3))
    b_sum = higher(add(b_low[0], b_2[0], b_3))
    cross = swap(b_sum, "fsdp", 2)
    t_y = swap(add(t_keep[1], t_core[1]), "dp", 1)
    part = point_backward(where, dx, points_kept, e_all, 1, 4, part)
    cross, part = after(cross, part)
    inner = swap(jnp.stack([a_sum[1], cross[1]]), "fsdp", 1)
    part = point_backward(where, dx, points_kept, e_all, 2, 4, part)
    inner, f_x, t_y, part = after(inner, f_x, t_y, part)
    a_mine = jnp.stack([a_sum[0], inner[0]])
    b_mine = jnp.stack([cross[0], inner[1]])
    a_two = swap(a_mine, "dp", 4)
    b_two = swap(b_mine, "dp", 1)
    f_low = add(f_keep[0], f_core[0], f_x)
    f_y = swap(f_low[1], "dp", 1)
    t_low = add(t_keep[0], t_core[0], t_y)
    t_x = swap(t_low[1], "fsdp", 2)
    e_grad = point_backward(where, dx, points_kept, e_all, 3, 4, part, (sg, loss, mask))
    e_grad, a_two, b_two, f_y, t_x = after(e_grad, a_two, b_two, f_y, t_x)

    e_core = swap(e_grad[1], "fsdp", 1)
    a_both = jnp.stack([a_mine, a_two])
    b_both = jnp.stack([b_mine, b_two])
    a_pair = swap(a_both, "dp", 2)
    b_pair = swap(b_both, "dp", 4)
    f_z1 = swap(add(f_low[0, 2:], f_y[2:]), "dp", 2)
    t_z1 = swap(add(t_low[0, 2:], t_x[2:]), "dp", 2)
    e_x = swap(e_grad[0, 1] + e_core[1], "fsdp", 2)
    f_z1, t_z1, e_x, a_pair, b_pair = after(f_z1, t_z1, e_x, a_pair, b_pair)
    f_deep = add(f_low[0, :2], f_y[:2])
    t_deep = add(t_low[0, :2], t_x[:2])
    f_z2 = swap(add(f_deep[1], f_z1[1]), "dp", 4)
    t_z2 = swap(add(t_deep[1], t_z1[1]), "dp", 4)
    e_sum = e_grad[0, 0] + e_core[0] + e_x
    e_y = swap(e_sum, "dp", 1)
    a_four = jnp.concatenate([a_both, a_pair], 0)
    b_four = jnp.concatenate([b_both, b_pair], 0)
    b_end = swap(b_four, "dp", 2)
    f_z2, t_z2, e_y, a_four = after(f_z2, t_z2, e_y, a_four)
    f_sum = higher(add(f_deep[0], f_z1[0], f_z2))
    t_sum = higher(add(t_deep[0], t_z1[0], t_z2))
    e_sum = e_sum + e_y
    e_z1 = swap(e_sum, "dp", 2)
    f_two = swap(f_sum, "dp", 4)
    t_two = swap(t_sum, "dp", 1)
    a_end = swap(a_four, "dp", 1)
    e_z1, f_two, t_two, b_end = after(e_z1, f_two, t_two, b_end)
    e_sum = e_sum + e_z1
    e_z2 = swap(e_sum, "dp", 4)
    f_both = jnp.stack([f_sum, f_two])
    t_both = jnp.stack([t_sum, t_two])
    f_pair = swap(f_both, "dp", 2)
    t_pair = swap(t_both, "dp", 4)
    e_z2, f_pair, t_pair, a_end = after(e_z2, f_pair, t_pair, a_end)
    e_sum = e_sum + e_z2
    bit = SPLIT
    while bit < dp:
        e_sum = e_sum + swap(e_sum, "dp", bit)
        bit *= 2
    f_four = jnp.concatenate([f_both, f_pair], 0)
    t_four = jnp.concatenate([t_both, t_pair], 0)
    f_end = swap(f_four, "dp", 1)
    t_end = swap(t_four, "dp", 2)
    grads = (f_four, f_end, t_four, t_end, a_four, a_end, b_four, b_end)

    sums = squares(*grads, e_sum)
    sums = sums + swap(sums, "fsdp", 1)
    sums = (sums, swap(sums, "fsdp", 2))
    states = (
        embed_in, embed_in_m, embed_in_v, embed_out, embed_out_m, embed_out_v,
        qkv_w, qkv_m, qkv_v, proj_w, proj_m, proj_v, fc1_w, fc1_m, fc1_v, fc2_w, fc2_m, fc2_v,
        gains, gains_m, gains_v, special, special_m, special_v, head, head_m, head_v,
    )
    *news, scalars = step_all(where, sums, e_sum, grads, states)
    news[:3] = [jnp.transpose(array, (1, 0, 2)) for array in news[:3]]
    return (*news, scalars[0, 0], scalars[1, 0], scalars[2, 0])


def solution(mesh):
    in_specs = (
        P(None, ("dp", "fsdp"), None),
        *[P(("dp", "fsdp"), None)] * 4,
        *[P(None, None, "fsdp")] * 3,
        *[P(None, "fsdp", None)] * 15,
        *[P(None, "fsdp")] * 6,
        *[P("fsdp", None)] * 3,
    )
    out_specs = in_specs[5:] + (P(), P(), P())
    step = functools.partial(body, mesh.shape["dp"], mesh.shape["fsdp"])
    return jax.shard_map(
        step, mesh=mesh, in_specs=in_specs, out_specs=out_specs, check_vma=False
    )
```

```python
import functools

import jax
import jax.numpy as jnp
from jax import lax
from jax.experimental import pallas as pl
from jax.experimental.pallas import tpu as pltpu
from jax.sharding import PartitionSpec as P

BF = jnp.bfloat16
F32 = jnp.float32
I32 = jnp.int32
D = 384
HEAD_DIM = 64
FF = 1536
PE = 128
NB = 32
PATCHES = 64
STEP_NUMBER = 10
MOST_MASKED = 36

BETA_ONE = 0.9
BETA_TWO = 0.95
EPSILON = 1e-08
DECAY = 0.05
RATE_MATRIX = 0.1
RATE_VECTOR = 0.5
CLIP = 0.005

TOP = 512
ROWS = 528
CAP = 288
CAPL = 384
VQ = 2048
SPLIT = 8
L_WIDE = 4608
L_HALF = 2304
F_ROWS = 2304
F_PIECE = F_ROWS // SPLIT
T_ROWS = 1152
T_PIECE = T_ROWS // SPLIT
H_PIECE = 192
E_ROWS = 224
E_GRAD = 216
CH = 256

GA = 0.7978845608028654
GB = GA * 0.044715


def dot(left, right, dims=((1,), (0,))):
    return lax.dot_general(left, right, (dims, ((), ())), preferred_element_type=F32)


def gelu_pair(x):
    square = x * x
    half = 0.5 * jnp.tanh(x * (GA + GB * square)) + 0.5
    value = x * half
    slope = half + (value * (1.0 - half)) * (2.0 * GA + (6.0 * GB) * square)
    return value, slope


def iota(shape, axis):
    return lax.broadcasted_iota(I32, shape, axis)


def params(mib=48):
    return pltpu.CompilerParams(vmem_limit_bytes=mib << 20)


VM = pl.BlockSpec(memory_space=pltpu.VMEM)
SM = pl.BlockSpec(memory_space=pltpu.SMEM)
HB = pl.BlockSpec(memory_space=pltpu.HBM)


def shape(dims, dtype=F32):
    return jax.ShapeDtypeStruct(dims, dtype)


def cost(flops, moved, trans=0):
    return pl.CostEstimate(flops=int(flops), bytes_accessed=int(moved), transcendentals=int(trans))


def pack_kernel(*refs):
    sources, (e_out, l_out, l_send) = refs[:10], refs[10:13]
    local, scr, sems = refs[13:23], refs[23], refs[24]
    copies = [
        pltpu.make_async_copy(source, target, sems.at[i])
        for i, (source, target) in enumerate(zip(sources, local))
    ]
    for copy in copies:
        copy.start()
    for copy in copies[:6]:
        copy.wait()
    ein, eout, gains, special, mask, targets, qkv, proj, fc1, fc2 = local
    for i in range(2):
        for j in range(3):
            e_out[(i * 3 + j) * 32 : (i * 3 + j + 1) * 32, :] = eout[
                i, :, j * 128 : (j + 1) * 128
            ].astype(BF)
    scr[...] = jnp.zeros_like(scr)
    for k in range(3):
        for i in range(2):
            scr[i * 3 + k : i * 3 + k + 1, 0:32] = ein[k, i : i + 1, :]
    scr[6:9, 0:96] = gains[...]
    scr[9:11, 0:96] = special[...]
    hidden = mask[...].astype(F32)
    codes = targets[...]
    high = (codes >> 7).astype(F32)
    low = (codes & 127).astype(F32)
    for part, rows in enumerate((hidden, high, low)):
        for c in range(8):
            at = 16 + part * 4 + c // 2
            scr[at : at + 1, (c % 2) * 64 : (c % 2) * 64 + 64] = rows[c : c + 1, :]
    e_out[192:224, :] = scr[...].astype(BF)
    for copy in copies[6:]:
        copy.wait()
    l_out[:, 0:1152] = qkv[0].astype(BF)
    l_out[:, 1152:1536] = proj[0].astype(BF)
    l_out[:, 1536:3072] = fc1[0].astype(BF)
    for q in range(4):
        l_out[:, 3072 + q * 384 : 3456 + q * 384] = fc2[0, q * 96 : (q + 1) * 96, :].astype(BF)
    half = lax.axis_index("dp") & 1
    l_send[...] = l_out[:, pl.ds(pl.multiple_of(half * L_HALF, L_HALF), L_HALF)]


def pack(*arrays):
    return pl.pallas_call(
        pack_kernel,
        out_shape=(shape((E_ROWS, 128), BF), shape((96, L_WIDE), BF), shape((96, L_HALF), BF)),
        in_specs=[HB] * 10,
        out_specs=(VM, VM, VM),
        scratch_shapes=[pltpu.VMEM(array.shape, array.dtype) for array in arrays]
        + [pltpu.VMEM((32, 128), F32), pltpu.SemaphoreType.DMA((10,))],
        compiler_params=params(60),
        name="pack_weights",
    )(*arrays)


def pack_head_kernel(where, head, own, core, far, held, sems):
    copies = []
    for pos in range(4):
        start = pl.multiple_of((pos ^ where[0]) * VQ, VQ)
        for third in range(3):
            rows = slice(third * 32, third * 32 + 32)
            copies.append(
                pltpu.make_async_copy(
                    head.at[rows, pl.ds(start, VQ)], held.at[pos, rows], sems.at[pos, third]
                )
            )
    for copy in copies:
        copy.start()
    for pos in range(4):
        for copy in copies[pos * 3 : pos * 3 + 3]:
            copy.wait()
        piece = held[pos].astype(BF)
        if pos == 0:
            own[...] = piece
        elif pos == 1:
            core[...] = piece
        else:
            far[pos - 2] = piece


def pack_head(where, head):
    return pl.pallas_call(
        pack_head_kernel,
        out_shape=(shape((96, VQ), BF), shape((96, VQ), BF), shape((2, 96, VQ), BF)),
        in_specs=[SM, HB],
        out_specs=(VM, VM, VM),
        scratch_shapes=[pltpu.VMEM((4, 96, VQ), F32), pltpu.SemaphoreType.DMA((4, 3))],
        compiler_params=params(56),
        name="pack_head",
    )(where, head)


def choose_kernel(where, e_ref, code_ref, pick_ref, small_ref):
    upper = (iota((TOP, TOP), 0) <= iota((TOP, TOP), 1)).astype(F32).astype(BF)
    flags, codes = [], []
    for pos in range(4):
        rows = e_ref[pos, 208:224, :].astype(F32)
        flags.append(jnp.concatenate([rows[u : u + 1] for u in range(4)], 1))
        high = jnp.concatenate([rows[4 + u : 5 + u] for u in range(4)], 1)
        low = jnp.concatenate([rows[8 + u : 9 + u] for u in range(4)], 1)
        codes.append(high * 128.0 + low)
    stack = jnp.concatenate(flags + [jnp.zeros((4, TOP), F32)], 0).astype(BF)
    ranks = dot(stack, upper)
    for pos in range(4):
        rank = ranks[pos : pos + 1]
        chosen = (rank == (iota((CAP, TOP), 0) + 1).astype(F32)) & (flags[pos] > 0.0)
        picked = jnp.where(chosen, 1.0, 0.0)
        code = jnp.sum(picked * codes[pos], 1, keepdims=True)
        real = jnp.sum(picked, 1, keepdims=True) > 0.0
        column = jnp.where(real, code, -1.0).astype(I32)
        code_ref[pos] = jnp.broadcast_to(column, (CAP, 128))
        if pos == 0:
            pick_ref[...] = picked.astype(BF)
    for r in range(4):
        small_ref[:, r * 96 : (r + 1) * 96] = e_ref[r ^ where[0], 192:208, :].astype(F32)[:, 0:96]


def choose(where, e_all):
    return pl.pallas_call(
        choose_kernel,
        out_shape=(shape((4, CAP, 128), I32), shape((CAP, TOP), BF), shape((16, D))),
        in_specs=[SM, VM],
        out_specs=(VM, VM, VM),
        compiler_params=params(8),
        cost_estimate=cost(1e4, 1e3),
        name="choose_rows",
    )(where, e_all)


def point_forward_kernel(
    base, where, points, centers, neighbours, mask, e_ref, *refs,
):
    (
        x_ref, kept_ref, rel_ref, cen_ref, up_ref, slope_up_ref, hid_ref,
        turned, cloud_pts, cloud_cen, cloud_flag, w_in, w_out, w_place, mark,
    ) = refs[-15:]
    slope_ref = kept_ref.at[:, 0:D]
    inner_ref = kept_ref.at[:, D : D + PE]
    slope_in_ref = kept_ref.at[:, D + PE : D + 2 * PE]
    c = pl.program_id(0) + base

    @pl.when(c == base)
    def _():
        lane = iota((8, 128), 1)
        patch = lane & 63
        for q in range(16):
            spot = (patch & 3) * 32 + 2 * q + (lane >> 6)
            found = jnp.zeros((8, 128), I32)
            for v in range(16):
                part = jnp.take_along_axis(
                    neighbours[:, v * 128 : (v + 1) * 128], spot, axis=1, mode="promise_in_bounds"
                )
                found = jnp.where((patch >> 2) == v, part, found)
            for cloud in range(8):
                turned[cloud, 0:1, q * 128 : (q + 1) * 128] = found[cloud : cloud + 1]
        merged = jnp.zeros((16, 128), F32)
        for r in range(4):
            rank = r ^ where[0]
            rows = e_ref[rank, 192:208, :].astype(F32)
            merged = merged + jnp.where(
                iota((16, 128), 1) >> 5 == r, pltpu.roll(rows, r * 32, 1), 0.0
            )
            mark[:, r * 96 : (r + 1) * 96] = rows[:, 0:96]
            for j in range(3):
                lanes = slice(j * 128, j * 128 + 128)
                w_out[r * 32 : (r + 1) * 32, lanes] = e_ref[
                    rank, j * 32 : (j + 1) * 32, :
                ].astype(F32)
                w_place[r * 32 : (r + 1) * 32, lanes] = e_ref[
                    rank, (3 + j) * 32 : (4 + j) * 32, :
                ]
        for i in range(2):
            rows = jnp.concatenate([merged[i * 3 : i * 3 + 3], jnp.zeros((125, 128), F32)], 0)
            w_in[i] = jnp.transpose(rows)
        cloud_pts[...] = jnp.zeros_like(cloud_pts)
        flags = mask[...].astype(F32)
        for cloud in range(8):
            row = slice(cloud, cloud + 1)
            for k in range(3):
                cloud_pts[cloud, k : k + 1, :] = points[k, row, :]
            cloud_cen[cloud, 0:1, 0:64] = centers[row, :]
            cloud_cen[cloud, 0:1, 64:128] = centers[row, :]
            cloud_flag[cloud, 0:1, 0:64] = flags[row, :]

    def look_up(index):
        index = jnp.broadcast_to(index, (8, 128))
        low = index & 127
        high = index >> 7
        found = jnp.zeros((8, 128), F32)
        for k in range(8):
            part = jnp.take_along_axis(
                cloud_pts[c, :, k * 128 : (k + 1) * 128], low, axis=1, mode="promise_in_bounds"
            )
            found = jnp.where(high == k, part, found)
        return found

    centre = look_up(cloud_cen[c, 0:1, :])
    in_point = w_in[0, :, 0:8].astype(BF)
    in_centre = w_in[1, :, 0:8].astype(BF)
    out_point = jnp.transpose(w_out[...]).astype(BF)
    total = jnp.zeros((D, 128), F32)
    for step in range(PATCHES * NB // CH):
        tiles = []
        for q in range(step * CH // 128, (step + 1) * CH // 128):
            near = look_up(turned[c, 0:1, q * 128 : (q + 1) * 128])
            tiles.append(near - centre)
        relative = jnp.concatenate(tiles, 1).astype(BF)
        at = slice(step * CH, (step + 1) * CH)
        rel_ref[0, :, at] = relative
        value, slope = gelu_pair(dot(in_point, relative))
        inner = value.astype(BF)
        inner_ref[0, :, at] = inner
        slope_in_ref[0, :, at] = slope.astype(BF)
        value, slope = gelu_pair(dot(out_point, inner).astype(BF))
        slope_ref[0, :, at] = slope
        for q in range(CH // 128):
            total = total + value[:, q * 128 : (q + 1) * 128].astype(F32)
    centre_b = centre.astype(BF)
    cen_ref[0] = centre_b
    value, slope = gelu_pair(dot(in_centre, centre_b))
    up = value.astype(BF)
    up_ref[0] = up
    slope_up_ref[0] = slope
    place = dot(up, w_place[...], ((0,), (0,)))[0:PATCHES]
    both = jnp.transpose(total)
    diagonal = iota((PATCHES, PATCHES), 0) == iota((PATCHES, PATCHES), 1)
    flags = jnp.broadcast_to(cloud_flag[c, 0:1, 0:64], (PATCHES, PATCHES))
    hidden = jnp.sum(jnp.where(diagonal, flags, 0.0), 1, keepdims=True)
    hid_ref[...] = jnp.broadcast_to(hidden, (PATCHES, 128))
    patch = (both[0:PATCHES] + both[PATCHES:128]) * (1.0 / NB)
    x_ref[...] = jnp.where(hidden > 0.0, mark[10:11, :], patch) + place


def point_forward(where, points, centers, neighbours, mask, e_all, part, parts, kept=None):
    clouds = mask.shape[0] // parts
    tokens = PATCHES * NB

    def whole(array):
        return pl.BlockSpec(array.shape, lambda c: (0,) * array.ndim)

    def per(*dims):
        return pl.BlockSpec((1,) + dims, lambda c: (c, 0, 0))

    inputs = (points, centers, neighbours, mask, e_all)
    return pl.pallas_call(
        functools.partial(point_forward_kernel, part * clouds),
        grid=(clouds,),
        input_output_aliases={6: 1} if part else {},
        out_shape=(
            shape((clouds * PATCHES, D)),
            shape((clouds * parts, D + 2 * PE, tokens), BF),
            shape((clouds, 8, tokens), BF),
            shape((clouds, 8, 128), BF),
            shape((clouds, PE, 128), BF),
            shape((clouds, PE, 128)),
            shape((clouds * PATCHES, 128)),
        ),
        in_specs=[SM] + [whole(array) for array in inputs] + [HB] * (part > 0),
        out_specs=(
            pl.BlockSpec((PATCHES, D), lambda c: (c, 0)),
            pl.BlockSpec((1, D + 2 * PE, tokens), lambda c: (c + part * clouds, 0, 0)),
            per(8, tokens),
            per(8, 128),
            per(PE, 128),
            per(PE, 128),
            pl.BlockSpec((PATCHES, 128), lambda c: (c, 0)),
        ),
        scratch_shapes=[
            pltpu.VMEM((8, 8, tokens), I32),
            pltpu.VMEM((8, 8, 1024), F32),
            pltpu.VMEM((8, 8, 128), I32),
            pltpu.VMEM((8, 8, 128), F32),
            pltpu.VMEM((2, 128, PE), F32),
            pltpu.VMEM((PE, D), F32),
            pltpu.VMEM((PE, D), BF),
            pltpu.VMEM((16, D), F32),
        ],
        compiler_params=params(44),
        cost_estimate=cost(30e9, 20e6, 8e6),
        name="point_forward",
    )(where, *inputs, *([kept] if part else []))


def layer_weights(where, shards, w_main, w_two, whole):
    own, near, far_a, far_b, last_a, last_b = shards
    half = where[1] & 1
    for i, (first, second) in enumerate(((far_a, far_b), (last_a, last_b))):
        whole[i, :, pl.ds(pl.multiple_of(half * L_HALF, L_HALF), L_HALF)] = first[...]
        whole[i, :, pl.ds(pl.multiple_of((1 - half) * L_HALF, L_HALF), L_HALF)] = second[...]
    for pos, shard in enumerate((own, near, whole.at[0], whole.at[1])):
        rank = pos ^ where[0]
        w_main[pl.ds(pl.multiple_of(rank * 96, 96), 96), :] = shard[:, 0:3072]
        for q in range(4):
            rows = pl.ds(pl.multiple_of(rank * 384 + q * 96, 96), 96)
            w_two[rows, :] = shard[:, 3072 + q * 384 : 3456 + q * 384]


def norm(x):
    centred = x - jnp.mean(x, -1, keepdims=True)
    scale = lax.rsqrt(jnp.mean(centred * centred, -1, keepdims=True) + 1e-06)
    return centred * scale, scale


def norm_back(grad, x, gain):
    hat, scale = norm(x)
    d_gain = jnp.sum(grad * hat, 0, keepdims=True)
    inner = grad * gain
    d_x = scale * (
        inner - jnp.mean(inner, -1, keepdims=True) - hat * jnp.mean(inner * hat, -1, keepdims=True)
    )
    return d_x, d_gain


def cloud_rows(ref, start, lanes):
    return jnp.concatenate([ref[pl.ds(start, 64), lanes], ref[TOP:ROWS, lanes]], 0)


def lane_masks():
    first = (iota((1, 128), 1) < HEAD_DIM).astype(F32)
    return first.astype(BF), (1.0 - first).astype(BF)


def layer_forward_kernel(
    where, xa, xb, small, pick, s0, s1, s2, s3, s4, s5,
    m_ref, xo_ref, y_ref, qkv_ref, a_ref, o_ref, z_ref, act_ref, slope_ref, f_ref, w_main, w_two,
    x_all, o_cls, whole,
):
    layer_weights(where, (s0, s1, s2, s3, s4, s5), w_main, w_two, whole)
    x_all[0 : TOP // 2, :] = xa[...]
    x_all[TOP // 2 : TOP, :] = xb[...]
    opening = jnp.broadcast_to(small[9:10, :], (16, D))
    x_all[TOP:ROWS, :] = jnp.where(iota((16, D), 0) < 8, opening, 0.0)
    hat, _ = norm(x_all[...])
    y_ref[...] = (hat * small[6:7, :]).astype(BF)
    qkv_ref[...] = dot(y_ref[...], w_main[:, 0:1152]).astype(BF)
    o_cls[...] = jnp.zeros_like(o_cls)
    mask0, mask1 = lane_masks()

    def one_cloud(c, carry):
        start = pl.multiple_of(c * 64, 64)
        column = iota((160, 80), 1)
        allowed = (column < 64) | (column == c + 64)
        for p in range(3):
            q = cloud_rows(qkv_ref, start, slice(p * 128, p * 128 + 128))
            k = cloud_rows(qkv_ref, start, slice(384 + p * 128, 512 + p * 128))
            v = cloud_rows(qkv_ref, start, slice(768 + p * 128, 896 + p * 128))
            both = jnp.concatenate([q * mask0, q * mask1], 0)
            scores = dot(both, k, ((1,), (1,))) * HEAD_DIM**-0.5
            scores = jnp.where(allowed, scores, -1e30)
            top = jnp.max(scores, -1, keepdims=True)
            e = jnp.exp(scores - top)
            a = (e / jnp.sum(e, -1, keepdims=True)).astype(BF)
            a_ref[c * 3 + p] = a
            o = dot(a, v)
            pair = jnp.where(iota((80, 128), 1) < HEAD_DIM, o[0:80], o[80:160])
            lanes = slice(p * 128, p * 128 + 128)
            o_ref[pl.ds(start, 64), lanes] = pair[0:64].astype(BF)
            o_cls[:, lanes] += jnp.where(iota((16, 128), 0) == c, pair[64:80], 0.0)
        return carry

    lax.fori_loop(0, 8, one_cloud, 0, unroll=4)
    o_ref[TOP:ROWS, :] = o_cls[...].astype(BF)
    m_ref[...] = x_all[...] + dot(o_ref[...], w_main[:, 1152:1536])
    hat, _ = norm(m_ref[...])
    z_ref[...] = (hat * small[7:8, :]).astype(BF)
    for part in range(3):
        lanes = slice(part * 512, part * 512 + 512)
        hidden = dot(z_ref[...], w_main[:, 1536 + part * 512 : 2048 + part * 512])
        value, slope = gelu_pair(hidden)
        act_ref[:, lanes] = value.astype(BF)
        slope_ref[:, lanes] = slope.astype(BF)
    xo = m_ref[0:TOP, :] + dot(act_ref[0:TOP, :], w_two[...])
    xo_ref[...] = xo
    hat, _ = norm(xo)
    f_ref[...] = dot(pick[...], (hat * small[8:9, :]).astype(BF)).astype(BF)


def layer_forward(where, xp, small, pick, shards):
    return pl.pallas_call(
        layer_forward_kernel,
        out_shape=(
            shape((ROWS, D)),
            shape((TOP, D)),
            shape((ROWS, D), BF),
            shape((ROWS, 1152), BF),
            shape((24, 160, 80), BF),
            shape((ROWS, D), BF),
            shape((ROWS, D), BF),
            shape((ROWS, FF), BF),
            shape((ROWS, FF), BF),
            shape((CAP, D), BF),
            shape((D, 3072), BF),
            shape((FF, D), BF),
        ),
        in_specs=[SM] + [VM] * 10,
        out_specs=(VM,) * 12,
        scratch_shapes=[
            pltpu.VMEM((ROWS, D), F32),
            pltpu.VMEM((16, D), F32),
            pltpu.VMEM((2, 96, L_WIDE), BF),
        ],
        compiler_params=params(24),
        cost_estimate=cost(1e4, 1e3),
        name="layer_forward",
    )(where, *xp, small, pick, *shards)


def head_scores_kernel(where, f0, f1, *refs):
    if len(refs) == 9:
        pieces, (codes, e_ref, stat_ref, table, scores) = refs[:4], refs[4:]
        for pos, piece in enumerate(pieces):
            rows = pl.ds(pl.multiple_of((pos ^ where[0]) * 96, 96), 96)
            table[rows, :] = piece[...] if len(piece.shape) == 2 else piece[0]
        begin = 0
    else:
        table, codes, e_ref, stat_ref, scores = refs
        begin = 2
    base = where[0] * VQ
    for half, rows in enumerate((f0, f1)):
        best = jnp.full((CAP, 128), -jnp.inf, F32)
        for t in range(4):
            part = dot(rows[...], table[:, t * 512 : t * 512 + 512])
            scores[:, t * 512 : t * 512 + 512] = part
            for u in range(4):
                best = jnp.maximum(best, part[:, u * 128 : u * 128 + 128])
        top = jnp.max(best, -1, keepdims=True)
        code = codes[begin + half] - base
        total = jnp.zeros((CAP, 128), F32)
        aimed = jnp.zeros((CAP, 128), F32)
        for u in range(16):
            lanes = slice(u * 128, u * 128 + 128)
            part = scores[:, lanes]
            e = jnp.exp(part - top)
            e_ref[half, :, lanes] = e.astype(BF)
            total = total + e
            aimed = aimed + jnp.where(iota((CAP, 128), 1) + u * 128 == code, part, 0.0)
        lane = iota((CAP, 128), 1)
        both = jnp.where(
            lane == 0,
            top,
            jnp.where(
                lane == 1,
                jnp.sum(total, -1, keepdims=True),
                jnp.where(lane == 2, jnp.sum(aimed, -1, keepdims=True), 0.0),
            ),
        )
        both = jnp.concatenate([both, jnp.zeros((CAPL - CAP, 128), F32)], 0)
        stat_ref[half] = jnp.transpose(both)[0:8, :]


def head_scores(where, rows, pieces, codes):
    outs = [shape((2, CAP, VQ), BF), shape((2, 8, CAPL))]
    if len(pieces) == 4:
        outs.append(shape((D, VQ), BF))
    return pl.pallas_call(
        head_scores_kernel,
        out_shape=tuple(outs),
        in_specs=[SM] + [VM] * (3 + len(pieces)),
        out_specs=(VM,) * len(outs),
        scratch_shapes=[pltpu.VMEM((CAP, VQ), F32)],
        compiler_params=params(20),
        cost_estimate=cost(4e9, 4e6, 3e6),
        name="head_scores",
    )(where, *rows, *pieces, codes)


def head_back_kernel(begin, where, e_ref, t0, t1, t2, t3, codes, table, d_ref, keep, send, *losses):
    stats = (t0, t1, t2, t3)
    columns, aims = [], []
    for half in range(2):
        tops = [stats[q][half ^ (q & 1), 0:1, :] for q in range(4)]
        sums = [stats[q][half ^ (q & 1), 1:2, :] for q in range(4)]
        top = jnp.maximum(jnp.maximum(tops[0], tops[1]), jnp.maximum(tops[2], tops[3]))
        total = jnp.zeros((1, CAPL), F32)
        for q in range(4):
            total = total + sums[q] * jnp.exp(tops[q] - top)
        columns.append(jnp.exp(tops[0] - top) / total)
        aims.append(jnp.exp(t0[half, 2:3, :] - top) / total - 1.0)
        if half == 0:
            aimed = (t0[0, 2:3, :] + t1[1, 2:3, :]) + (t2[0, 2:3, :] + t3[1, 2:3, :])
            loss = top + jnp.log(total) - aimed
    block = jnp.concatenate(columns + aims + [loss, jnp.zeros((123, CAPL), F32)], 0)
    turned = jnp.transpose(block)[0:CAP, :]
    if begin == 0:
        loss = jnp.where(codes[0][:, 0:1] >= 0, turned[:, 4:5], 0.0)
        losses[0][...] = jnp.broadcast_to(jnp.sum(loss, 0, keepdims=True), (8, 128))
    base = where[0] * VQ
    for half in range(2):
        code = codes[begin + half]
        scale = jnp.where(code[:, 0:1] >= 0, turned[:, half : half + 1], 0.0)
        aim = turned[:, 2 + half : 3 + half]
        code = code - base
        for u in range(16):
            lanes = slice(u * 128, u * 128 + 128)
            hit = iota((CAP, 128), 1) + u * 128 == code
            grad = jnp.where(hit, aim, e_ref[half, :, lanes].astype(F32) * scale)
            d_ref[half, :, lanes] = grad.astype(BF)
        back = dot(d_ref[half], table[...], ((1,), (1,)))
        if half == 0:
            keep[...] = back
        else:
            send[...] = back.astype(BF)


def head_back(where, begin, e, stats, codes, table):
    outs = [shape((2, CAP, VQ), BF), shape((CAP, D)), shape((CAP, D), BF)]
    if begin == 0:
        outs.append(shape((8, 128)))
    return pl.pallas_call(
        functools.partial(head_back_kernel, begin),
        out_shape=tuple(outs),
        in_specs=[SM] + [VM] * 7,
        out_specs=(VM,) * len(outs),
        compiler_params=params(20),
        cost_estimate=cost(4e9, 6e6),
        name="head_back",
    )(where, e, *stats, codes, table)


def place_y(rel):
    return rel & 1, ((rel >> 1) & 1) * 2 + ((rel >> 2) & 1)


def place_z(rel):
    return (rel >> 1) & 1, (rel & 1) * 2 + ((rel >> 2) & 1)


def place_b(rel):
    return (rel >> 1) & 1, ((rel >> 2) & 1) * 2 + (rel & 1)


def head_grad_kernel(where, f0, f1, f2, f3, d0, d1, a_keep, a_send, b_keep, b_send, joined, held):
    for pos, rows in enumerate((f0, f1, f2, f3)):
        joined[:, pos * CAP : (pos + 1) * CAP] = jnp.transpose(rows[...].astype(F32)).astype(BF)
    for rel in range(SPLIT):
        lanes = pl.ds(pl.multiple_of((rel ^ where[1]) * 256, 256), 256)
        cols = jnp.concatenate([d0[0, :, lanes], d0[1, :, lanes], d1[0, :, lanes], d1[1, :, lanes]], 0)
        held[rel % 2] = dot(joined[...], cols).astype(BF)
        first_a, index_a = place_y(rel)
        first_b, index_b = place_b(rel)
        for pos in range(4):
            rows = held[rel % 2, pl.ds(pl.multiple_of((pos ^ where[0]) * 96, 96), 96), :]
            if pos < 2:
                ref, index = (a_send if first_a else a_keep), index_a
            else:
                ref, index = (b_send if first_b else b_keep), index_b
            for j in range(2):
                ref[index, pos & 1, j * 96 : j * 96 + 96, :] = rows[:, j * 128 : j * 128 + 128]


def head_grad(where, rows, *d):
    return pl.pallas_call(
        head_grad_kernel,
        out_shape=(shape((4, 2, H_PIECE, 128), BF),) * 4,
        in_specs=[SM] + [VM] * 6,
        out_specs=(VM,) * 4,
        scratch_shapes=[pltpu.VMEM((D, 4 * CAP), BF), pltpu.VMEM((2, D, 256), BF)],
        compiler_params=params(16),
        cost_estimate=cost(4e9, 8e6),
        name="head_grad",
    )(where, *rows, *d)


def hold_grad(held, block, grad):
    for r in range(4):
        held[r, block * 96 : block * 96 + 96, :] = grad[r * 96 : r * 96 + 96, :].astype(BF)


def spread_grad(where, held, keep, send, piece_rows):
    for pos in range(4):
        ref, far = (send if pos & 1 else keep), pos >> 1
        for rel in range(SPLIT):
            first, index = place_y(rel)
            start = pl.multiple_of((rel ^ where[1]) * piece_rows, 16)
            ref[far, first, index] = held[pos ^ where[0], pl.ds(start, piece_rows), :]


def ffn_backward_kernel(
    where, keep, rc, rx, pick, xo, m_ref, small, z_ref, act_ref, slope_ref, w_main, w_two,
    keep_ref, send_ref, dm_ref, sg_ref,
    d_hid, held,
):
    compact = keep[...] + rc[...].astype(F32) + rx[...].astype(F32)
    high = compact.astype(BF)
    low = (compact - high.astype(F32)).astype(BF)
    d_rows = dot(pick[...], high, ((0,), (0,))) + dot(pick[...], low, ((0,), (0,)))
    d_out, d_gain = norm_back(d_rows, xo[...], small[8:9, :])
    sg_ref[...] = jnp.zeros_like(sg_ref)
    sg_ref[1:2, :] = d_gain
    grad_b = d_out.astype(BF)
    for part in range(3):
        lanes = slice(part * 512, part * 512 + 512)
        back = dot(grad_b, w_two[lanes, :], ((1,), (1,)))
        d_hid[:, lanes] = (back * slope_ref[0:TOP, lanes].astype(F32)).astype(BF)
    d_fc2 = dot(jnp.transpose(d_out).astype(BF), act_ref[0:TOP, :])
    for j in range(3):
        for q in range(4):
            parts = [
                d_fc2[q * 96 : q * 96 + 96, r * 384 + j * 128 : r * 384 + j * 128 + 128]
                for r in range(4)
            ]
            hold_grad(held, 12 + j * 4 + q, jnp.concatenate(parts, 0))
    turned = jnp.transpose(z_ref[0:TOP, :].astype(F32)).astype(BF)
    for part in range(3):
        grad = dot(turned, d_hid[:, part * 512 : part * 512 + 512])
        for j in range(4):
            hold_grad(held, part * 4 + j, grad[:, j * 128 : j * 128 + 128])
    spread_grad(where, held, keep_ref, send_ref, F_PIECE)
    d_z = dot(d_hid[...], w_main[:, 1536:3072], ((1,), (1,)))
    d_m, d_gain = norm_back(d_z, m_ref[0:TOP, :], small[7:8, :])
    sg_ref[0:1, :] = d_gain
    dm_ref[...] = d_m + d_out


def ffn_backward(where, *arrays):
    return pl.pallas_call(
        ffn_backward_kernel,
        out_shape=(
            shape((2, 2, 4, F_PIECE, 128), BF),
            shape((2, 2, 4, F_PIECE, 128), BF),
            shape((TOP, D)),
            shape((8, D)),
        ),
        in_specs=[SM] + [VM] * 12,
        out_specs=(VM,) * 4,
        scratch_shapes=[
            pltpu.VMEM((TOP, FF), BF),
            pltpu.VMEM((4, F_ROWS, 128), BF),
        ],
        compiler_params=params(24),
        cost_estimate=cost(10e9, 10e6),
        name="ffn_backward",
    )(where, *arrays)


def attention_backward_kernel(
    where, dm_ref, sgf, xa, xb, small, y_ref, qkv_ref, a_ref, o_ref, hid_a, hid_b, w_main,
    keep_ref, send_ref, dx_ref, sg_ref,
    x_all, d_o, d_qkv, d_cls, held,
):
    x_all[0 : TOP // 2, :] = xa[...]
    x_all[TOP // 2 : TOP, :] = xb[...]
    opening = jnp.broadcast_to(small[9:10, :], (16, D))
    x_all[TOP:ROWS, :] = jnp.where(iota((16, D), 0) < 8, opening, 0.0)
    m_b = dm_ref[...].astype(BF)
    d_o[...] = dot(m_b, w_main[:, 1152:1536], ((1,), (1,))).astype(BF)
    d_cls[...] = jnp.zeros_like(d_cls)
    mask0, mask1 = lane_masks()

    def one_cloud(c, carry):
        start = pl.multiple_of(c * 64, 64)
        for p in range(3):
            lanes = slice(p * 128, p * 128 + 128)
            q = qkv_ref[pl.ds(start, 64), lanes]
            k = cloud_rows(qkv_ref, start, slice(384 + p * 128, 512 + p * 128))
            v = cloud_rows(qkv_ref, start, slice(768 + p * 128, 896 + p * 128))
            d = d_o[pl.ds(start, 64), lanes]
            q2 = jnp.concatenate([q * mask0, q * mask1], 0)
            d2 = jnp.concatenate([d * mask0, d * mask1], 0)
            a = jnp.concatenate([a_ref[c * 3 + p, 0:64, :], a_ref[c * 3 + p, 80:144, :]], 0)
            d_a = dot(d2, v, ((1,), (1,)))
            full = a.astype(F32)
            d_s = full * (d_a - jnp.sum(d_a * full, -1, keepdims=True)) * HEAD_DIM**-0.5
            d_s = d_s.astype(BF)
            d_q = dot(d_s, k)
            d_q = jnp.where(iota((64, 128), 1) < HEAD_DIM, d_q[0:64], d_q[64:128])
            d_k = dot(d_s, q2, ((0,), (0,)))
            d_v = dot(a, d2, ((0,), (0,)))
            d_qkv[pl.ds(start, 64), p * 128 : p * 128 + 128] = d_q.astype(BF)
            d_qkv[pl.ds(start, 64), 384 + p * 128 : 512 + p * 128] = d_k[0:64].astype(BF)
            d_qkv[pl.ds(start, 64), 768 + p * 128 : 896 + p * 128] = d_v[0:64].astype(BF)
            d_cls[:, 384 + p * 128 : 512 + p * 128] += d_k[64:80]
            d_cls[:, 768 + p * 128 : 896 + p * 128] += d_v[64:80]
        return carry

    lax.fori_loop(0, 8, one_cloud, 0, unroll=4)
    d_qkv[TOP:ROWS, :] = d_cls[...].astype(BF)
    turned = jnp.transpose(o_ref[0:TOP, :].astype(F32)).astype(BF)
    grad = dot(turned, m_b)
    for j in range(3):
        hold_grad(held, 9 + j, grad[:, j * 128 : j * 128 + 128])
    turned = jnp.transpose(y_ref[...].astype(F32)).astype(BF)
    for part in range(3):
        grad = dot(turned, d_qkv[:, part * 384 : part * 384 + 384])
        for j in range(3):
            hold_grad(held, part * 3 + j, grad[:, j * 128 : j * 128 + 128])
    spread_grad(where, held, keep_ref, send_ref, T_PIECE)
    d_y = dot(d_qkv[...], w_main[:, 0:1152], ((1,), (1,)))
    d_x, d_gain = norm_back(d_y, x_all[...], small[6:7, :])
    d_x = d_x + jnp.concatenate([dm_ref[...], jnp.zeros((16, D), F32)], 0)
    dx_ref[...] = d_x
    sg_ref[...] = jnp.zeros_like(sg_ref)
    sg_ref[6:7, :] = d_gain
    sg_ref[7:9, :] = sgf[0:2, :]
    sg_ref[9:10, :] = jnp.sum(d_x[TOP:ROWS], 0, keepdims=True)
    hidden = jnp.concatenate([hid_a[:, 0:1], hid_b[:, 0:1]], 0)
    sg_ref[10:11, :] = jnp.sum(jnp.where(hidden > 0.0, d_x[0:TOP], 0.0), 0, keepdims=True)


def attention_backward(where, *arrays):
    return pl.pallas_call(
        attention_backward_kernel,
        out_shape=(
            shape((2, 2, 4, T_PIECE, 128), BF),
            shape((2, 2, 4, T_PIECE, 128), BF),
            shape((ROWS, D)),
            shape((16, D)),
        ),
        in_specs=[SM] + [VM] * 12,
        out_specs=(VM,) * 4,
        scratch_shapes=[
            pltpu.VMEM((ROWS, D), F32),
            pltpu.VMEM((TOP, D), BF),
            pltpu.VMEM((ROWS, 1152), BF),
            pltpu.VMEM((16, 1152), F32),
            pltpu.VMEM((4, T_ROWS, 128), BF),
        ],
        compiler_params=params(20),
        cost_estimate=cost(10e9, 10e6),
        name="attention_backward",
    )(where, *arrays)


def point_backward_kernel(
    where, dx_ref, hid, kept_ref, rel_ref, cen_ref, up_ref, slope_up_ref, e_ref, *rest,
):
    c = pl.program_id(0)
    slope_ref = kept_ref.at[:, 0:D]
    inner_ref = kept_ref.at[:, D : D + PE]
    slope_in_ref = kept_ref.at[:, D + PE : D + 2 * PE]
    first, last = len(rest) == 5, len(rest) == 11
    w_out, spread, lift = rest[-3:]
    if first:
        d_out, d_in = rest[:2]
    elif last:
        start_out, start_in, sg_ref, loss_ref, mask, g_ref, d_out, d_in = rest[:8]
    else:
        start_out, start_in, d_out, d_in = rest[:4]

    @pl.when(c == 0)
    def _():
        for r in range(4):
            for i in range(2):
                for j in range(3):
                    w_out[i, r * 32 : (r + 1) * 32, j * 128 : (j + 1) * 128] = e_ref[
                        r ^ where[0], (i * 3 + j) * 32 : (i * 3 + j + 1) * 32, :
                    ]
        if first:
            d_out[...] = jnp.zeros_like(d_out)
            d_in[...] = jnp.zeros_like(d_in)
        else:
            d_out[...] = start_out[...]
            d_in[...] = start_in[...]

    across = ((1,), (1,))
    rows = dx_ref[...]
    place = rows.astype(BF)
    d_out[1] += dot(up_ref[0, :, 0:PATCHES], place)
    d_up = (dot(w_out[1], place, across) * slope_up_ref[0, :, 0:PATCHES]).astype(BF)
    d_in[1] += dot(d_up, cen_ref[0, :, 0:PATCHES], across)
    d_patch = jnp.where(hid[:, 0:1] > 0.0, 0.0, rows) * (1.0 / NB)
    turned = jnp.transpose(jnp.concatenate([d_patch, d_patch], 0))
    for step in range(PATCHES * NB // CH):
        at = slice(step * CH, (step + 1) * CH)
        for q in range(step * CH // 128, (step + 1) * CH // 128):
            lanes = slice(q * 128, q * 128 + 128)
            spread[:, lanes] = (turned * slope_ref[0, :, lanes].astype(F32)).astype(BF)
        back = dot(w_out[0], spread[:, at])
        lift[:, at] = (back * slope_in_ref[0, :, at].astype(F32)).astype(BF)
    d_out[0] += dot(inner_ref[0], spread[...], across)
    d_in[0] += dot(lift[...], rel_ref[0], across)
    if not last:
        return

    @pl.when(c == pl.num_programs(0) - 1)
    def _():
        lane = iota((8, 128), 1)
        seen = jnp.sum(jnp.sum(mask[...].astype(F32), 1, keepdims=True), 0, keepdims=True)
        ins = [
            jnp.transpose(jnp.concatenate([d_in[i], jnp.zeros((PE, 120), F32)], 1))[0:8]
            for i in range(2)
        ]
        for r in range(4):
            pos = r ^ where[0]
            for i in range(2):
                for j in range(3):
                    g_ref[pos, (i * 3 + j) * 32 : (i * 3 + j + 1) * 32, :] = d_out[
                        i, r * 32 : (r + 1) * 32, j * 128 : (j + 1) * 128
                    ]
            g_ref[pos, 192:216, :] = jnp.zeros((24, 128), F32)
            turn = (128 - r * 32) % 128
            for i in range(2):
                rolled = ins[i] if turn == 0 else pltpu.roll(ins[i], turn, 1)
                rolled = jnp.where(lane < 32, rolled, 0.0)
                g_ref[pos, 192 + i * 3 : 195 + i * 3, :] = rolled[0:3]
            g_ref[pos, 198:203, 0:96] = sg_ref[6:11, r * 96 : (r + 1) * 96]
            g_ref[pos, 208:209, :] = loss_ref[0:1, :]
            g_ref[pos, 209:210, :] = jnp.broadcast_to(seen, (1, 128))


def point_backward(where, dx, kept, e_all, begin, count, start=(), last=()):
    big, rel, cen, up, slope_up, hid = kept
    local = begin % rel.shape[0]
    tokens = PATCHES * NB

    def whole(array):
        return pl.BlockSpec(array.shape, lambda c: (0,) * len(array.shape))

    def per(*dims):
        return pl.BlockSpec((1,) + dims, lambda c: (c + local, 0, 0))

    sums = (shape((2, PE, D)), shape((2, PE, 8)))
    more = (*start, *last)
    packed = shape((4, E_GRAD, 128))
    return pl.pallas_call(
        point_backward_kernel,
        grid=(count,),
        out_shape=packed if last else sums,
        in_specs=[
            SM,
            pl.BlockSpec((PATCHES, D), lambda c: (c + begin, 0)),
            pl.BlockSpec((PATCHES, 128), lambda c: (c + local, 0)),
            pl.BlockSpec((1, D + 2 * PE, tokens), lambda c: (c + begin, 0, 0)),
            per(8, tokens),
            per(8, 128),
            per(PE, 128),
            per(PE, 128),
            whole(e_all),
            *[whole(array) for array in more],
        ],
        out_specs=whole(packed) if last else tuple(whole(array) for array in sums),
        scratch_shapes=([pltpu.VMEM(array.shape, F32) for array in sums] if last else [])
        + [
            pltpu.VMEM((2, PE, D), BF),
            pltpu.VMEM((D, tokens), BF),
            pltpu.VMEM((PE, tokens), BF),
        ],
        compiler_params=params(44),
        cost_estimate=cost(6e9, 6e6),
        name="point_backward",
    )(where, dx, hid, big, rel, cen, up, slope_up, e_all, *more)


def squares_kernel(*refs):
    total = jnp.zeros((16, 128), F32)
    for ref in refs[:-2]:
        rows = ref.shape[-2]
        for lead in range(ref.shape[0] * (ref.shape[1] if len(ref.shape) == 4 else 1)):
            part = ref[divmod(lead, ref.shape[1])] if len(ref.shape) == 4 else ref[lead]
            part = part.astype(F32)
            total = total + jnp.sum((part * part).reshape(rows // 16, 16, 128), 0)
    part = refs[-2][0:208, :]
    total = total + jnp.sum((part * part).reshape(13, 16, 128), 0)
    total = jnp.sum(jnp.sum(total, 1, keepdims=True), 0, keepdims=True)
    refs[-1][...] = jnp.broadcast_to(total, (8, 128))


def squares(*arrays):
    return pl.pallas_call(
        squares_kernel,
        out_shape=shape((8, 128)),
        in_specs=[VM] * len(arrays),
        out_specs=VM,
        compiler_params=params(8),
        name="squares",
    )(*arrays)


def adam(grad, first, second, weight, factor, vector):
    rate = RATE_VECTOR if vector else RATE_MATRIX
    clipped = grad * factor
    first = BETA_ONE * first + (1 - BETA_ONE) * clipped
    second = BETA_TWO * second + (1 - BETA_TWO) * (clipped * clipped)
    level = second * (1.0 / (1 - BETA_TWO**STEP_NUMBER))
    root = level * lax.rsqrt(level) + EPSILON
    update = (first * (rate / (1 - BETA_ONE**STEP_NUMBER))) * pl.reciprocal(root)
    if vector:
        return first, second, weight - update
    return first, second, weight * (1.0 - rate * DECAY) - update


def clip_factor(s0, s1, e_ref):
    count = e_ref[209:210, :]
    length = jnp.sqrt(s0[0:1, :] + s1[0:1, :]) / count
    return jnp.minimum(1.0, CLIP / length) / count, length


def step_kernel(where, s0, s1, e_ref, f0, f1, t0, t1, a0, a1, b0, b1, *refs):
    ins, outs, scalars = refs[:27], refs[27:54], refs[54]
    done, joined, turned, sems = refs[55:82], refs[82], refs[83], refs[84]
    factor, length = clip_factor(s0, s1, e_ref)
    copies = []

    def send(which, at=None):
        for k in range(3):
            i = which * 3 + k
            source = done[i] if at is None else done[i].at[at]
            target = outs[i] if at is None else outs[i].at[at]
            copy = pltpu.make_async_copy(source, target, sems.at[len(copies)])
            copy.start()
            copies.append(copy)

    def update(which, at, grad, vector=False):
        w, m, v = (ins[which * 3 + k] for k in range(3))
        out = adam(grad, m[at], v[at], w[at], factor[:, 0 : grad.shape[-1]], vector)
        for k in range(3):
            done[which * 3 + k][at] = out[k]

    for piece in range(SPLIT):
        first, index = place_y(piece ^ where[1])
        rows = slice(T_ROWS + piece * F_PIECE, T_ROWS + (piece + 1) * F_PIECE)
        joined[rows, :] = jnp.where(first == 0, f0[index], f1[index])
        first, index = place_z(piece ^ where[1])
        rows = slice(piece * T_PIECE, (piece + 1) * T_PIECE)
        joined[rows, :] = jnp.where(first == 0, t0[index], t1[index])

    starts = {0: (2, 0), 9: (3, 9), 12: (4, 12)}
    which = base = 0
    for block in range(36):
        grad = joined[block * 96 : block * 96 + 96, :].astype(F32)
        if block >= 24:
            j, q = divmod(block - 24, 4)
            turned[q * 96 : q * 96 + 96, j * 128 : j * 128 + 128] = grad
            continue
        if block in starts:
            which, base = starts[block]
        j = block - base
        update(which, (0, slice(None), slice(j * 128, j * 128 + 128)), grad)
        if block in (8, 11, 23):
            send(which)
    grad = jnp.transpose(turned[...])
    for j in range(3):
        lanes = slice(j * 128, j * 128 + 128)
        update(5, (0, slice(None), lanes), grad[:, lanes])
    send(5)
    for i in range(2):
        for k in range(3):
            at = 192 + i * 3 + k
            update(0, (k, slice(i, i + 1)), e_ref[at : at + 1, 0:32])
        for j in range(3):
            block = i * 3 + j
            grad = e_ref[block * 32 : block * 32 + 32, :]
            update(1, (i, slice(None), slice(j * 128, j * 128 + 128)), grad)
    update(6, (slice(0, 3),), e_ref[198:201, 0:96], True)
    update(7, (slice(0, 2),), e_ref[201:203, 0:96], True)
    for which in (0, 1, 6, 7):
        send(which)
    scalars[0:1, :] = e_ref[208:209, :]
    scalars[1:2, :] = e_ref[209:210, :]
    scalars[2:3, :] = length
    for piece in range(32):
        quarter = (piece // SPLIT) ^ where[0]
        first_a, index_a = place_y((piece % SPLIT) ^ where[1])
        first_b, index_b = place_z((piece % SPLIT) ^ where[1])
        for j in range(2):
            lanes = slice(piece * 256 + j * 128, piece * 256 + j * 128 + 128)
            rows = slice(j * 96, j * 96 + 96)
            near = quarter & 1
            grad = jnp.where(
                quarter < 2,
                jnp.where(first_a == 0, a0[index_a, near, rows, :], a1[index_a, near, rows, :]),
                jnp.where(first_b == 0, b0[index_b, near, rows, :], b1[index_b, near, rows, :]),
            )
            update(8, (slice(None), lanes), grad.astype(F32))
        if piece % 4 == 3:
            send(8, (slice(None), slice((piece - 3) * 256, (piece + 1) * 256)))
    for copy in copies:
        copy.wait()


def step_all(where, sums, e, grads, states):
    outs = tuple(shape(array.shape) for array in states)
    return pl.pallas_call(
        step_kernel,
        out_shape=outs + (shape((8, 128)),),
        in_specs=[SM] + [VM] * (11 + len(states)),
        out_specs=(HB,) * len(outs) + (VM,),
        scratch_shapes=[pltpu.VMEM(array.shape, F32) for array in states]
        + [
            pltpu.VMEM((T_ROWS + F_ROWS, 128), BF),
            pltpu.VMEM((D, D), F32),
            pltpu.SemaphoreType.DMA((48,)),
        ],
        compiler_params=params(24),
        cost_estimate=cost(4e7, 3e7),
        name="step_all",
    )(where, *sums, e, *grads, *states)


def add(*parts):
    total = parts[0].astype(F32)
    for part in parts[1:]:
        total = total + part.astype(F32)
    return total.astype(BF)


def after(*arrays):
    return lax.optimization_barrier(arrays)


def body(dp, fsdp, *args):
    (
        points, centers, neighbours, mask, targets,
        embed_in, embed_in_m, embed_in_v, embed_out, embed_out_m, embed_out_v,
        qkv_w, qkv_m, qkv_v, proj_w, proj_m, proj_v, fc1_w, fc1_m, fc1_v, fc2_w, fc2_m, fc2_v,
        gains, gains_m, gains_v, special, special_m, special_v, head, head_m, head_v,
    ) = args
    rank = lax.axis_index("fsdp").astype(I32)
    group = lax.axis_index("dp").astype(I32)
    where = jnp.stack([rank, group % SPLIT])

    def swap(x, axis, bit):
        size = dp if axis == "dp" else fsdp
        return lax.ppermute(x, axis, [(i, i ^ bit) for i in range(size)])

    def higher(total):
        bit = SPLIT
        while bit < dp:
            total = add(total, swap(total, "dp", bit))
            bit *= 2
        return total

    embed_in, embed_in_m, embed_in_v = (
        jnp.transpose(array, (1, 0, 2)) for array in (embed_in, embed_in_m, embed_in_v)
    )
    e_own, l_own, l_send = pack(
        embed_in, embed_out, gains, special, mask, targets, qkv_w, proj_w, fc1_w, fc2_w
    )
    e_far = swap(e_own, "fsdp", 2)
    e_near = swap(e_own, "fsdp", 1)
    h_own, h_core, h_far = pack_head(where, head)
    e_far, l_send, h_own = after(e_far, l_send, h_own)
    l_far = swap(l_send, "fsdp", 2)
    e_all = jnp.stack([e_own, e_near, e_far, swap(e_far, "fsdp", 1)])
    xa, big, *kept_a = point_forward(where, points, centers, neighbours, mask, e_all, 0, 2)
    l_far, xa, e_all, l_own, h_far = after(l_far, xa, e_all, l_own, h_far)
    l_far_b = swap(l_far, "dp", 1)
    l_near = swap(l_own, "fsdp", 1)
    l_last = swap(l_far, "fsdp", 1)
    h_got = swap(h_far, "fsdp", 2)
    xb, big, *kept_b = point_forward(where, points, centers, neighbours, mask, e_all, 1, 2, big)
    l_far_b, xb, e_late = after(l_far_b, xb, e_all)
    codes, pick, small = choose(where, e_late)
    l_last_b = swap(l_far_b, "fsdp", 1)
    h_near = swap(h_core, "fsdp", 1)
    shards = (l_own, l_near, l_far, l_far_b, l_last, l_last_b)
    *kept, f_own, w_main, w_two = layer_forward(where, (xa, xb), small, pick, shards)
    m, xo, y, qkv, a, o, z, act, slope = kept
    f_far = swap(f_own, "fsdp", 2)
    f_near = swap(f_own, "fsdp", 1)
    h_got, f_near = after(h_got, f_near)
    pieces = (h_own, h_near, h_got, swap(h_got[1], "fsdp", 1))
    e01, stat01, table = head_scores(where, (f_own, f_near), pieces, codes)
    f_far, stat01, e01 = after(f_far, stat01, e01)
    f_last = swap(f_far, "fsdp", 1)
    near01, far01, last01 = (swap(stat01, "fsdp", pos) for pos in (1, 2, 3))
    e23, stat23 = head_scores(where, (f_far, f_last), (table,), codes)
    rows = (f_own, f_near, f_far, f_last)
    near23, far23, last23 = (swap(stat23, "fsdp", pos) for pos in (1, 2, 3))
    d23, keep23, send23 = head_back(where, 2, e23, (stat23, near23, far01, last01), codes, table)
    keep23, send23, far23, last23 = after(keep23, send23, far23, last23)
    got23 = swap(send23, "fsdp", 1)
    passed, far23 = after(add(keep23, got23), far23)
    got_far = swap(passed, "fsdp", 2)
    d01, keep, send, loss = head_back(where, 0, e01, (stat01, near01, far23, last23), codes, table)
    got = swap(send, "fsdp", 1)
    a_keep, a_send, b_keep, b_send = head_grad(where, rows, d01, d23)

    a_send, b_send, got_far, got = after(a_send, b_send, got_far, got)
    a_1 = swap(a_send, "dp", 1)
    b_1 = swap(b_send, "dp", 2)
    f_keep, f_send, dm, sgf = ffn_backward(
        where, keep, got, got_far, pick, xo, m, small, z, act, slope, w_main, w_two
    )
    a_1, b_1, f_send, dm = after(a_1, b_1, f_send, dm)
    a_2 = swap(add(a_keep[2:], a_1[2:]), "dp", 2)
    b_2 = swap(add(b_keep[2:], b_1[2:]), "dp", 4)
    f_core = swap(f_send, "fsdp", 1)
    f_core, dm = after(f_core, dm)
    f_x = swap(add(f_keep[1], f_core[1]), "fsdp", 2)
    t_keep, t_send, dx, sg = attention_backward(
        where, dm, sgf, xa, xb, small, y, qkv, a, o, kept_a[-1], kept_b[-1], w_main
    )
    a_2, b_2, f_x, t_send, dx = after(a_2, b_2, f_x, t_send, dx)
    t_core = swap(t_send, "fsdp", 1)
    f_low = add(f_keep[0], f_core[0], f_x)
    f_y = swap(f_low[1], "dp", 1)
    a_low = add(a_keep[:2], a_1[:2])
    b_low = add(b_keep[:2], b_1[:2])
    a_3 = swap(add(a_low[1], a_2[1]), "dp", 4)
    b_3 = swap(add(b_low[1], b_2[1]), "dp", 1)
    t_core, dx = after(t_core, dx)
    t_x = swap(add(t_keep[1], t_core[1]), "fsdp", 2)
    part = point_backward(where, dx, (big, *kept_a), e_all, 0, 2)
    a_3, b_3, t_x, part = after(a_3, b_3, t_x, part)
    ab_sum = higher(
        jnp.concatenate([add(a_low[0], a_2[0], a_3), add(b_low[0], b_2[0], b_3)], 0)
    )
    h_got = [swap(ab_sum[pos], "fsdp", pos) for pos in (1, 2, 3)]
    t_low = add(t_keep[0], t_core[0], t_x)
    t_y = swap(t_low[1], "dp", 1)
    part = point_backward(where, dx, (big, *kept_a), e_all, 2, 2, part)
    *h_got, f_y, t_y, part = after(*h_got, f_y, t_y, part)
    h_mine = jnp.stack([ab_sum[0], *h_got])
    h_two = swap(h_mine, "dp", 4)
    ft_low = jnp.concatenate([add(f_low[0], f_y), add(t_low[0], t_y)], 1)
    ft_z1 = swap(ft_low[2:], "dp", 2)
    part = point_backward(where, dx, (big, *kept_b), e_all, 4, 3, part)
    h_two, ft_z1, part = after(h_two, ft_z1, part)
    h_both = jnp.stack([h_mine, h_two])
    a_both, b_both = h_both[:, 0:2], h_both[:, 2:4]
    a_pair = swap(a_both, "dp", 2)
    b_pair = swap(b_both, "dp", 1)
    ft_z2 = swap(add(ft_low[1], ft_z1[1]), "dp", 4)
    e_grad = point_backward(where, dx, (big, *kept_b), e_all, 7, 1, part, (sg, loss, mask))
    e_grad, ft_z2, a_pair, b_pair = after(e_grad, ft_z2, a_pair, b_pair)
    e_got = [swap(e_grad[pos], "fsdp", pos) for pos in (1, 2, 3)]
    ft_sum = higher(add(ft_low[0], ft_z1[0], ft_z2))
    ft_two = swap(ft_sum, "dp", 4)
    a_four = jnp.concatenate([a_both, a_pair], 0)
    b_four = jnp.concatenate([b_both, b_pair], 0)
    b_end = swap(b_four, "dp", 2)
    a_end = swap(a_four, "dp", 1)
    *e_got, ft_two = after(*e_got, ft_two)
    e_sum = (e_grad[0] + e_got[0]) + (e_got[1] + e_got[2])
    e_y = swap(e_sum, "dp", 1)
    ft_both = jnp.stack([ft_sum, ft_two])
    f_both, t_both = ft_both[:, :F_PIECE], ft_both[:, F_PIECE:]
    f_pair = swap(f_both, "dp", 2)
    t_pair = swap(t_both, "dp", 1)
    e_y, f_pair, t_pair, a_end, b_end = after(e_y, f_pair, t_pair, a_end, b_end)
    e_sum = e_sum + e_y
    e_z2 = swap(e_sum, "dp", 4)
    f_four = jnp.concatenate([f_both, f_pair], 0)
    t_four = jnp.concatenate([t_both, t_pair], 0)
    f_end = swap(f_four, "dp", 1)
    t_end = swap(t_four, "dp", 2)
    e_sum = e_sum + e_z2
    e_sum = e_sum + swap(e_sum, "dp", 2)
    bit = SPLIT
    while bit < dp:
        e_sum = e_sum + swap(e_sum, "dp", bit)
        bit *= 2
    grads = (f_four, f_end, t_four, t_end, a_four, a_end, b_four, b_end)

    sums = squares(*grads, e_sum)
    sums = sums + swap(sums, "fsdp", 1)
    sums = (sums, swap(sums, "fsdp", 2))
    states = (
        embed_in, embed_in_m, embed_in_v, embed_out, embed_out_m, embed_out_v,
        qkv_w, qkv_m, qkv_v, proj_w, proj_m, proj_v, fc1_w, fc1_m, fc1_v, fc2_w, fc2_m, fc2_v,
        gains, gains_m, gains_v, special, special_m, special_v, head, head_m, head_v,
    )
    *news, scalars = step_all(where, sums, e_sum, grads, states)
    news[:3] = [jnp.transpose(array, (1, 0, 2)) for array in news[:3]]
    return (*news, scalars[0, 0], scalars[1, 0], scalars[2, 0])


def solution(mesh):
    in_specs = (
        P(None, ("dp", "fsdp"), None),
        *[P(("dp", "fsdp"), None)] * 4,
        *[P(None, None, "fsdp")] * 3,
        *[P(None, "fsdp", None)] * 15,
        *[P(None, "fsdp")] * 6,
        *[P("fsdp", None)] * 3,
    )
    out_specs = in_specs[5:] + (P(), P(), P())
    step = functools.partial(body, mesh.shape["dp"], mesh.shape["fsdp"])
    return jax.shard_map(
        step, mesh=mesh, in_specs=in_specs, out_specs=out_specs, check_vma=False
    )
```

```python
import functools

import jax
import jax.numpy as jnp
from jax import lax
from jax.experimental import pallas as pl
from jax.experimental.pallas import tpu as pltpu
from jax.sharding import PartitionSpec as P

BF = jnp.bfloat16
F32 = jnp.float32
I32 = jnp.int32
D = 384
HEAD_DIM = 64
FF = 1536
PE = 128
NB = 32
PATCHES = 64
STEP_NUMBER = 10
MOST_MASKED = 36

BETA_ONE = 0.9
BETA_TWO = 0.95
EPSILON = 1e-08
DECAY = 0.05
RATE_MATRIX = 0.1
RATE_VECTOR = 0.5
CLIP = 0.005

TOP = 512
ROWS = 528
CAP = 288
CAPL = 384
VQ = 2048
SPLIT = 8
L_WIDE = 4608
L_HALF = 2304
F_ROWS = 2304
F_PIECE = F_ROWS // SPLIT
T_ROWS = 1152
T_PIECE = T_ROWS // SPLIT
H_PIECE = 192
E_ROWS = 224
E_GRAD = 216
CH = 256

GA = 0.7978845608028654
GB = GA * 0.044715


def dot(left, right, dims=((1,), (0,))):
    return lax.dot_general(left, right, (dims, ((), ())), preferred_element_type=F32)


def gelu_pair(x):
    square = x * x
    half = 0.5 * jnp.tanh(x * (GA + GB * square)) + 0.5
    value = x * half
    slope = half + (value * (1.0 - half)) * (2.0 * GA + (6.0 * GB) * square)
    return value, slope


def iota(shape, axis):
    return lax.broadcasted_iota(I32, shape, axis)


def params(mib=48):
    return pltpu.CompilerParams(vmem_limit_bytes=mib << 20)


VM = pl.BlockSpec(memory_space=pltpu.VMEM)
SM = pl.BlockSpec(memory_space=pltpu.SMEM)
HB = pl.BlockSpec(memory_space=pltpu.HBM)


def shape(dims, dtype=F32):
    return jax.ShapeDtypeStruct(dims, dtype)


def cost(flops, moved, trans=0):
    return pl.CostEstimate(flops=int(flops), bytes_accessed=int(moved), transcendentals=int(trans))


def pack_kernel(*refs):
    sources, (e_out, l_out, l_send) = refs[:10], refs[10:13]
    local, scr, sems = refs[13:23], refs[23], refs[24]
    copies = [
        pltpu.make_async_copy(source, target, sems.at[i])
        for i, (source, target) in enumerate(zip(sources, local))
    ]
    for copy in copies:
        copy.start()
    for copy in copies[:6]:
        copy.wait()
    ein, eout, gains, special, mask, targets, qkv, proj, fc1, fc2 = local
    for i in range(2):
        for j in range(3):
            e_out[(i * 3 + j) * 32 : (i * 3 + j + 1) * 32, :] = eout[
                i, :, j * 128 : (j + 1) * 128
            ].astype(BF)
    scr[...] = jnp.zeros_like(scr)
    for k in range(3):
        for i in range(2):
            scr[i * 3 + k : i * 3 + k + 1, 0:32] = ein[k, i : i + 1, :]
    scr[6:9, 0:96] = gains[...]
    scr[9:11, 0:96] = special[...]
    hidden = mask[...].astype(F32)
    codes = targets[...]
    high = (codes >> 7).astype(F32)
    low = (codes & 127).astype(F32)
    for part, rows in enumerate((hidden, high, low)):
        for c in range(8):
            at = 16 + part * 4 + c // 2
            scr[at : at + 1, (c % 2) * 64 : (c % 2) * 64 + 64] = rows[c : c + 1, :]
    e_out[192:224, :] = scr[...].astype(BF)
    for copy in copies[6:]:
        copy.wait()
    l_out[:, 0:1152] = qkv[0].astype(BF)
    l_out[:, 1152:1536] = proj[0].astype(BF)
    l_out[:, 1536:3072] = fc1[0].astype(BF)
    for q in range(4):
        l_out[:, 3072 + q * 384 : 3456 + q * 384] = fc2[0, q * 96 : (q + 1) * 96, :].astype(BF)
    half = lax.axis_index("dp") & 1
    l_send[...] = l_out[:, pl.ds(pl.multiple_of(half * L_HALF, L_HALF), L_HALF)]


def pack(*arrays):
    return pl.pallas_call(
        pack_kernel,
        out_shape=(shape((E_ROWS, 128), BF), shape((96, L_WIDE), BF), shape((96, L_HALF), BF)),
        in_specs=[HB] * 10,
        out_specs=(VM, VM, VM),
        scratch_shapes=[pltpu.VMEM(array.shape, array.dtype) for array in arrays]
        + [pltpu.VMEM((32, 128), F32), pltpu.SemaphoreType.DMA((10,))],
        compiler_params=params(60),
        name="pack_weights",
    )(*arrays)


def pack_head_kernel(where, head, own, core, far, held, sems):
    copies = []
    for pos in range(4):
        start = pl.multiple_of((pos ^ where[0]) * VQ, VQ)
        for third in range(3):
            rows = slice(third * 32, third * 32 + 32)
            copies.append(
                pltpu.make_async_copy(
                    head.at[rows, pl.ds(start, VQ)], held.at[pos, rows], sems.at[pos, third]
                )
            )
    for copy in copies:
        copy.start()
    for pos in range(4):
        for copy in copies[pos * 3 : pos * 3 + 3]:
            copy.wait()
        piece = held[pos].astype(BF)
        if pos == 0:
            own[...] = piece
        elif pos == 1:
            core[...] = piece
        else:
            far[pos - 2] = piece


def pack_head(where, head):
    return pl.pallas_call(
        pack_head_kernel,
        out_shape=(shape((96, VQ), BF), shape((96, VQ), BF), shape((2, 96, VQ), BF)),
        in_specs=[SM, HB],
        out_specs=(VM, VM, VM),
        scratch_shapes=[pltpu.VMEM((4, 96, VQ), F32), pltpu.SemaphoreType.DMA((4, 3))],
        compiler_params=params(56),
        name="pack_head",
    )(where, head)


def choose_kernel(where, e_ref, code_ref, pick_ref, small_ref):
    upper = (iota((TOP, TOP), 0) <= iota((TOP, TOP), 1)).astype(F32).astype(BF)
    flags, codes = [], []
    for pos in range(4):
        rows = e_ref[pos, 208:224, :].astype(F32)
        flags.append(jnp.concatenate([rows[u : u + 1] for u in range(4)], 1))
        high = jnp.concatenate([rows[4 + u : 5 + u] for u in range(4)], 1)
        low = jnp.concatenate([rows[8 + u : 9 + u] for u in range(4)], 1)
        codes.append(high * 128.0 + low)
    stack = jnp.concatenate(flags + [jnp.zeros((4, TOP), F32)], 0).astype(BF)
    ranks = dot(stack, upper)
    for pos in range(4):
        rank = ranks[pos : pos + 1]
        chosen = (rank == (iota((CAP, TOP), 0) + 1).astype(F32)) & (flags[pos] > 0.0)
        picked = jnp.where(chosen, 1.0, 0.0)
        code = jnp.sum(picked * codes[pos], 1, keepdims=True)
        real = jnp.sum(picked, 1, keepdims=True) > 0.0
        column = jnp.where(real, code, -1.0).astype(I32)
        code_ref[pos] = jnp.broadcast_to(column, (CAP, 128))
        if pos == 0:
            pick_ref[...] = picked.astype(BF)
    for r in range(4):
        small_ref[:, r * 96 : (r + 1) * 96] = e_ref[r ^ where[0], 192:208, :].astype(F32)[:, 0:96]


def choose(where, e_all):
    return pl.pallas_call(
        choose_kernel,
        out_shape=(shape((4, CAP, 128), I32), shape((CAP, TOP), BF), shape((16, D))),
        in_specs=[SM, VM],
        out_specs=(VM, VM, VM),
        compiler_params=params(8),
        cost_estimate=cost(1e4, 1e3),
        name="choose_rows",
    )(where, e_all)


def point_forward_kernel(
    base, where, points, centers, neighbours, mask, e_ref, *refs,
):
    (
        x_ref, kept_ref, rel_ref, cen_ref, up_ref, slope_up_ref, hid_ref,
        turned, cloud_pts, cloud_cen, cloud_flag, w_in, w_out, w_place, mark,
    ) = refs[-15:]
    slope_ref = kept_ref.at[:, 0:D]
    inner_ref = kept_ref.at[:, D : D + PE]
    slope_in_ref = kept_ref.at[:, D + PE : D + 2 * PE]
    c = pl.program_id(0) + base

    @pl.when(c == base)
    def _():
        lane = iota((8, 128), 1)
        patch = lane & 63
        for q in range(16):
            spot = (patch & 3) * 32 + 2 * q + (lane >> 6)
            found = jnp.zeros((8, 128), I32)
            for v in range(16):
                part = jnp.take_along_axis(
                    neighbours[:, v * 128 : (v + 1) * 128], spot, axis=1, mode="promise_in_bounds"
                )
                found = jnp.where((patch >> 2) == v, part, found)
            for cloud in range(8):
                turned[cloud, 0:1, q * 128 : (q + 1) * 128] = found[cloud : cloud + 1]
        merged = jnp.zeros((16, 128), F32)
        for r in range(4):
            rank = r ^ where[0]
            rows = e_ref[rank, 192:208, :].astype(F32)
            merged = merged + jnp.where(
                iota((16, 128), 1) >> 5 == r, pltpu.roll(rows, r * 32, 1), 0.0
            )
            mark[:, r * 96 : (r + 1) * 96] = rows[:, 0:96]
            for j in range(3):
                lanes = slice(j * 128, j * 128 + 128)
                w_out[r * 32 : (r + 1) * 32, lanes] = e_ref[
                    rank, j * 32 : (j + 1) * 32, :
                ].astype(F32)
                w_place[r * 32 : (r + 1) * 32, lanes] = e_ref[
                    rank, (3 + j) * 32 : (4 + j) * 32, :
                ]
        for i in range(2):
            rows = jnp.concatenate([merged[i * 3 : i * 3 + 3], jnp.zeros((125, 128), F32)], 0)
            w_in[i] = jnp.transpose(rows)
        cloud_pts[...] = jnp.zeros_like(cloud_pts)
        flags = mask[...].astype(F32)
        for cloud in range(8):
            row = slice(cloud, cloud + 1)
            for k in range(3):
                cloud_pts[cloud, k : k + 1, :] = points[k, row, :]
            cloud_cen[cloud, 0:1, 0:64] = centers[row, :]
            cloud_cen[cloud, 0:1, 64:128] = centers[row, :]
            cloud_flag[cloud, 0:1, 0:64] = flags[row, :]

    def look_up(index):
        index = jnp.broadcast_to(index, (8, 128))
        low = index & 127
        high = index >> 7
        found = jnp.zeros((8, 128), F32)
        for k in range(8):
            part = jnp.take_along_axis(
                cloud_pts[c, :, k * 128 : (k + 1) * 128], low, axis=1, mode="promise_in_bounds"
            )
            found = jnp.where(high == k, part, found)
        return found

    centre = look_up(cloud_cen[c, 0:1, :])
    in_point = w_in[0, :, 0:8].astype(BF)
    in_centre = w_in[1, :, 0:8].astype(BF)
    out_point = jnp.transpose(w_out[...]).astype(BF)
    total = jnp.zeros((D, 128), F32)
    for step in range(PATCHES * NB // CH):
        tiles = []
        for q in range(step * CH // 128, (step + 1) * CH // 128):
            near = look_up(turned[c, 0:1, q * 128 : (q + 1) * 128])
            tiles.append(near - centre)
        relative = jnp.concatenate(tiles, 1).astype(BF)
        at = slice(step * CH, (step + 1) * CH)
        rel_ref[0, :, at] = relative
        value, slope = gelu_pair(dot(in_point, relative))
        inner = value.astype(BF)
        inner_ref[0, :, at] = inner
        slope_in_ref[0, :, at] = slope.astype(BF)
        value, slope = gelu_pair(dot(out_point, inner).astype(BF))
        slope_ref[0, :, at] = slope
        for q in range(CH // 128):
            total = total + value[:, q * 128 : (q + 1) * 128].astype(F32)
    centre_b = centre.astype(BF)
    cen_ref[0] = centre_b
    value, slope = gelu_pair(dot(in_centre, centre_b))
    up = value.astype(BF)
    up_ref[0] = up
    slope_up_ref[0] = slope
    place = dot(up, w_place[...], ((0,), (0,)))[0:PATCHES]
    both = jnp.transpose(total)
    diagonal = iota((PATCHES, PATCHES), 0) == iota((PATCHES, PATCHES), 1)
    flags = jnp.broadcast_to(cloud_flag[c, 0:1, 0:64], (PATCHES, PATCHES))
    hidden = jnp.sum(jnp.where(diagonal, flags, 0.0), 1, keepdims=True)
    hid_ref[...] = jnp.broadcast_to(hidden, (PATCHES, 128))
    patch = (both[0:PATCHES] + both[PATCHES:128]) * (1.0 / NB)
    x_ref[...] = jnp.where(hidden > 0.0, mark[10:11, :], patch) + place


def point_forward(where, points, centers, neighbours, mask, e_all, part, parts, kept=None):
    clouds = mask.shape[0] // parts
    tokens = PATCHES * NB

    def whole(array):
        return pl.BlockSpec(array.shape, lambda c: (0,) * array.ndim)

    def per(*dims):
        return pl.BlockSpec((1,) + dims, lambda c: (c, 0, 0))

    inputs = (points, centers, neighbours, mask, e_all)
    return pl.pallas_call(
        functools.partial(point_forward_kernel, part * clouds),
        grid=(clouds,),
        input_output_aliases={6: 1} if part else {},
        out_shape=(
            shape((clouds * PATCHES, D)),
            shape((clouds * parts, D + 2 * PE, tokens), BF),
            shape((clouds, 8, tokens), BF),
            shape((clouds, 8, 128), BF),
            shape((clouds, PE, 128), BF),
            shape((clouds, PE, 128)),
            shape((clouds * PATCHES, 128)),
        ),
        in_specs=[SM] + [whole(array) for array in inputs] + [HB] * (part > 0),
        out_specs=(
            pl.BlockSpec((PATCHES, D), lambda c: (c, 0)),
            pl.BlockSpec((1, D + 2 * PE, tokens), lambda c: (c + part * clouds, 0, 0)),
            per(8, tokens),
            per(8, 128),
            per(PE, 128),
            per(PE, 128),
            pl.BlockSpec((PATCHES, 128), lambda c: (c, 0)),
        ),
        scratch_shapes=[
            pltpu.VMEM((8, 8, tokens), I32),
            pltpu.VMEM((8, 8, 1024), F32),
            pltpu.VMEM((8, 8, 128), I32),
            pltpu.VMEM((8, 8, 128), F32),
            pltpu.VMEM((2, 128, PE), F32),
            pltpu.VMEM((PE, D), F32),
            pltpu.VMEM((PE, D), BF),
            pltpu.VMEM((16, D), F32),
        ],
        compiler_params=params(44),
        cost_estimate=cost(30e9, 20e6, 8e6),
        name="point_forward",
    )(where, *inputs, *([kept] if part else []))


def layer_weights(where, shards, w_main, w_two, whole):
    own, near, far_a, far_b, last_a, last_b = shards
    half = where[1] & 1
    for i, (first, second) in enumerate(((far_a, far_b), (last_a, last_b))):
        whole[i, :, pl.ds(pl.multiple_of(half * L_HALF, L_HALF), L_HALF)] = first[...]
        whole[i, :, pl.ds(pl.multiple_of((1 - half) * L_HALF, L_HALF), L_HALF)] = second[...]
    for pos, shard in enumerate((own, near, whole.at[0], whole.at[1])):
        rank = pos ^ where[0]
        w_main[pl.ds(pl.multiple_of(rank * 96, 96), 96), :] = shard[:, 0:3072]
        for q in range(4):
            rows = pl.ds(pl.multiple_of(rank * 384 + q * 96, 96), 96)
            w_two[rows, :] = shard[:, 3072 + q * 384 : 3456 + q * 384]


def norm(x):
    centred = x - jnp.mean(x, -1, keepdims=True)
    scale = lax.rsqrt(jnp.mean(centred * centred, -1, keepdims=True) + 1e-06)
    return centred * scale, scale


def norm_back(grad, x, gain):
    hat, scale = norm(x)
    d_gain = jnp.sum(grad * hat, 0, keepdims=True)
    inner = grad * gain
    d_x = scale * (
        inner - jnp.mean(inner, -1, keepdims=True) - hat * jnp.mean(inner * hat, -1, keepdims=True)
    )
    return d_x, d_gain


def cloud_rows(ref, start, lanes):
    return jnp.concatenate([ref[pl.ds(start, 64), lanes], ref[TOP:ROWS, lanes]], 0)


def lane_masks():
    first = (iota((1, 128), 1) < HEAD_DIM).astype(F32)
    return first.astype(BF), (1.0 - first).astype(BF)


def layer_forward_kernel(
    where, xa, xb, small, pick, s0, s1, s2, s3, s4, s5,
    m_ref, xo_ref, y_ref, qkv_ref, a_ref, o_ref, z_ref, act_ref, slope_ref, f_ref, w_main, w_two,
    x_all, o_cls, whole,
):
    layer_weights(where, (s0, s1, s2, s3, s4, s5), w_main, w_two, whole)
    x_all[0 : TOP // 2, :] = xa[...]
    x_all[TOP // 2 : TOP, :] = xb[...]
    opening = jnp.broadcast_to(small[9:10, :], (16, D))
    x_all[TOP:ROWS, :] = jnp.where(iota((16, D), 0) < 8, opening, 0.0)
    hat, _ = norm(x_all[...])
    y_ref[...] = (hat * small[6:7, :]).astype(BF)
    qkv_ref[...] = dot(y_ref[...], w_main[:, 0:1152]).astype(BF)
    o_cls[...] = jnp.zeros_like(o_cls)
    mask0, mask1 = lane_masks()

    def one_cloud(c, carry):
        start = pl.multiple_of(c * 64, 64)
        column = iota((160, 80), 1)
        allowed = (column < 64) | (column == c + 64)
        for p in range(3):
            q = cloud_rows(qkv_ref, start, slice(p * 128, p * 128 + 128))
            k = cloud_rows(qkv_ref, start, slice(384 + p * 128, 512 + p * 128))
            v = cloud_rows(qkv_ref, start, slice(768 + p * 128, 896 + p * 128))
            both = jnp.concatenate([q * mask0, q * mask1], 0)
            scores = dot(both, k, ((1,), (1,))) * HEAD_DIM**-0.5
            scores = jnp.where(allowed, scores, -1e30)
            top = jnp.max(scores, -1, keepdims=True)
            e = jnp.exp(scores - top)
            a = (e / jnp.sum(e, -1, keepdims=True)).astype(BF)
            a_ref[c * 3 + p] = a
            o = dot(a, v)
            pair = jnp.where(iota((80, 128), 1) < HEAD_DIM, o[0:80], o[80:160])
            lanes = slice(p * 128, p * 128 + 128)
            o_ref[pl.ds(start, 64), lanes] = pair[0:64].astype(BF)
            o_cls[:, lanes] += jnp.where(iota((16, 128), 0) == c, pair[64:80], 0.0)
        return carry

    lax.fori_loop(0, 8, one_cloud, 0, unroll=4)
    o_ref[TOP:ROWS, :] = o_cls[...].astype(BF)
    m_ref[...] = x_all[...] + dot(o_ref[...], w_main[:, 1152:1536])
    hat, _ = norm(m_ref[...])
    z_ref[...] = (hat * small[7:8, :]).astype(BF)
    for part in range(3):
        lanes = slice(part * 512, part * 512 + 512)
        hidden = dot(z_ref[...], w_main[:, 1536 + part * 512 : 2048 + part * 512])
        value, slope = gelu_pair(hidden)
        act_ref[:, lanes] = value.astype(BF)
        slope_ref[:, lanes] = slope.astype(BF)
    xo = m_ref[0:TOP, :] + dot(act_ref[0:TOP, :], w_two[...])
    xo_ref[...] = xo
    hat, _ = norm(xo)
    f_ref[...] = dot(pick[...], (hat * small[8:9, :]).astype(BF)).astype(BF)


def layer_forward(where, xp, small, pick, shards):
    return pl.pallas_call(
        layer_forward_kernel,
        out_shape=(
            shape((ROWS, D)),
            shape((TOP, D)),
            shape((ROWS, D), BF),
            shape((ROWS, 1152), BF),
            shape((24, 160, 80), BF),
            shape((ROWS, D), BF),
            shape((ROWS, D), BF),
            shape((ROWS, FF), BF),
            shape((ROWS, FF), BF),
            shape((CAP, D), BF),
            shape((D, 3072), BF),
            shape((FF, D), BF),
        ),
        in_specs=[SM] + [VM] * 10,
        out_specs=(VM,) * 12,
        scratch_shapes=[
            pltpu.VMEM((ROWS, D), F32),
            pltpu.VMEM((16, D), F32),
            pltpu.VMEM((2, 96, L_WIDE), BF),
        ],
        compiler_params=params(24),
        cost_estimate=cost(1e4, 1e3),
        name="layer_forward",
    )(where, *xp, small, pick, *shards)


def head_scores_kernel(where, f0, f1, *refs):
    if len(refs) == 9:
        pieces, (codes, e_ref, stat_ref, table, scores) = refs[:4], refs[4:]
        for pos, piece in enumerate(pieces):
            rows = pl.ds(pl.multiple_of((pos ^ where[0]) * 96, 96), 96)
            table[rows, :] = piece[...] if len(piece.shape) == 2 else piece[0]
        begin = 0
    else:
        table, codes, e_ref, stat_ref, scores = refs
        begin = 2
    base = where[0] * VQ
    for half, rows in enumerate((f0, f1)):
        best = jnp.full((CAP, 128), -jnp.inf, F32)
        for t in range(4):
            part = dot(rows[...], table[:, t * 512 : t * 512 + 512])
            scores[:, t * 512 : t * 512 + 512] = part
            for u in range(4):
                best = jnp.maximum(best, part[:, u * 128 : u * 128 + 128])
        top = jnp.max(best, -1, keepdims=True)
        code = codes[begin + half] - base
        total = jnp.zeros((CAP, 128), F32)
        aimed = jnp.zeros((CAP, 128), F32)
        for u in range(16):
            lanes = slice(u * 128, u * 128 + 128)
            part = scores[:, lanes]
            e = jnp.exp(part - top)
            e_ref[half, :, lanes] = e.astype(BF)
            total = total + e
            aimed = aimed + jnp.where(iota((CAP, 128), 1) + u * 128 == code, part, 0.0)
        lane = iota((CAP, 128), 1)
        both = jnp.where(
            lane == 0,
            top,
            jnp.where(
                lane == 1,
                jnp.sum(total, -1, keepdims=True),
                jnp.where(lane == 2, jnp.sum(aimed, -1, keepdims=True), 0.0),
            ),
        )
        both = jnp.concatenate([both, jnp.zeros((CAPL - CAP, 128), F32)], 0)
        stat_ref[half] = jnp.transpose(both)[0:8, :]


def head_scores(where, rows, pieces, codes):
    outs = [shape((2, CAP, VQ), BF), shape((2, 8, CAPL))]
    if len(pieces) == 4:
        outs.append(shape((D, VQ), BF))
    return pl.pallas_call(
        head_scores_kernel,
        out_shape=tuple(outs),
        in_specs=[SM] + [VM] * (3 + len(pieces)),
        out_specs=(VM,) * len(outs),
        scratch_shapes=[pltpu.VMEM((CAP, VQ), F32)],
        compiler_params=params(20),
        cost_estimate=cost(4e9, 4e6, 3e6),
        name="head_scores",
    )(where, *rows, *pieces, codes)


def head_back_kernel(begin, where, e_ref, t0, t1, t2, t3, codes, table, d_ref, keep, send, *losses):
    stats = (t0, t1, t2, t3)
    columns, aims = [], []
    for half in range(2):
        tops = [stats[q][half ^ (q & 1), 0:1, :] for q in range(4)]
        sums = [stats[q][half ^ (q & 1), 1:2, :] for q in range(4)]
        top = jnp.maximum(jnp.maximum(tops[0], tops[1]), jnp.maximum(tops[2], tops[3]))
        total = jnp.zeros((1, CAPL), F32)
        for q in range(4):
            total = total + sums[q] * jnp.exp(tops[q] - top)
        columns.append(jnp.exp(tops[0] - top) / total)
        aims.append(jnp.exp(t0[half, 2:3, :] - top) / total - 1.0)
        if half == 0:
            aimed = (t0[0, 2:3, :] + t1[1, 2:3, :]) + (t2[0, 2:3, :] + t3[1, 2:3, :])
            loss = top + jnp.log(total) - aimed
    block = jnp.concatenate(columns + aims + [loss, jnp.zeros((123, CAPL), F32)], 0)
    turned = jnp.transpose(block)[0:CAP, :]
    if begin == 0:
        loss = jnp.where(codes[0][:, 0:1] >= 0, turned[:, 4:5], 0.0)
        losses[0][...] = jnp.broadcast_to(jnp.sum(loss, 0, keepdims=True), (8, 128))
    base = where[0] * VQ
    for half in range(2):
        code = codes[begin + half]
        scale = jnp.where(code[:, 0:1] >= 0, turned[:, half : half + 1], 0.0)
        aim = turned[:, 2 + half : 3 + half]
        code = code - base
        for u in range(16):
            lanes = slice(u * 128, u * 128 + 128)
            hit = iota((CAP, 128), 1) + u * 128 == code
            grad = jnp.where(hit, aim, e_ref[half, :, lanes].astype(F32) * scale)
            d_ref[half, :, lanes] = grad.astype(BF)
        back = dot(d_ref[half], table[...], ((1,), (1,)))
        if half == 0:
            keep[...] = back
        else:
            send[...] = back.astype(BF)


def head_back(where, begin, e, stats, codes, table):
    outs = [shape((2, CAP, VQ), BF), shape((CAP, D)), shape((CAP, D), BF)]
    if begin == 0:
        outs.append(shape((8, 128)))
    return pl.pallas_call(
        functools.partial(head_back_kernel, begin),
        out_shape=tuple(outs),
        in_specs=[SM] + [VM] * 7,
        out_specs=(VM,) * len(outs),
        compiler_params=params(20),
        cost_estimate=cost(4e9, 6e6),
        name="head_back",
    )(where, e, *stats, codes, table)


def place_y(rel):
    return rel & 1, ((rel >> 1) & 1) * 2 + ((rel >> 2) & 1)


def place_z(rel):
    return (rel >> 1) & 1, (rel & 1) * 2 + ((rel >> 2) & 1)


def place_b(rel):
    return (rel >> 1) & 1, ((rel >> 2) & 1) * 2 + (rel & 1)


def head_grad_kernel(where, f0, f1, f2, f3, d0, d1, a_keep, a_send, b_keep, b_send, joined, held):
    for pos, rows in enumerate((f0, f1, f2, f3)):
        joined[:, pos * CAP : (pos + 1) * CAP] = jnp.transpose(rows[...].astype(F32)).astype(BF)
    for rel in range(SPLIT):
        lanes = pl.ds(pl.multiple_of((rel ^ where[1]) * 256, 256), 256)
        cols = jnp.concatenate([d0[0, :, lanes], d0[1, :, lanes], d1[0, :, lanes], d1[1, :, lanes]], 0)
        held[rel % 2] = dot(joined[...], cols).astype(BF)
        first_a, index_a = place_y(rel)
        first_b, index_b = place_b(rel)
        for pos in range(4):
            rows = held[rel % 2, pl.ds(pl.multiple_of((pos ^ where[0]) * 96, 96), 96), :]
            if pos < 2:
                ref, index = (a_send if first_a else a_keep), index_a
            else:
                ref, index = (b_send if first_b else b_keep), index_b
            for j in range(2):
                ref[index, pos & 1, j * 96 : j * 96 + 96, :] = rows[:, j * 128 : j * 128 + 128]


def head_grad(where, rows, *d):
    return pl.pallas_call(
        head_grad_kernel,
        out_shape=(shape((4, 2, H_PIECE, 128), BF),) * 4,
        in_specs=[SM] + [VM] * 6,
        out_specs=(VM,) * 4,
        scratch_shapes=[pltpu.VMEM((D, 4 * CAP), BF), pltpu.VMEM((2, D, 256), BF)],
        compiler_params=params(16),
        cost_estimate=cost(4e9, 8e6),
        name="head_grad",
    )(where, *rows, *d)


def hold_grad(held, block, grad):
    for r in range(4):
        held[r, block * 96 : block * 96 + 96, :] = grad[r * 96 : r * 96 + 96, :].astype(BF)


def spread_grad(where, held, keep, send, piece_rows):
    for pos in range(4):
        ref, far = (send if pos & 1 else keep), pos >> 1
        for rel in range(SPLIT):
            first, index = place_y(rel)
            start = pl.multiple_of((rel ^ where[1]) * piece_rows, 16)
            ref[far, first, index] = held[pos ^ where[0], pl.ds(start, piece_rows), :]


def ffn_backward_kernel(
    where, keep, rc, rx, pick, xo, m_ref, small, z_ref, act_ref, slope_ref, w_main, w_two,
    keep_ref, send_ref, dm_ref, sg_ref,
    d_hid, held,
):
    compact = keep[...] + rc[...].astype(F32) + rx[...].astype(F32)
    high = compact.astype(BF)
    low = (compact - high.astype(F32)).astype(BF)
    d_rows = dot(pick[...], high, ((0,), (0,))) + dot(pick[...], low, ((0,), (0,)))
    d_out, d_gain = norm_back(d_rows, xo[...], small[8:9, :])
    sg_ref[...] = jnp.zeros_like(sg_ref)
    sg_ref[1:2, :] = d_gain
    grad_b = d_out.astype(BF)
    for part in range(3):
        lanes = slice(part * 512, part * 512 + 512)
        back = dot(grad_b, w_two[lanes, :], ((1,), (1,)))
        d_hid[:, lanes] = (back * slope_ref[0:TOP, lanes].astype(F32)).astype(BF)
    d_fc2 = dot(jnp.transpose(d_out).astype(BF), act_ref[0:TOP, :])
    for j in range(3):
        for q in range(4):
            parts = [
                d_fc2[q * 96 : q * 96 + 96, r * 384 + j * 128 : r * 384 + j * 128 + 128]
                for r in range(4)
            ]
            hold_grad(held, 12 + j * 4 + q, jnp.concatenate(parts, 0))
    turned = jnp.transpose(z_ref[0:TOP, :].astype(F32)).astype(BF)
    for part in range(3):
        grad = dot(turned, d_hid[:, part * 512 : part * 512 + 512])
        for j in range(4):
            hold_grad(held, part * 4 + j, grad[:, j * 128 : j * 128 + 128])
    spread_grad(where, held, keep_ref, send_ref, F_PIECE)
    d_z = dot(d_hid[...], w_main[:, 1536:3072], ((1,), (1,)))
    d_m, d_gain = norm_back(d_z, m_ref[0:TOP, :], small[7:8, :])
    sg_ref[0:1, :] = d_gain
    dm_ref[...] = d_m + d_out


def ffn_backward(where, *arrays):
    return pl.pallas_call(
        ffn_backward_kernel,
        out_shape=(
            shape((2, 2, 4, F_PIECE, 128), BF),
            shape((2, 2, 4, F_PIECE, 128), BF),
            shape((TOP, D)),
            shape((8, D)),
        ),
        in_specs=[SM] + [VM] * 12,
        out_specs=(VM,) * 4,
        scratch_shapes=[
            pltpu.VMEM((TOP, FF), BF),
            pltpu.VMEM((4, F_ROWS, 128), BF),
        ],
        compiler_params=params(24),
        cost_estimate=cost(10e9, 10e6),
        name="ffn_backward",
    )(where, *arrays)


def attention_backward_kernel(
    where, dm_ref, sgf, xa, xb, small, y_ref, qkv_ref, a_ref, o_ref, hid_a, hid_b, w_main,
    keep_ref, send_ref, dx_ref, sg_ref,
    x_all, d_o, d_qkv, d_cls, held,
):
    x_all[0 : TOP // 2, :] = xa[...]
    x_all[TOP // 2 : TOP, :] = xb[...]
    opening = jnp.broadcast_to(small[9:10, :], (16, D))
    x_all[TOP:ROWS, :] = jnp.where(iota((16, D), 0) < 8, opening, 0.0)
    m_b = dm_ref[...].astype(BF)
    d_o[...] = dot(m_b, w_main[:, 1152:1536], ((1,), (1,))).astype(BF)
    d_cls[...] = jnp.zeros_like(d_cls)
    mask0, mask1 = lane_masks()

    def one_cloud(c, carry):
        start = pl.multiple_of(c * 64, 64)
        for p in range(3):
            lanes = slice(p * 128, p * 128 + 128)
            q = qkv_ref[pl.ds(start, 64), lanes]
            k = cloud_rows(qkv_ref, start, slice(384 + p * 128, 512 + p * 128))
            v = cloud_rows(qkv_ref, start, slice(768 + p * 128, 896 + p * 128))
            d = d_o[pl.ds(start, 64), lanes]
            q2 = jnp.concatenate([q * mask0, q * mask1], 0)
            d2 = jnp.concatenate([d * mask0, d * mask1], 0)
            a = jnp.concatenate([a_ref[c * 3 + p, 0:64, :], a_ref[c * 3 + p, 80:144, :]], 0)
            d_a = dot(d2, v, ((1,), (1,)))
            full = a.astype(F32)
            d_s = full * (d_a - jnp.sum(d_a * full, -1, keepdims=True)) * HEAD_DIM**-0.5
            d_s = d_s.astype(BF)
            d_q = dot(d_s, k)
            d_q = jnp.where(iota((64, 128), 1) < HEAD_DIM, d_q[0:64], d_q[64:128])
            d_k = dot(d_s, q2, ((0,), (0,)))
            d_v = dot(a, d2, ((0,), (0,)))
            d_qkv[pl.ds(start, 64), p * 128 : p * 128 + 128] = d_q.astype(BF)
            d_qkv[pl.ds(start, 64), 384 + p * 128 : 512 + p * 128] = d_k[0:64].astype(BF)
            d_qkv[pl.ds(start, 64), 768 + p * 128 : 896 + p * 128] = d_v[0:64].astype(BF)
            d_cls[:, 384 + p * 128 : 512 + p * 128] += d_k[64:80]
            d_cls[:, 768 + p * 128 : 896 + p * 128] += d_v[64:80]
        return carry

    lax.fori_loop(0, 8, one_cloud, 0, unroll=4)
    d_qkv[TOP:ROWS, :] = d_cls[...].astype(BF)
    turned = jnp.transpose(o_ref[0:TOP, :].astype(F32)).astype(BF)
    grad = dot(turned, m_b)
    for j in range(3):
        hold_grad(held, 9 + j, grad[:, j * 128 : j * 128 + 128])
    turned = jnp.transpose(y_ref[...].astype(F32)).astype(BF)
    for part in range(3):
        grad = dot(turned, d_qkv[:, part * 384 : part * 384 + 384])
        for j in range(3):
            hold_grad(held, part * 3 + j, grad[:, j * 128 : j * 128 + 128])
    spread_grad(where, held, keep_ref, send_ref, T_PIECE)
    d_y = dot(d_qkv[...], w_main[:, 0:1152], ((1,), (1,)))
    d_x, d_gain = norm_back(d_y, x_all[...], small[6:7, :])
    d_x = d_x + jnp.concatenate([dm_ref[...], jnp.zeros((16, D), F32)], 0)
    dx_ref[...] = d_x
    sg_ref[...] = jnp.zeros_like(sg_ref)
    sg_ref[6:7, :] = d_gain
    sg_ref[7:9, :] = sgf[0:2, :]
    sg_ref[9:10, :] = jnp.sum(d_x[TOP:ROWS], 0, keepdims=True)
    hidden = jnp.concatenate([hid_a[:, 0:1], hid_b[:, 0:1]], 0)
    sg_ref[10:11, :] = jnp.sum(jnp.where(hidden > 0.0, d_x[0:TOP], 0.0), 0, keepdims=True)


def attention_backward(where, *arrays):
    return pl.pallas_call(
        attention_backward_kernel,
        out_shape=(
            shape((2, 2, 4, T_PIECE, 128), BF),
            shape((2, 2, 4, T_PIECE, 128), BF),
            shape((ROWS, D)),
            shape((16, D)),
        ),
        in_specs=[SM] + [VM] * 12,
        out_specs=(VM,) * 4,
        scratch_shapes=[
            pltpu.VMEM((ROWS, D), F32),
            pltpu.VMEM((TOP, D), BF),
            pltpu.VMEM((ROWS, 1152), BF),
            pltpu.VMEM((16, 1152), F32),
            pltpu.VMEM((4, T_ROWS, 128), BF),
        ],
        compiler_params=params(20),
        cost_estimate=cost(10e9, 10e6),
        name="attention_backward",
    )(where, *arrays)


def point_backward_kernel(
    where, dx_ref, hid, kept_ref, rel_ref, cen_ref, up_ref, slope_up_ref, e_ref, *rest,
):
    c = pl.program_id(0)
    slope_ref = kept_ref.at[:, 0:D]
    inner_ref = kept_ref.at[:, D : D + PE]
    slope_in_ref = kept_ref.at[:, D + PE : D + 2 * PE]
    first, last = len(rest) == 5, len(rest) == 11
    w_out, spread, lift = rest[-3:]
    if first:
        d_out, d_in = rest[:2]
    elif last:
        start_out, start_in, sg_ref, loss_ref, mask, g_ref, d_out, d_in = rest[:8]
    else:
        start_out, start_in, d_out, d_in = rest[:4]

    @pl.when(c == 0)
    def _():
        for r in range(4):
            for i in range(2):
                for j in range(3):
                    w_out[i, r * 32 : (r + 1) * 32, j * 128 : (j + 1) * 128] = e_ref[
                        r ^ where[0], (i * 3 + j) * 32 : (i * 3 + j + 1) * 32, :
                    ]
        if first:
            d_out[...] = jnp.zeros_like(d_out)
            d_in[...] = jnp.zeros_like(d_in)
        else:
            d_out[...] = start_out[...]
            d_in[...] = start_in[...]

    across = ((1,), (1,))
    rows = dx_ref[...]
    place = rows.astype(BF)
    d_out[1] += dot(up_ref[0, :, 0:PATCHES], place)
    d_up = (dot(w_out[1], place, across) * slope_up_ref[0, :, 0:PATCHES]).astype(BF)
    d_in[1] += dot(d_up, cen_ref[0, :, 0:PATCHES], across)
    d_patch = jnp.where(hid[:, 0:1] > 0.0, 0.0, rows) * (1.0 / NB)
    turned = jnp.transpose(jnp.concatenate([d_patch, d_patch], 0))
    for step in range(PATCHES * NB // CH):
        at = slice(step * CH, (step + 1) * CH)
        for q in range(step * CH // 128, (step + 1) * CH // 128):
            lanes = slice(q * 128, q * 128 + 128)
            spread[:, lanes] = (turned * slope_ref[0, :, lanes].astype(F32)).astype(BF)
        back = dot(w_out[0], spread[:, at])
        lift[:, at] = (back * slope_in_ref[0, :, at].astype(F32)).astype(BF)
    d_out[0] += dot(inner_ref[0], spread[...], across)
    d_in[0] += dot(lift[...], rel_ref[0], across)
    if not last:
        return

    @pl.when(c == pl.num_programs(0) - 1)
    def _():
        lane = iota((8, 128), 1)
        seen = jnp.sum(jnp.sum(mask[...].astype(F32), 1, keepdims=True), 0, keepdims=True)
        ins = [
            jnp.transpose(jnp.concatenate([d_in[i], jnp.zeros((PE, 120), F32)], 1))[0:8]
            for i in range(2)
        ]
        for r in range(4):
            pos = r ^ where[0]
            pos = (pos & 1) * 2 + (pos >> 1)
            for i in range(2):
                for j in range(3):
                    g_ref[pos, (i * 3 + j) * 32 : (i * 3 + j + 1) * 32, :] = d_out[
                        i, r * 32 : (r + 1) * 32, j * 128 : (j + 1) * 128
                    ]
            g_ref[pos, 192:216, :] = jnp.zeros((24, 128), F32)
            turn = (128 - r * 32) % 128
            for i in range(2):
                rolled = ins[i] if turn == 0 else pltpu.roll(ins[i], turn, 1)
                rolled = jnp.where(lane < 32, rolled, 0.0)
                g_ref[pos, 192 + i * 3 : 195 + i * 3, :] = rolled[0:3]
            g_ref[pos, 198:203, 0:96] = sg_ref[6:11, r * 96 : (r + 1) * 96]
            g_ref[pos, 208:209, :] = loss_ref[0:1, :]
            g_ref[pos, 209:210, :] = jnp.broadcast_to(seen, (1, 128))


def point_backward(where, dx, kept, e_all, begin, count, start=(), last=()):
    big, rel, cen, up, slope_up, hid = kept
    local = begin % rel.shape[0]
    tokens = PATCHES * NB

    def whole(array):
        return pl.BlockSpec(array.shape, lambda c: (0,) * len(array.shape))

    def per(*dims):
        return pl.BlockSpec((1,) + dims, lambda c: (c + local, 0, 0))

    sums = (shape((2, PE, D)), shape((2, PE, 8)))
    more = (*start, *last)
    packed = shape((4, E_GRAD, 128))
    return pl.pallas_call(
        point_backward_kernel,
        grid=(count,),
        out_shape=packed if last else sums,
        in_specs=[
            SM,
            pl.BlockSpec((PATCHES, D), lambda c: (c + begin, 0)),
            pl.BlockSpec((PATCHES, 128), lambda c: (c + local, 0)),
            pl.BlockSpec((1, D + 2 * PE, tokens), lambda c: (c + begin, 0, 0)),
            per(8, tokens),
            per(8, 128),
            per(PE, 128),
            per(PE, 128),
            whole(e_all),
            *[whole(array) for array in more],
        ],
        out_specs=whole(packed) if last else tuple(whole(array) for array in sums),
        scratch_shapes=([pltpu.VMEM(array.shape, F32) for array in sums] if last else [])
        + [
            pltpu.VMEM((2, PE, D), BF),
            pltpu.VMEM((D, tokens), BF),
            pltpu.VMEM((PE, tokens), BF),
        ],
        compiler_params=params(44),
        cost_estimate=cost(6e9, 6e6),
        name="point_backward",
    )(where, dx, hid, big, rel, cen, up, slope_up, e_all, *more)


def squares_kernel(*refs):
    total = jnp.zeros((16, 128), F32)
    for ref in refs[:-2]:
        rows = ref.shape[-2]
        for lead in range(ref.shape[0] * (ref.shape[1] if len(ref.shape) == 4 else 1)):
            part = ref[divmod(lead, ref.shape[1])] if len(ref.shape) == 4 else ref[lead]
            part = part.astype(F32)
            total = total + jnp.sum((part * part).reshape(rows // 16, 16, 128), 0)
    part = refs[-2][0:208, :]
    total = total + jnp.sum((part * part).reshape(13, 16, 128), 0)
    total = jnp.sum(jnp.sum(total, 1, keepdims=True), 0, keepdims=True)
    refs[-1][...] = jnp.broadcast_to(total, (8, 128))


def squares(*arrays):
    return pl.pallas_call(
        squares_kernel,
        out_shape=shape((8, 128)),
        in_specs=[VM] * len(arrays),
        out_specs=VM,
        compiler_params=params(8),
        name="squares",
    )(*arrays)


def adam(grad, first, second, weight, factor, vector):
    rate = RATE_VECTOR if vector else RATE_MATRIX
    clipped = grad * factor
    first = BETA_ONE * first + (1 - BETA_ONE) * clipped
    second = BETA_TWO * second + (1 - BETA_TWO) * (clipped * clipped)
    level = second * (1.0 / (1 - BETA_TWO**STEP_NUMBER))
    root = level * lax.rsqrt(level) + EPSILON
    update = (first * (rate / (1 - BETA_ONE**STEP_NUMBER))) * pl.reciprocal(root)
    if vector:
        return first, second, weight - update
    return first, second, weight * (1.0 - rate * DECAY) - update


def clip_factor(s0, s1, e_ref):
    count = e_ref[209:210, :]
    length = jnp.sqrt(s0[0:1, :] + s1[0:1, :]) / count
    return jnp.minimum(1.0, CLIP / length) / count, length


def step_kernel(where, s0, s1, e_ref, f0, f1, t0, t1, a0, a1, b0, b1, *refs):
    ins, outs, scalars = refs[:27], refs[27:54], refs[54]
    done, joined, turned, sems = refs[55:82], refs[82], refs[83], refs[84]
    factor, length = clip_factor(s0, s1, e_ref)
    copies = []

    def send(which, at=None):
        for k in range(3):
            i = which * 3 + k
            source = done[i] if at is None else done[i].at[at]
            target = outs[i] if at is None else outs[i].at[at]
            copy = pltpu.make_async_copy(source, target, sems.at[len(copies)])
            copy.start()
            copies.append(copy)

    def update(which, at, grad, vector=False):
        w, m, v = (ins[which * 3 + k] for k in range(3))
        out = adam(grad, m[at], v[at], w[at], factor[:, 0 : grad.shape[-1]], vector)
        for k in range(3):
            done[which * 3 + k][at] = out[k]

    for piece in range(SPLIT):
        first, index = place_y(piece ^ where[1])
        rows = slice(T_ROWS + piece * F_PIECE, T_ROWS + (piece + 1) * F_PIECE)
        joined[rows, :] = jnp.where(first == 0, f0[index], f1[index])
        first, index = place_z(piece ^ where[1])
        rows = slice(piece * T_PIECE, (piece + 1) * T_PIECE)
        joined[rows, :] = jnp.where(first == 0, t0[index], t1[index])

    starts = {0: (2, 0), 9: (3, 9), 12: (4, 12)}
    which = base = 0
    for block in range(36):
        grad = joined[block * 96 : block * 96 + 96, :].astype(F32)
        if block >= 24:
            j, q = divmod(block - 24, 4)
            turned[q * 96 : q * 96 + 96, j * 128 : j * 128 + 128] = grad
            continue
        if block in starts:
            which, base = starts[block]
        j = block - base
        update(which, (0, slice(None), slice(j * 128, j * 128 + 128)), grad)
        if block in (8, 11, 23):
            send(which)
    grad = jnp.transpose(turned[...])
    for j in range(3):
        lanes = slice(j * 128, j * 128 + 128)
        update(5, (0, slice(None), lanes), grad[:, lanes])
    send(5)
    for i in range(2):
        for k in range(3):
            at = 192 + i * 3 + k
            update(0, (k, slice(i, i + 1)), e_ref[at : at + 1, 0:32])
        for j in range(3):
            block = i * 3 + j
            grad = e_ref[block * 32 : block * 32 + 32, :]
            update(1, (i, slice(None), slice(j * 128, j * 128 + 128)), grad)
    update(6, (slice(0, 3),), e_ref[198:201, 0:96], True)
    update(7, (slice(0, 2),), e_ref[201:203, 0:96], True)
    for which in (0, 1, 6, 7):
        send(which)
    scalars[0:1, :] = e_ref[208:209, :]
    scalars[1:2, :] = e_ref[209:210, :]
    scalars[2:3, :] = length
    for piece in range(32):
        quarter = (piece // SPLIT) ^ where[0]
        first_a, index_a = place_y((piece % SPLIT) ^ where[1])
        first_b, index_b = place_z((piece % SPLIT) ^ where[1])
        for j in range(2):
            lanes = slice(piece * 256 + j * 128, piece * 256 + j * 128 + 128)
            rows = slice(j * 96, j * 96 + 96)
            near = quarter & 1
            grad = jnp.where(
                quarter < 2,
                jnp.where(first_a == 0, a0[index_a, near, rows, :], a1[index_a, near, rows, :]),
                jnp.where(first_b == 0, b0[index_b, near, rows, :], b1[index_b, near, rows, :]),
            )
            update(8, (slice(None), lanes), grad.astype(F32))
        if piece % 4 == 3:
            send(8, (slice(None), slice((piece - 3) * 256, (piece + 1) * 256)))
    for copy in copies:
        copy.wait()


def step_all(where, sums, e, grads, states):
    outs = tuple(shape(array.shape) for array in states)
    return pl.pallas_call(
        step_kernel,
        out_shape=outs + (shape((8, 128)),),
        in_specs=[SM] + [VM] * (11 + len(states)),
        out_specs=(HB,) * len(outs) + (VM,),
        scratch_shapes=[pltpu.VMEM(array.shape, F32) for array in states]
        + [
            pltpu.VMEM((T_ROWS + F_ROWS, 128), BF),
            pltpu.VMEM((D, D), F32),
            pltpu.SemaphoreType.DMA((48,)),
        ],
        compiler_params=params(24),
        cost_estimate=cost(4e7, 3e7),
        name="step_all",
    )(where, *sums, e, *grads, *states)


def add(*parts):
    total = parts[0].astype(F32)
    for part in parts[1:]:
        total = total + part.astype(F32)
    return total.astype(BF)


def after(*arrays):
    return lax.optimization_barrier(arrays)


def body(dp, fsdp, *args):
    (
        points, centers, neighbours, mask, targets,
        embed_in, embed_in_m, embed_in_v, embed_out, embed_out_m, embed_out_v,
        qkv_w, qkv_m, qkv_v, proj_w, proj_m, proj_v, fc1_w, fc1_m, fc1_v, fc2_w, fc2_m, fc2_v,
        gains, gains_m, gains_v, special, special_m, special_v, head, head_m, head_v,
    ) = args
    rank = lax.axis_index("fsdp").astype(I32)
    group = lax.axis_index("dp").astype(I32)
    where = jnp.stack([rank, group % SPLIT])

    def swap(x, axis, bit):
        size = dp if axis == "dp" else fsdp
        return lax.ppermute(x, axis, [(i, i ^ bit) for i in range(size)])

    def higher(total):
        bit = SPLIT
        while bit < dp:
            total = add(total, swap(total, "dp", bit))
            bit *= 2
        return total

    embed_in, embed_in_m, embed_in_v = (
        jnp.transpose(array, (1, 0, 2)) for array in (embed_in, embed_in_m, embed_in_v)
    )
    e_own, l_own, l_send = pack(
        embed_in, embed_out, gains, special, mask, targets, qkv_w, proj_w, fc1_w, fc2_w
    )
    e_far = swap(e_own, "fsdp", 2)
    e_near = swap(e_own, "fsdp", 1)
    h_own, h_core, h_far = pack_head(where, head)
    e_far, l_send, h_own = after(e_far, l_send, h_own)
    l_far = swap(l_send, "fsdp", 2)
    e_all = jnp.stack([e_own, e_near, e_far, swap(e_far, "fsdp", 1)])
    xa, big, *kept_a = point_forward(where, points, centers, neighbours, mask, e_all, 0, 2)
    l_far, xa, e_all, l_own, h_far = after(l_far, xa, e_all, l_own, h_far)
    l_far_b = swap(l_far, "dp", 1)
    l_near = swap(l_own, "fsdp", 1)
    l_last = swap(l_far, "fsdp", 1)
    h_got = swap(h_far, "fsdp", 2)
    xb, big, *kept_b = point_forward(where, points, centers, neighbours, mask, e_all, 1, 2, big)
    l_far_b, xb, e_late = after(l_far_b, xb, e_all)
    codes, pick, small = choose(where, e_late)
    l_last_b = swap(l_far_b, "fsdp", 1)
    h_near = swap(h_core, "fsdp", 1)
    shards = (l_own, l_near, l_far, l_far_b, l_last, l_last_b)
    *kept, f_own, w_main, w_two = layer_forward(where, (xa, xb), small, pick, shards)
    m, xo, y, qkv, a, o, z, act, slope = kept
    f_far = swap(f_own, "fsdp", 2)
    f_near = swap(f_own, "fsdp", 1)
    h_got, f_near = after(h_got, f_near)
    pieces = (h_own, h_near, h_got, swap(h_got[1], "fsdp", 1))
    e01, stat01, table = head_scores(where, (f_own, f_near), pieces, codes)
    f_far, stat01, e01 = after(f_far, stat01, e01)
    f_last = swap(f_far, "fsdp", 1)
    near01, far01, last01 = (swap(stat01, "fsdp", pos) for pos in (1, 2, 3))
    e23, stat23 = head_scores(where, (f_far, f_last), (table,), codes)
    rows = (f_own, f_near, f_far, f_last)
    near23, far23, last23 = (swap(stat23, "fsdp", pos) for pos in (1, 2, 3))
    d23, keep23, send23 = head_back(where, 2, e23, (stat23, near23, far01, last01), codes, table)
    keep23, send23, far23, last23 = after(keep23, send23, far23, last23)
    got23 = swap(send23, "fsdp", 1)
    passed, far23 = after(add(keep23, got23), far23)
    got_far = swap(passed, "fsdp", 2)
    d01, keep, send, loss = head_back(where, 0, e01, (stat01, near01, far23, last23), codes, table)
    got = swap(send, "fsdp", 1)
    a_keep, a_send, b_keep, b_send = head_grad(where, rows, d01, d23)

    a_send, b_send, got_far, got = after(a_send, b_send, got_far, got)
    a_1 = swap(a_send, "dp", 1)
    b_1 = swap(b_send, "dp", 2)
    f_keep, f_send, dm, sgf = ffn_backward(
        where, keep, got, got_far, pick, xo, m, small, z, act, slope, w_main, w_two
    )
    a_1, b_1, f_send, dm = after(a_1, b_1, f_send, dm)
    a_2 = swap(add(a_keep[2:], a_1[2:]), "dp", 2)
    b_2 = swap(add(b_keep[2:], b_1[2:]), "dp", 4)
    f_core = swap(f_send, "fsdp", 1)
    f_core, dm = after(f_core, dm)
    f_x = swap(add(f_keep[1], f_core[1]), "fsdp", 2)
    t_keep, t_send, dx, sg = attention_backward(
        where, dm, sgf, xa, xb, small, y, qkv, a, o, kept_a[-1], kept_b[-1], w_main
    )
    a_2, b_2, f_x, t_send, dx = after(a_2, b_2, f_x, t_send, dx)
    t_core = swap(t_send, "fsdp", 1)
    f_low = add(f_keep[0], f_core[0], f_x)
    f_y = swap(f_low[1], "dp", 1)
    a_low = add(a_keep[:2], a_1[:2])
    b_low = add(b_keep[:2], b_1[:2])
    a_3 = swap(add(a_low[1], a_2[1]), "dp", 4)
    b_3 = swap(add(b_low[1], b_2[1]), "dp", 1)
    t_core, dx = after(t_core, dx)
    t_x = swap(add(t_keep[1], t_core[1]), "fsdp", 2)
    part = point_backward(where, dx, (big, *kept_a), e_all, 0, 3)
    a_3, b_3, t_x, part = after(a_3, b_3, t_x, part)
    ab_sum = higher(
        jnp.concatenate([add(a_low[0], a_2[0], a_3), add(b_low[0], b_2[0], b_3)], 0)
    )
    h_got = [swap(ab_sum[pos], "fsdp", pos) for pos in (1, 2, 3)]
    t_low = add(t_keep[0], t_core[0], t_x)
    t_y = swap(t_low[1], "dp", 1)
    part = point_backward(where, dx, (big, *kept_a), e_all, 3, 1, part)
    *h_got, f_y, t_y, part = after(*h_got, f_y, t_y, part)
    h_mine = jnp.stack([ab_sum[0], *h_got])
    h_two = swap(h_mine, "dp", 4)
    ft_low = jnp.concatenate([add(f_low[0], f_y), add(t_low[0], t_y)], 1)
    ft_z1 = swap(ft_low[2:], "dp", 2)
    e_grad = point_backward(where, dx, (big, *kept_b), e_all, 4, 4, part, (sg, loss, mask))
    h_two, ft_z1, e_grad = after(h_two, ft_z1, e_grad)
    e_core = swap(e_grad[2:], "fsdp", 1)
    h_both = jnp.stack([h_mine, h_two])
    a_both, b_both = h_both[:, 0:2], h_both[:, 2:4]
    a_pair = swap(a_both, "dp", 2)
    b_pair = swap(b_both, "dp", 1)
    ft_z2 = swap(add(ft_low[1], ft_z1[1]), "dp", 4)
    e_x = swap(e_grad[1] + e_core[1], "fsdp", 2)
    e_x, ft_z2, a_pair, b_pair = after(e_x, ft_z2, a_pair, b_pair)
    ft_sum = higher(add(ft_low[0], ft_z1[0], ft_z2))
    ft_two = swap(ft_sum, "dp", 4)
    a_four = jnp.concatenate([a_both, a_pair], 0)
    b_four = jnp.concatenate([b_both, b_pair], 0)
    b_end = swap(b_four, "dp", 2)
    a_end = swap(a_four, "dp", 1)
    e_sum = e_grad[0] + e_core[0] + e_x
    e_y = swap(e_sum, "dp", 1)
    e_y, ft_two = after(e_y, ft_two)
    ft_both = jnp.stack([ft_sum, ft_two])
    f_both, t_both = ft_both[:, :F_PIECE], ft_both[:, F_PIECE:]
    f_pair = swap(f_both, "dp", 2)
    t_pair = swap(t_both, "dp", 1)
    e_sum = e_sum + e_y
    e_z2 = swap(e_sum, "dp", 4)
    e_z2, f_pair, t_pair, a_end, b_end = after(e_z2, f_pair, t_pair, a_end, b_end)
    f_four = jnp.concatenate([f_both, f_pair], 0)
    t_four = jnp.concatenate([t_both, t_pair], 0)
    f_end = swap(f_four, "dp", 1)
    t_end = swap(t_four, "dp", 2)
    e_sum = e_sum + e_z2
    e_sum = e_sum + swap(e_sum, "dp", 2)
    bit = SPLIT
    while bit < dp:
        e_sum = e_sum + swap(e_sum, "dp", bit)
        bit *= 2
    grads = (f_four, f_end, t_four, t_end, a_four, a_end, b_four, b_end)

    sums = squares(*grads, e_sum)
    sums = sums + swap(sums, "fsdp", 1)
    sums = (sums, swap(sums, "fsdp", 2))
    states = (
        embed_in, embed_in_m, embed_in_v, embed_out, embed_out_m, embed_out_v,
        qkv_w, qkv_m, qkv_v, proj_w, proj_m, proj_v, fc1_w, fc1_m, fc1_v, fc2_w, fc2_m, fc2_v,
        gains, gains_m, gains_v, special, special_m, special_v, head, head_m, head_v,
    )
    *news, scalars = step_all(where, sums, e_sum, grads, states)
    news[:3] = [jnp.transpose(array, (1, 0, 2)) for array in news[:3]]
    return (*news, scalars[0, 0], scalars[1, 0], scalars[2, 0])


def solution(mesh):
    in_specs = (
        P(None, ("dp", "fsdp"), None),
        *[P(("dp", "fsdp"), None)] * 4,
        *[P(None, None, "fsdp")] * 3,
        *[P(None, "fsdp", None)] * 15,
        *[P(None, "fsdp")] * 6,
        *[P("fsdp", None)] * 3,
    )
    out_specs = in_specs[5:] + (P(), P(), P())
    step = functools.partial(body, mesh.shape["dp"], mesh.shape["fsdp"])
    return jax.shard_map(
        step, mesh=mesh, in_specs=in_specs, out_specs=out_specs, check_vma=False
    )
```

```python
import functools

import jax
import jax.numpy as jnp
from jax import lax
from jax.experimental import pallas as pl
from jax.experimental.pallas import tpu as pltpu
from jax.sharding import PartitionSpec as P

BF = jnp.bfloat16
F32 = jnp.float32
I32 = jnp.int32
D = 384
HEAD_DIM = 64
FF = 1536
PE = 128
NB = 32
PATCHES = 64
STEP_NUMBER = 10
MOST_MASKED = 36

BETA_ONE = 0.9
BETA_TWO = 0.95
EPSILON = 1e-08
DECAY = 0.05
RATE_MATRIX = 0.1
RATE_VECTOR = 0.5
CLIP = 0.005

TOP = 512
ROWS = 528
CAP = 288
CAPL = 384
VQ = 2048
SPLIT = 8
L_WIDE = 4608
L_HALF = 2304
F_ROWS = 2304
F_PIECE = F_ROWS // SPLIT
T_ROWS = 1152
T_PIECE = T_ROWS // SPLIT
H_PIECE = 192
E_ROWS = 224
E_GRAD = 216
CH = 256

GA = 0.7978845608028654
GB = GA * 0.044715


def dot(left, right, dims=((1,), (0,))):
    return lax.dot_general(left, right, (dims, ((), ())), preferred_element_type=F32)


def gelu_pair(x):
    square = x * x
    half = 0.5 * jnp.tanh(x * (GA + GB * square)) + 0.5
    value = x * half
    slope = half + (value * (1.0 - half)) * (2.0 * GA + (6.0 * GB) * square)
    return value, slope


def iota(shape, axis):
    return lax.broadcasted_iota(I32, shape, axis)


def params(mib=48):
    return pltpu.CompilerParams(vmem_limit_bytes=mib << 20)


VM = pl.BlockSpec(memory_space=pltpu.VMEM)
SM = pl.BlockSpec(memory_space=pltpu.SMEM)
HB = pl.BlockSpec(memory_space=pltpu.HBM)


def shape(dims, dtype=F32):
    return jax.ShapeDtypeStruct(dims, dtype)


def cost(flops, moved, trans=0):
    return pl.CostEstimate(flops=int(flops), bytes_accessed=int(moved), transcendentals=int(trans))


def pack_kernel(*refs):
    sources, (e_out, l_out, l_send) = refs[:10], refs[10:13]
    local, scr, sems = refs[13:23], refs[23], refs[24]
    copies = [
        pltpu.make_async_copy(source, target, sems.at[i])
        for i, (source, target) in enumerate(zip(sources, local))
    ]
    for copy in copies:
        copy.start()
    for copy in copies[:6]:
        copy.wait()
    ein, eout, gains, special, mask, targets, qkv, proj, fc1, fc2 = local
    for i in range(2):
        for j in range(3):
            e_out[(i * 3 + j) * 32 : (i * 3 + j + 1) * 32, :] = eout[
                i, :, j * 128 : (j + 1) * 128
            ].astype(BF)
    scr[...] = jnp.zeros_like(scr)
    for k in range(3):
        for i in range(2):
            scr[i * 3 + k : i * 3 + k + 1, 0:32] = ein[k, i : i + 1, :]
    scr[6:9, 0:96] = gains[...]
    scr[9:11, 0:96] = special[...]
    hidden = mask[...].astype(F32)
    codes = targets[...]
    high = (codes >> 7).astype(F32)
    low = (codes & 127).astype(F32)
    for part, rows in enumerate((hidden, high, low)):
        for c in range(8):
            at = 16 + part * 4 + c // 2
            scr[at : at + 1, (c % 2) * 64 : (c % 2) * 64 + 64] = rows[c : c + 1, :]
    e_out[192:224, :] = scr[...].astype(BF)
    for copy in copies[6:]:
        copy.wait()
    l_out[:, 0:1152] = qkv[0].astype(BF)
    l_out[:, 1152:1536] = proj[0].astype(BF)
    l_out[:, 1536:3072] = fc1[0].astype(BF)
    for q in range(4):
        l_out[:, 3072 + q * 384 : 3456 + q * 384] = fc2[0, q * 96 : (q + 1) * 96, :].astype(BF)
    half = lax.axis_index("dp") & 1
    l_send[...] = l_out[:, pl.ds(pl.multiple_of(half * L_HALF, L_HALF), L_HALF)]


def pack(*arrays):
    return pl.pallas_call(
        pack_kernel,
        out_shape=(shape((E_ROWS, 128), BF), shape((96, L_WIDE), BF), shape((96, L_HALF), BF)),
        in_specs=[HB] * 10,
        out_specs=(VM, VM, VM),
        scratch_shapes=[pltpu.VMEM(array.shape, array.dtype) for array in arrays]
        + [pltpu.VMEM((32, 128), F32), pltpu.SemaphoreType.DMA((10,))],
        compiler_params=params(60),
        name="pack_weights",
    )(*arrays)


def pack_head_kernel(where, head, own, core, far, held, sems):
    copies = []
    for pos in range(4):
        start = pl.multiple_of((pos ^ where[0]) * VQ, VQ)
        for third in range(3):
            rows = slice(third * 32, third * 32 + 32)
            copies.append(
                pltpu.make_async_copy(
                    head.at[rows, pl.ds(start, VQ)], held.at[pos, rows], sems.at[pos, third]
                )
            )
    for copy in copies:
        copy.start()
    for pos in range(4):
        for copy in copies[pos * 3 : pos * 3 + 3]:
            copy.wait()
        piece = held[pos].astype(BF)
        if pos == 0:
            own[...] = piece
        elif pos == 1:
            core[...] = piece
        else:
            far[pos - 2] = piece


def pack_head(where, head):
    return pl.pallas_call(
        pack_head_kernel,
        out_shape=(shape((96, VQ), BF), shape((96, VQ), BF), shape((2, 96, VQ), BF)),
        in_specs=[SM, HB],
        out_specs=(VM, VM, VM),
        scratch_shapes=[pltpu.VMEM((4, 96, VQ), F32), pltpu.SemaphoreType.DMA((4, 3))],
        compiler_params=params(56),
        name="pack_head",
    )(where, head)


def choose_kernel(where, e_ref, code_ref, pick_ref, small_ref):
    upper = (iota((TOP, TOP), 0) <= iota((TOP, TOP), 1)).astype(F32).astype(BF)
    flags, codes = [], []
    for pos in range(4):
        rows = e_ref[pos, 208:224, :].astype(F32)
        flags.append(jnp.concatenate([rows[u : u + 1] for u in range(4)], 1))
        high = jnp.concatenate([rows[4 + u : 5 + u] for u in range(4)], 1)
        low = jnp.concatenate([rows[8 + u : 9 + u] for u in range(4)], 1)
        codes.append(high * 128.0 + low)
    stack = jnp.concatenate(flags + [jnp.zeros((4, TOP), F32)], 0).astype(BF)
    ranks = dot(stack, upper)
    for pos in range(4):
        rank = ranks[pos : pos + 1]
        chosen = (rank == (iota((CAP, TOP), 0) + 1).astype(F32)) & (flags[pos] > 0.0)
        picked = jnp.where(chosen, 1.0, 0.0)
        code = jnp.sum(picked * codes[pos], 1, keepdims=True)
        real = jnp.sum(picked, 1, keepdims=True) > 0.0
        column = jnp.where(real, code, -1.0).astype(I32)
        code_ref[pos] = jnp.broadcast_to(column, (CAP, 128))
        if pos == 0:
            pick_ref[...] = picked.astype(BF)
    for r in range(4):
        small_ref[:, r * 96 : (r + 1) * 96] = e_ref[r ^ where[0], 192:208, :].astype(F32)[:, 0:96]


def choose(where, e_all):
    return pl.pallas_call(
        choose_kernel,
        out_shape=(shape((4, CAP, 128), I32), shape((CAP, TOP), BF), shape((16, D))),
        in_specs=[SM, VM],
        out_specs=(VM, VM, VM),
        compiler_params=params(8),
        cost_estimate=cost(1e4, 1e3),
        name="choose_rows",
    )(where, e_all)


def point_forward_kernel(
    base, where, points, centers, neighbours, mask, e_ref, *refs,
):
    (
        x_ref, kept_ref, rel_ref, cen_ref, up_ref, slope_up_ref, hid_ref,
        turned, cloud_pts, cloud_cen, cloud_flag, w_in, w_out, w_place, mark,
        out_point,
    ) = refs[-16:]
    slope_ref = kept_ref.at[:, 0:D]
    inner_ref = kept_ref.at[:, D : D + PE]
    slope_in_ref = kept_ref.at[:, D + PE : D + 2 * PE]
    c = pl.program_id(0) + base

    @pl.when(c == base)
    def _():
        lane = iota((8, 128), 1)
        patch = lane & 63
        for q in range(16):
            spot = (patch & 3) * 32 + 2 * q + (lane >> 6)
            found = jnp.zeros((8, 128), I32)
            for v in range(16):
                part = jnp.take_along_axis(
                    neighbours[:, v * 128 : (v + 1) * 128], spot, axis=1, mode="promise_in_bounds"
                )
                found = jnp.where((patch >> 2) == v, part, found)
            for cloud in range(8):
                turned[cloud, 0:1, q * 128 : (q + 1) * 128] = found[cloud : cloud + 1]
        merged = jnp.zeros((16, 128), F32)
        for r in range(4):
            rank = r ^ where[0]
            rows = e_ref[rank, 192:208, :].astype(F32)
            merged = merged + jnp.where(
                iota((16, 128), 1) >> 5 == r, pltpu.roll(rows, r * 32, 1), 0.0
            )
            mark[:, r * 96 : (r + 1) * 96] = rows[:, 0:96]
            for j in range(3):
                lanes = slice(j * 128, j * 128 + 128)
                w_out[r * 32 : (r + 1) * 32, lanes] = e_ref[
                    rank, j * 32 : (j + 1) * 32, :
                ].astype(F32)
                w_place[r * 32 : (r + 1) * 32, lanes] = e_ref[
                    rank, (3 + j) * 32 : (4 + j) * 32, :
                ]
        out_point[...] = jnp.transpose(w_out[...]).astype(BF)
        for i in range(2):
            rows = jnp.concatenate([merged[i * 3 : i * 3 + 3], jnp.zeros((125, 128), F32)], 0)
            w_in[i] = jnp.transpose(rows)
        cloud_pts[...] = jnp.zeros_like(cloud_pts)
        flags = mask[...].astype(F32)
        for cloud in range(8):
            row = slice(cloud, cloud + 1)
            for k in range(3):
                cloud_pts[cloud, k : k + 1, :] = points[k, row, :]
            cloud_cen[cloud, 0:1, 0:64] = centers[row, :]
            cloud_cen[cloud, 0:1, 64:128] = centers[row, :]
            cloud_flag[cloud, 0:1, 0:64] = flags[row, :]

    def look_up(index):
        index = jnp.broadcast_to(index, (8, 128))
        low = index & 127
        high = index >> 7
        found = jnp.zeros((8, 128), F32)
        for k in range(8):
            part = jnp.take_along_axis(
                cloud_pts[c, :, k * 128 : (k + 1) * 128], low, axis=1, mode="promise_in_bounds"
            )
            found = jnp.where(high == k, part, found)
        return found

    centre = look_up(cloud_cen[c, 0:1, :])
    in_point = w_in[0, :, 0:8].astype(BF)
    in_centre = w_in[1, :, 0:8].astype(BF)
    total = jnp.zeros((D, 128), F32)
    for step in range(PATCHES * NB // CH):
        tiles = []
        for q in range(step * CH // 128, (step + 1) * CH // 128):
            near = look_up(turned[c, 0:1, q * 128 : (q + 1) * 128])
            tiles.append(near - centre)
        relative = jnp.concatenate(tiles, 1).astype(BF)
        at = slice(step * CH, (step + 1) * CH)
        rel_ref[0, :, at] = relative
        inner, slope = gelu_pair(dot(in_point, relative).astype(BF))
        inner_ref[0, :, at] = inner
        slope_in_ref[0, :, at] = slope
        value, slope = gelu_pair(dot(out_point[...], inner).astype(BF))
        slope_ref[0, :, at] = slope
        for q in range(CH // 128):
            total = total + value[:, q * 128 : (q + 1) * 128].astype(F32)
    centre_b = centre.astype(BF)
    cen_ref[0] = centre_b
    value, slope = gelu_pair(dot(in_centre, centre_b))
    up = value.astype(BF)
    up_ref[0] = up
    slope_up_ref[0] = slope
    place = dot(up, w_place[...], ((0,), (0,)))[0:PATCHES]
    both = jnp.transpose(total)
    diagonal = iota((PATCHES, PATCHES), 0) == iota((PATCHES, PATCHES), 1)
    flags = jnp.broadcast_to(cloud_flag[c, 0:1, 0:64], (PATCHES, PATCHES))
    hidden = jnp.sum(jnp.where(diagonal, flags, 0.0), 1, keepdims=True)
    hid_ref[...] = jnp.broadcast_to(hidden, (PATCHES, 128))
    patch = (both[0:PATCHES] + both[PATCHES:128]) * (1.0 / NB)
    x_ref[...] = jnp.where(hidden > 0.0, mark[10:11, :], patch) + place


def point_forward(where, points, centers, neighbours, mask, e_all, part, parts, kept=None):
    clouds = mask.shape[0] // parts
    tokens = PATCHES * NB

    def whole(array):
        return pl.BlockSpec(array.shape, lambda c: (0,) * array.ndim)

    def per(*dims):
        return pl.BlockSpec((1,) + dims, lambda c: (c, 0, 0))

    inputs = (points, centers, neighbours, mask, e_all)
    return pl.pallas_call(
        functools.partial(point_forward_kernel, part * clouds),
        grid=(clouds,),
        input_output_aliases={6: 1} if part else {},
        out_shape=(
            shape((clouds * PATCHES, D)),
            shape((clouds * parts, D + 2 * PE, tokens), BF),
            shape((clouds, 8, tokens), BF),
            shape((clouds, 8, 128), BF),
            shape((clouds, PE, 128), BF),
            shape((clouds, PE, 128)),
            shape((clouds * PATCHES, 128)),
        ),
        in_specs=[SM] + [whole(array) for array in inputs] + [HB] * (part > 0),
        out_specs=(
            pl.BlockSpec((PATCHES, D), lambda c: (c, 0)),
            pl.BlockSpec((1, D + 2 * PE, tokens), lambda c: (c + part * clouds, 0, 0)),
            per(8, tokens),
            per(8, 128),
            per(PE, 128),
            per(PE, 128),
            pl.BlockSpec((PATCHES, 128), lambda c: (c, 0)),
        ),
        scratch_shapes=[
            pltpu.VMEM((8, 8, tokens), I32),
            pltpu.VMEM((8, 8, 1024), F32),
            pltpu.VMEM((8, 8, 128), I32),
            pltpu.VMEM((8, 8, 128), F32),
            pltpu.VMEM((2, 128, PE), F32),
            pltpu.VMEM((PE, D), F32),
            pltpu.VMEM((PE, D), BF),
            pltpu.VMEM((16, D), F32),
            pltpu.VMEM((D, PE), BF),
        ],
        compiler_params=params(44),
        cost_estimate=cost(30e9, 20e6, 8e6),
        name="point_forward",
    )(where, *inputs, *([kept] if part else []))


def layer_weights(where, shards, w_main, w_two, whole):
    own, near, far_a, far_b, last_a, last_b = shards
    half = where[1] & 1
    for i, (first, second) in enumerate(((far_a, far_b), (last_a, last_b))):
        whole[i, :, pl.ds(pl.multiple_of(half * L_HALF, L_HALF), L_HALF)] = first[...]
        whole[i, :, pl.ds(pl.multiple_of((1 - half) * L_HALF, L_HALF), L_HALF)] = second[...]
    for pos, shard in enumerate((own, near, whole.at[0], whole.at[1])):
        rank = pos ^ where[0]
        w_main[pl.ds(pl.multiple_of(rank * 96, 96), 96), :] = shard[:, 0:3072]
        for q in range(4):
            rows = pl.ds(pl.multiple_of(rank * 384 + q * 96, 96), 96)
            w_two[rows, :] = shard[:, 3072 + q * 384 : 3456 + q * 384]


def norm(x):
    centred = x - jnp.mean(x, -1, keepdims=True)
    scale = lax.rsqrt(jnp.mean(centred * centred, -1, keepdims=True) + 1e-06)
    return centred * scale, scale


def norm_back(grad, x, gain):
    hat, scale = norm(x)
    d_gain = jnp.sum(grad * hat, 0, keepdims=True)
    inner = grad * gain
    d_x = scale * (
        inner - jnp.mean(inner, -1, keepdims=True) - hat * jnp.mean(inner * hat, -1, keepdims=True)
    )
    return d_x, d_gain


def cloud_rows(ref, start, lanes):
    return jnp.concatenate([ref[pl.ds(start, 64), lanes], ref[TOP:ROWS, lanes]], 0)


def lane_masks():
    first = (iota((1, 128), 1) < HEAD_DIM).astype(F32)
    return first.astype(BF), (1.0 - first).astype(BF)


def layer_forward_kernel(
    where, xa, xb, small, pick, s0, s1, s2, s3, s4, s5,
    m_ref, xo_ref, y_ref, qkv_ref, a_ref, o_ref, z_ref, act_ref, slope_ref, f_ref, w_main, w_two,
    x_all, o_cls, whole,
):
    layer_weights(where, (s0, s1, s2, s3, s4, s5), w_main, w_two, whole)
    x_all[0 : TOP // 2, :] = xa[...]
    x_all[TOP // 2 : TOP, :] = xb[...]
    opening = jnp.broadcast_to(small[9:10, :], (16, D))
    x_all[TOP:ROWS, :] = jnp.where(iota((16, D), 0) < 8, opening, 0.0)
    hat, _ = norm(x_all[...])
    y_ref[...] = (hat * small[6:7, :]).astype(BF)
    qkv_ref[...] = dot(y_ref[...], w_main[:, 0:1152]).astype(BF)
    o_cls[...] = jnp.zeros_like(o_cls)
    mask0, mask1 = lane_masks()

    def one_cloud(c, carry):
        start = pl.multiple_of(c * 64, 64)
        column = iota((160, 80), 1)
        allowed = (column < 64) | (column == c + 64)
        for p in range(3):
            q = cloud_rows(qkv_ref, start, slice(p * 128, p * 128 + 128))
            k = cloud_rows(qkv_ref, start, slice(384 + p * 128, 512 + p * 128))
            v = cloud_rows(qkv_ref, start, slice(768 + p * 128, 896 + p * 128))
            both = jnp.concatenate([q * mask0, q * mask1], 0)
            scores = dot(both, k, ((1,), (1,))) * HEAD_DIM**-0.5
            scores = jnp.where(allowed, scores, -1e30)
            top = jnp.max(scores, -1, keepdims=True)
            e = jnp.exp(scores - top)
            a = (e / jnp.sum(e, -1, keepdims=True)).astype(BF)
            a_ref[c * 3 + p] = a
            o = dot(a, v)
            pair = jnp.where(iota((80, 128), 1) < HEAD_DIM, o[0:80], o[80:160])
            lanes = slice(p * 128, p * 128 + 128)
            o_ref[pl.ds(start, 64), lanes] = pair[0:64].astype(BF)
            o_cls[:, lanes] += jnp.where(iota((16, 128), 0) == c, pair[64:80], 0.0)
        return carry

    lax.fori_loop(0, 8, one_cloud, 0, unroll=4)
    o_ref[TOP:ROWS, :] = o_cls[...].astype(BF)
    m_ref[...] = x_all[...] + dot(o_ref[...], w_main[:, 1152:1536])
    hat, _ = norm(m_ref[...])
    z_ref[...] = (hat * small[7:8, :]).astype(BF)
    for part in range(3):
        lanes = slice(part * 512, part * 512 + 512)
        hidden = dot(z_ref[...], w_main[:, 1536 + part * 512 : 2048 + part * 512])
        value, slope = gelu_pair(hidden)
        act_ref[:, lanes] = value.astype(BF)
        slope_ref[:, lanes] = slope.astype(BF)
    xo = m_ref[0:TOP, :] + dot(act_ref[0:TOP, :], w_two[...])
    xo_ref[...] = xo
    hat, _ = norm(xo)
    f_ref[...] = dot(pick[...], (hat * small[8:9, :]).astype(BF)).astype(BF)


def layer_forward(where, xp, small, pick, shards):
    return pl.pallas_call(
        layer_forward_kernel,
        out_shape=(
            shape((ROWS, D)),
            shape((TOP, D)),
            shape((ROWS, D), BF),
            shape((ROWS, 1152), BF),
            shape((24, 160, 80), BF),
            shape((ROWS, D), BF),
            shape((ROWS, D), BF),
            shape((ROWS, FF), BF),
            shape((ROWS, FF), BF),
            shape((CAP, D), BF),
            shape((D, 3072), BF),
            shape((FF, D), BF),
        ),
        in_specs=[SM] + [VM] * 10,
        out_specs=(VM,) * 12,
        scratch_shapes=[
            pltpu.VMEM((ROWS, D), F32),
            pltpu.VMEM((16, D), F32),
            pltpu.VMEM((2, 96, L_WIDE), BF),
        ],
        compiler_params=params(24),
        cost_estimate=cost(1e4, 1e3),
        name="layer_forward",
    )(where, *xp, small, pick, *shards)


def head_scores_kernel(where, f0, f1, *refs):
    if len(refs) == 9:
        pieces, (codes, e_ref, stat_ref, table, scores) = refs[:4], refs[4:]
        for pos, piece in enumerate(pieces):
            rows = pl.ds(pl.multiple_of((pos ^ where[0]) * 96, 96), 96)
            table[rows, :] = piece[...] if len(piece.shape) == 2 else piece[0]
        begin = 0
    else:
        table, codes, e_ref, stat_ref, scores = refs
        begin = 2
    base = where[0] * VQ
    for half, rows in enumerate((f0, f1)):
        best = jnp.full((CAP, 128), -jnp.inf, F32)
        for t in range(4):
            part = dot(rows[...], table[:, t * 512 : t * 512 + 512])
            scores[:, t * 512 : t * 512 + 512] = part
            for u in range(4):
                best = jnp.maximum(best, part[:, u * 128 : u * 128 + 128])
        top = jnp.max(best, -1, keepdims=True)
        code = codes[begin + half] - base
        total = jnp.zeros((CAP, 128), F32)
        aimed = jnp.zeros((CAP, 128), F32)
        for u in range(16):
            lanes = slice(u * 128, u * 128 + 128)
            part = scores[:, lanes]
            e = jnp.exp(part - top)
            e_ref[half, :, lanes] = e.astype(BF)
            total = total + e
            aimed = aimed + jnp.where(iota((CAP, 128), 1) + u * 128 == code, part, 0.0)
        lane = iota((CAP, 128), 1)
        both = jnp.where(
            lane == 0,
            top,
            jnp.where(
                lane == 1,
                jnp.sum(total, -1, keepdims=True),
                jnp.where(lane == 2, jnp.sum(aimed, -1, keepdims=True), 0.0),
            ),
        )
        both = jnp.concatenate([both, jnp.zeros((CAPL - CAP, 128), F32)], 0)
        stat_ref[half] = jnp.transpose(both)[0:8, :]


def head_scores(where, rows, pieces, codes):
    outs = [shape((2, CAP, VQ), BF), shape((2, 8, CAPL))]
    if len(pieces) == 4:
        outs.append(shape((D, VQ), BF))
    return pl.pallas_call(
        head_scores_kernel,
        out_shape=tuple(outs),
        in_specs=[SM] + [VM] * (3 + len(pieces)),
        out_specs=(VM,) * len(outs),
        scratch_shapes=[pltpu.VMEM((CAP, VQ), F32)],
        compiler_params=params(20),
        cost_estimate=cost(4e9, 4e6, 3e6),
        name="head_scores",
    )(where, *rows, *pieces, codes)


def head_back_kernel(begin, where, e_ref, t0, t1, t2, t3, codes, table, d_ref, keep, send, *losses):
    stats = (t0, t1, t2, t3)
    columns, aims = [], []
    for half in range(2):
        tops = [stats[q][half ^ (q & 1), 0:1, :] for q in range(4)]
        sums = [stats[q][half ^ (q & 1), 1:2, :] for q in range(4)]
        top = jnp.maximum(jnp.maximum(tops[0], tops[1]), jnp.maximum(tops[2], tops[3]))
        total = jnp.zeros((1, CAPL), F32)
        for q in range(4):
            total = total + sums[q] * jnp.exp(tops[q] - top)
        columns.append(jnp.exp(tops[0] - top) / total)
        aims.append(jnp.exp(t0[half, 2:3, :] - top) / total - 1.0)
        if half == 0:
            aimed = (t0[0, 2:3, :] + t1[1, 2:3, :]) + (t2[0, 2:3, :] + t3[1, 2:3, :])
            loss = top + jnp.log(total) - aimed
    block = jnp.concatenate(columns + aims + [loss, jnp.zeros((123, CAPL), F32)], 0)
    turned = jnp.transpose(block)[0:CAP, :]
    if begin == 0:
        loss = jnp.where(codes[0][:, 0:1] >= 0, turned[:, 4:5], 0.0)
        losses[0][...] = jnp.broadcast_to(jnp.sum(loss, 0, keepdims=True), (8, 128))
    base = where[0] * VQ
    for half in range(2):
        code = codes[begin + half]
        scale = jnp.where(code[:, 0:1] >= 0, turned[:, half : half + 1], 0.0)
        aim = turned[:, 2 + half : 3 + half]
        code = code - base
        for u in range(16):
            lanes = slice(u * 128, u * 128 + 128)
            hit = iota((CAP, 128), 1) + u * 128 == code
            grad = jnp.where(hit, aim, e_ref[half, :, lanes].astype(F32) * scale)
            d_ref[half, :, lanes] = grad.astype(BF)
        back = dot(d_ref[half], table[...], ((1,), (1,)))
        if half == 0:
            keep[...] = back
        else:
            send[...] = back.astype(BF)


def head_back(where, begin, e, stats, codes, table):
    outs = [shape((2, CAP, VQ), BF), shape((CAP, D)), shape((CAP, D), BF)]
    if begin == 0:
        outs.append(shape((8, 128)))
    return pl.pallas_call(
        functools.partial(head_back_kernel, begin),
        out_shape=tuple(outs),
        in_specs=[SM] + [VM] * 7,
        out_specs=(VM,) * len(outs),
        compiler_params=params(20),
        cost_estimate=cost(4e9, 6e6),
        name="head_back",
    )(where, e, *stats, codes, table)


def place_y(rel):
    return rel & 1, ((rel >> 1) & 1) * 2 + ((rel >> 2) & 1)


def place_z(rel):
    return (rel >> 1) & 1, (rel & 1) * 2 + ((rel >> 2) & 1)


def place_b(rel):
    return (rel >> 1) & 1, ((rel >> 2) & 1) * 2 + (rel & 1)


def head_grad_kernel(where, f0, f1, f2, f3, d0, d1, a_keep, a_send, b_keep, b_send, joined, held):
    for pos, rows in enumerate((f0, f1, f2, f3)):
        joined[:, pos * CAP : (pos + 1) * CAP] = jnp.transpose(rows[...].astype(F32)).astype(BF)
    for rel in range(SPLIT):
        lanes = pl.ds(pl.multiple_of((rel ^ where[1]) * 256, 256), 256)
        cols = jnp.concatenate([d0[0, :, lanes], d0[1, :, lanes], d1[0, :, lanes], d1[1, :, lanes]], 0)
        held[rel % 2] = dot(joined[...], cols).astype(BF)
        first_a, index_a = place_y(rel)
        first_b, index_b = place_b(rel)
        for pos in range(4):
            rows = held[rel % 2, pl.ds(pl.multiple_of((pos ^ where[0]) * 96, 96), 96), :]
            if pos < 2:
                ref, index = (a_send if first_a else a_keep), index_a
            else:
                ref, index = (b_send if first_b else b_keep), index_b
            for j in range(2):
                ref[index, pos & 1, j * 96 : j * 96 + 96, :] = rows[:, j * 128 : j * 128 + 128]


def head_grad(where, rows, *d):
    return pl.pallas_call(
        head_grad_kernel,
        out_shape=(shape((4, 2, H_PIECE, 128), BF),) * 4,
        in_specs=[SM] + [VM] * 6,
        out_specs=(VM,) * 4,
        scratch_shapes=[pltpu.VMEM((D, 4 * CAP), BF), pltpu.VMEM((2, D, 256), BF)],
        compiler_params=params(16),
        cost_estimate=cost(4e9, 8e6),
        name="head_grad",
    )(where, *rows, *d)


def hold_grad(held, block, grad):
    for r in range(4):
        held[r, block * 96 : block * 96 + 96, :] = grad[r * 96 : r * 96 + 96, :].astype(BF)


def spread_grad(where, held, keep, send, piece_rows):
    for pos in range(4):
        ref, far = (send if pos & 1 else keep), pos >> 1
        for rel in range(SPLIT):
            first, index = place_y(rel)
            start = pl.multiple_of((rel ^ where[1]) * piece_rows, 16)
            ref[far, first, index] = held[pos ^ where[0], pl.ds(start, piece_rows), :]


def ffn_backward_kernel(
    where, keep, rc, rx, pick, xo, m_ref, small, z_ref, act_ref, slope_ref, w_main, w_two,
    keep_ref, send_ref, dm_ref, sg_ref,
    d_hid, held,
):
    compact = keep[...] + rc[...].astype(F32) + rx[...].astype(F32)
    high = compact.astype(BF)
    low = (compact - high.astype(F32)).astype(BF)
    d_rows = dot(pick[...], high, ((0,), (0,))) + dot(pick[...], low, ((0,), (0,)))
    d_out, d_gain = norm_back(d_rows, xo[...], small[8:9, :])
    sg_ref[...] = jnp.zeros_like(sg_ref)
    sg_ref[1:2, :] = d_gain
    grad_b = d_out.astype(BF)
    for part in range(3):
        lanes = slice(part * 512, part * 512 + 512)
        back = dot(grad_b, w_two[lanes, :], ((1,), (1,)))
        d_hid[:, lanes] = (back * slope_ref[0:TOP, lanes].astype(F32)).astype(BF)
    d_fc2 = dot(jnp.transpose(d_out).astype(BF), act_ref[0:TOP, :])
    for j in range(3):
        for q in range(4):
            parts = [
                d_fc2[q * 96 : q * 96 + 96, r * 384 + j * 128 : r * 384 + j * 128 + 128]
                for r in range(4)
            ]
            hold_grad(held, 12 + j * 4 + q, jnp.concatenate(parts, 0))
    turned = jnp.transpose(z_ref[0:TOP, :].astype(F32)).astype(BF)
    for part in range(3):
        grad = dot(turned, d_hid[:, part * 512 : part * 512 + 512])
        for j in range(4):
            hold_grad(held, part * 4 + j, grad[:, j * 128 : j * 128 + 128])
    spread_grad(where, held, keep_ref, send_ref, F_PIECE)
    d_z = dot(d_hid[...], w_main[:, 1536:3072], ((1,), (1,)))
    d_m, d_gain = norm_back(d_z, m_ref[0:TOP, :], small[7:8, :])
    sg_ref[0:1, :] = d_gain
    dm_ref[...] = d_m + d_out


def ffn_backward(where, *arrays):
    return pl.pallas_call(
        ffn_backward_kernel,
        out_shape=(
            shape((2, 2, 4, F_PIECE, 128), BF),
            shape((2, 2, 4, F_PIECE, 128), BF),
            shape((TOP, D)),
            shape((8, D)),
        ),
        in_specs=[SM] + [VM] * 12,
        out_specs=(VM,) * 4,
        scratch_shapes=[
            pltpu.VMEM((TOP, FF), BF),
            pltpu.VMEM((4, F_ROWS, 128), BF),
        ],
        compiler_params=params(24),
        cost_estimate=cost(10e9, 10e6),
        name="ffn_backward",
    )(where, *arrays)


def attention_backward_kernel(
    where, dm_ref, sgf, xa, xb, small, y_ref, qkv_ref, a_ref, o_ref, hid_a, hid_b, w_main,
    keep_ref, send_ref, dx_ref, sg_ref,
    x_all, d_o, d_qkv, d_cls, held,
):
    x_all[0 : TOP // 2, :] = xa[...]
    x_all[TOP // 2 : TOP, :] = xb[...]
    opening = jnp.broadcast_to(small[9:10, :], (16, D))
    x_all[TOP:ROWS, :] = jnp.where(iota((16, D), 0) < 8, opening, 0.0)
    m_b = dm_ref[...].astype(BF)
    d_o[...] = dot(m_b, w_main[:, 1152:1536], ((1,), (1,))).astype(BF)
    d_cls[...] = jnp.zeros_like(d_cls)
    mask0, mask1 = lane_masks()

    def one_cloud(c, carry):
        start = pl.multiple_of(c * 64, 64)
        for p in range(3):
            lanes = slice(p * 128, p * 128 + 128)
            q = qkv_ref[pl.ds(start, 64), lanes]
            k = cloud_rows(qkv_ref, start, slice(384 + p * 128, 512 + p * 128))
            v = cloud_rows(qkv_ref, start, slice(768 + p * 128, 896 + p * 128))
            d = d_o[pl.ds(start, 64), lanes]
            q2 = jnp.concatenate([q * mask0, q * mask1], 0)
            d2 = jnp.concatenate([d * mask0, d * mask1], 0)
            a = jnp.concatenate([a_ref[c * 3 + p, 0:64, :], a_ref[c * 3 + p, 80:144, :]], 0)
            d_a = dot(d2, v, ((1,), (1,)))
            full = a.astype(F32)
            d_s = full * (d_a - jnp.sum(d_a * full, -1, keepdims=True)) * HEAD_DIM**-0.5
            d_s = d_s.astype(BF)
            d_q = dot(d_s, k)
            d_q = jnp.where(iota((64, 128), 1) < HEAD_DIM, d_q[0:64], d_q[64:128])
            d_k = dot(d_s, q2, ((0,), (0,)))
            d_v = dot(a, d2, ((0,), (0,)))
            d_qkv[pl.ds(start, 64), p * 128 : p * 128 + 128] = d_q.astype(BF)
            d_qkv[pl.ds(start, 64), 384 + p * 128 : 512 + p * 128] = d_k[0:64].astype(BF)
            d_qkv[pl.ds(start, 64), 768 + p * 128 : 896 + p * 128] = d_v[0:64].astype(BF)
            d_cls[:, 384 + p * 128 : 512 + p * 128] += d_k[64:80]
            d_cls[:, 768 + p * 128 : 896 + p * 128] += d_v[64:80]
        return carry

    lax.fori_loop(0, 8, one_cloud, 0, unroll=4)
    d_qkv[TOP:ROWS, :] = d_cls[...].astype(BF)
    turned = jnp.transpose(o_ref[0:TOP, :].astype(F32)).astype(BF)
    grad = dot(turned, m_b)
    for j in range(3):
        hold_grad(held, 9 + j, grad[:, j * 128 : j * 128 + 128])
    turned = jnp.transpose(y_ref[...].astype(F32)).astype(BF)
    for part in range(3):
        grad = dot(turned, d_qkv[:, part * 384 : part * 384 + 384])
        for j in range(3):
            hold_grad(held, part * 3 + j, grad[:, j * 128 : j * 128 + 128])
    spread_grad(where, held, keep_ref, send_ref, T_PIECE)
    d_y = dot(d_qkv[...], w_main[:, 0:1152], ((1,), (1,)))
    d_x, d_gain = norm_back(d_y, x_all[...], small[6:7, :])
    d_x = d_x + jnp.concatenate([dm_ref[...], jnp.zeros((16, D), F32)], 0)
    dx_ref[...] = d_x
    sg_ref[...] = jnp.zeros_like(sg_ref)
    sg_ref[6:7, :] = d_gain
    sg_ref[7:9, :] = sgf[0:2, :]
    sg_ref[9:10, :] = jnp.sum(d_x[TOP:ROWS], 0, keepdims=True)
    hidden = jnp.concatenate([hid_a[:, 0:1], hid_b[:, 0:1]], 0)
    sg_ref[10:11, :] = jnp.sum(jnp.where(hidden > 0.0, d_x[0:TOP], 0.0), 0, keepdims=True)


def attention_backward(where, *arrays):
    return pl.pallas_call(
        attention_backward_kernel,
        out_shape=(
            shape((2, 2, 4, T_PIECE, 128), BF),
            shape((2, 2, 4, T_PIECE, 128), BF),
            shape((ROWS, D)),
            shape((16, D)),
        ),
        in_specs=[SM] + [VM] * 12,
        out_specs=(VM,) * 4,
        scratch_shapes=[
            pltpu.VMEM((ROWS, D), F32),
            pltpu.VMEM((TOP, D), BF),
            pltpu.VMEM((ROWS, 1152), BF),
            pltpu.VMEM((16, 1152), F32),
            pltpu.VMEM((4, T_ROWS, 128), BF),
        ],
        compiler_params=params(20),
        cost_estimate=cost(10e9, 10e6),
        name="attention_backward",
    )(where, *arrays)


def point_backward_kernel(
    where, dx_ref, hid, kept_ref, rel_ref, cen_ref, up_ref, slope_up_ref, e_ref, *rest,
):
    c = pl.program_id(0)
    slope_ref = kept_ref.at[:, 0:D]
    inner_ref = kept_ref.at[:, D : D + PE]
    slope_in_ref = kept_ref.at[:, D + PE : D + 2 * PE]
    first, last = len(rest) == 5, len(rest) == 11
    w_out, spread, lift = rest[-3:]
    if first:
        d_out, d_in = rest[:2]
    elif last:
        start_out, start_in, sg_ref, loss_ref, mask, g_ref, d_out, d_in = rest[:8]
    else:
        start_out, start_in, d_out, d_in = rest[:4]

    @pl.when(c == 0)
    def _():
        for r in range(4):
            for i in range(2):
                for j in range(3):
                    w_out[i, r * 32 : (r + 1) * 32, j * 128 : (j + 1) * 128] = e_ref[
                        r ^ where[0], (i * 3 + j) * 32 : (i * 3 + j + 1) * 32, :
                    ]
        if first:
            d_out[...] = jnp.zeros_like(d_out)
            d_in[...] = jnp.zeros_like(d_in)
        else:
            d_out[...] = start_out[...]
            d_in[...] = start_in[...]

    across = ((1,), (1,))
    rows = dx_ref[...]
    place = rows.astype(BF)
    d_out[1] += dot(up_ref[0, :, 0:PATCHES], place)
    d_up = (dot(w_out[1], place, across) * slope_up_ref[0, :, 0:PATCHES]).astype(BF)
    d_in[1] += dot(d_up, cen_ref[0, :, 0:PATCHES], across)
    d_patch = jnp.where(hid[:, 0:1] > 0.0, 0.0, rows) * (1.0 / NB)
    turned = jnp.transpose(jnp.concatenate([d_patch, d_patch], 0))
    for step in range(PATCHES * NB // CH):
        at = slice(step * CH, (step + 1) * CH)
        for q in range(step * CH // 128, (step + 1) * CH // 128):
            lanes = slice(q * 128, q * 128 + 128)
            spread[:, lanes] = (turned * slope_ref[0, :, lanes].astype(F32)).astype(BF)
        back = dot(w_out[0], spread[:, at])
        lift[:, at] = (back * slope_in_ref[0, :, at].astype(F32)).astype(BF)
    d_out[0] += dot(inner_ref[0], spread[...], across)
    d_in[0] += dot(lift[...], rel_ref[0], across)
    if not last:
        return

    @pl.when(c == pl.num_programs(0) - 1)
    def _():
        lane = iota((8, 128), 1)
        seen = jnp.sum(jnp.sum(mask[...].astype(F32), 1, keepdims=True), 0, keepdims=True)
        ins = [
            jnp.transpose(jnp.concatenate([d_in[i], jnp.zeros((PE, 120), F32)], 1))[0:8]
            for i in range(2)
        ]
        for r in range(4):
            pos = r ^ where[0]
            pos = (pos & 1) * 2 + (pos >> 1)
            for i in range(2):
                for j in range(3):
                    g_ref[pos, (i * 3 + j) * 32 : (i * 3 + j + 1) * 32, :] = d_out[
                        i, r * 32 : (r + 1) * 32, j * 128 : (j + 1) * 128
                    ]
            g_ref[pos, 192:216, :] = jnp.zeros((24, 128), F32)
            turn = (128 - r * 32) % 128
            for i in range(2):
                rolled = ins[i] if turn == 0 else pltpu.roll(ins[i], turn, 1)
                rolled = jnp.where(lane < 32, rolled, 0.0)
                g_ref[pos, 192 + i * 3 : 195 + i * 3, :] = rolled[0:3]
            g_ref[pos, 198:203, 0:96] = sg_ref[6:11, r * 96 : (r + 1) * 96]
            g_ref[pos, 208:209, :] = loss_ref[0:1, :]
            g_ref[pos, 209:210, :] = jnp.broadcast_to(seen, (1, 128))


def point_backward(where, dx, kept, e_all, begin, count, start=(), last=()):
    big, rel, cen, up, slope_up, hid = kept
    local = begin % rel.shape[0]
    tokens = PATCHES * NB

    def whole(array):
        return pl.BlockSpec(array.shape, lambda c: (0,) * len(array.shape))

    def per(*dims):
        return pl.BlockSpec((1,) + dims, lambda c: (c + local, 0, 0))

    sums = (shape((2, PE, D)), shape((2, PE, 8)))
    more = (*start, *last)
    packed = shape((4, E_GRAD, 128))
    return pl.pallas_call(
        point_backward_kernel,
        grid=(count,),
        out_shape=packed if last else sums,
        in_specs=[
            SM,
            pl.BlockSpec((PATCHES, D), lambda c: (c + begin, 0)),
            pl.BlockSpec((PATCHES, 128), lambda c: (c + local, 0)),
            pl.BlockSpec((1, D + 2 * PE, tokens), lambda c: (c + begin, 0, 0)),
            per(8, tokens),
            per(8, 128),
            per(PE, 128),
            per(PE, 128),
            whole(e_all),
            *[whole(array) for array in more],
        ],
        out_specs=whole(packed) if last else tuple(whole(array) for array in sums),
        scratch_shapes=([pltpu.VMEM(array.shape, F32) for array in sums] if last else [])
        + [
            pltpu.VMEM((2, PE, D), BF),
            pltpu.VMEM((D, tokens), BF),
            pltpu.VMEM((PE, tokens), BF),
        ],
        compiler_params=params(44),
        cost_estimate=cost(6e9, 6e6),
        name="point_backward",
    )(where, dx, hid, big, rel, cen, up, slope_up, e_all, *more)


def squares_kernel(*refs):
    total = jnp.zeros((16, 128), F32)
    for ref in refs[:-2]:
        rows = ref.shape[-2]
        for lead in range(ref.shape[0] * (ref.shape[1] if len(ref.shape) == 4 else 1)):
            part = ref[divmod(lead, ref.shape[1])] if len(ref.shape) == 4 else ref[lead]
            part = part.astype(F32)
            total = total + jnp.sum((part * part).reshape(rows // 16, 16, 128), 0)
    part = refs[-2][0:208, :]
    total = total + jnp.sum((part * part).reshape(13, 16, 128), 0)
    total = jnp.sum(jnp.sum(total, 1, keepdims=True), 0, keepdims=True)
    refs[-1][...] = jnp.broadcast_to(total, (8, 128))


def squares(*arrays):
    return pl.pallas_call(
        squares_kernel,
        out_shape=shape((8, 128)),
        in_specs=[VM] * len(arrays),
        out_specs=VM,
        compiler_params=params(8),
        name="squares",
    )(*arrays)


def adam(grad, first, second, weight, factor, vector):
    rate = RATE_VECTOR if vector else RATE_MATRIX
    clipped = grad * factor
    first = BETA_ONE * first + (1 - BETA_ONE) * clipped
    second = BETA_TWO * second + (1 - BETA_TWO) * (clipped * clipped)
    level = second * (1.0 / (1 - BETA_TWO**STEP_NUMBER))
    root = level * lax.rsqrt(level) + EPSILON
    update = (first * (rate / (1 - BETA_ONE**STEP_NUMBER))) * pl.reciprocal(root)
    if vector:
        return first, second, weight - update
    return first, second, weight * (1.0 - rate * DECAY) - update


def clip_factor(s0, s1, e_ref):
    count = e_ref[209:210, :]
    length = jnp.sqrt(s0[0:1, :] + s1[0:1, :]) / count
    return jnp.minimum(1.0, CLIP / length) / count, length


def step_kernel(where, s0, s1, e_ref, f0, f1, t0, t1, a0, a1, b0, b1, *refs):
    ins, outs, scalars = refs[:27], refs[27:54], refs[54]
    done, joined, turned, sems = refs[55:82], refs[82], refs[83], refs[84]
    factor, length = clip_factor(s0, s1, e_ref)
    copies = []

    def send(which, at=None):
        for k in range(3):
            i = which * 3 + k
            source = done[i] if at is None else done[i].at[at]
            target = outs[i] if at is None else outs[i].at[at]
            copy = pltpu.make_async_copy(source, target, sems.at[len(copies)])
            copy.start()
            copies.append(copy)

    def update(which, at, grad, vector=False):
        w, m, v = (ins[which * 3 + k] for k in range(3))
        out = adam(grad, m[at], v[at], w[at], factor[:, 0 : grad.shape[-1]], vector)
        for k in range(3):
            done[which * 3 + k][at] = out[k]

    for piece in range(SPLIT):
        first, index = place_y(piece ^ where[1])
        rows = slice(T_ROWS + piece * F_PIECE, T_ROWS + (piece + 1) * F_PIECE)
        joined[rows, :] = jnp.where(first == 0, f0[index], f1[index])
        first, index = place_z(piece ^ where[1])
        rows = slice(piece * T_PIECE, (piece + 1) * T_PIECE)
        joined[rows, :] = jnp.where(first == 0, t0[index], t1[index])

    starts = {0: (2, 0), 9: (3, 9), 12: (4, 12)}
    which = base = 0
    for block in range(36):
        grad = joined[block * 96 : block * 96 + 96, :].astype(F32)
        if block >= 24:
            j, q = divmod(block - 24, 4)
            turned[q * 96 : q * 96 + 96, j * 128 : j * 128 + 128] = grad
            continue
        if block in starts:
            which, base = starts[block]
        j = block - base
        update(which, (0, slice(None), slice(j * 128, j * 128 + 128)), grad)
        if block in (8, 11, 23):
            send(which)
    grad = jnp.transpose(turned[...])
    for j in range(3):
        lanes = slice(j * 128, j * 128 + 128)
        update(5, (0, slice(None), lanes), grad[:, lanes])
    send(5)
    for i in range(2):
        for k in range(3):
            at = 192 + i * 3 + k
            update(0, (k, slice(i, i + 1)), e_ref[at : at + 1, 0:32])
        for j in range(3):
            block = i * 3 + j
            grad = e_ref[block * 32 : block * 32 + 32, :]
            update(1, (i, slice(None), slice(j * 128, j * 128 + 128)), grad)
    update(6, (slice(0, 3),), e_ref[198:201, 0:96], True)
    update(7, (slice(0, 2),), e_ref[201:203, 0:96], True)
    for which in (0, 1, 6, 7):
        send(which)
    scalars[0:1, :] = e_ref[208:209, :]
    scalars[1:2, :] = e_ref[209:210, :]
    scalars[2:3, :] = length
    for piece in range(32):
        quarter = (piece // SPLIT) ^ where[0]
        first_a, index_a = place_y((piece % SPLIT) ^ where[1])
        first_b, index_b = place_z((piece % SPLIT) ^ where[1])
        for j in range(2):
            lanes = slice(piece * 256 + j * 128, piece * 256 + j * 128 + 128)
            rows = slice(j * 96, j * 96 + 96)
            near = quarter & 1
            grad = jnp.where(
                quarter < 2,
                jnp.where(first_a == 0, a0[index_a, near, rows, :], a1[index_a, near, rows, :]),
                jnp.where(first_b == 0, b0[index_b, near, rows, :], b1[index_b, near, rows, :]),
            )
            update(8, (slice(None), lanes), grad.astype(F32))
        if piece % 4 == 3:
            send(8, (slice(None), slice((piece - 3) * 256, (piece + 1) * 256)))
    for copy in copies:
        copy.wait()


def step_all(where, sums, e, grads, states):
    outs = tuple(shape(array.shape) for array in states)
    return pl.pallas_call(
        step_kernel,
        out_shape=outs + (shape((8, 128)),),
        in_specs=[SM] + [VM] * (11 + len(states)),
        out_specs=(HB,) * len(outs) + (VM,),
        scratch_shapes=[pltpu.VMEM(array.shape, F32) for array in states]
        + [
            pltpu.VMEM((T_ROWS + F_ROWS, 128), BF),
            pltpu.VMEM((D, D), F32),
            pltpu.SemaphoreType.DMA((48,)),
        ],
        compiler_params=params(24),
        cost_estimate=cost(4e7, 3e7),
        name="step_all",
    )(where, *sums, e, *grads, *states)


def add(*parts):
    total = parts[0].astype(F32)
    for part in parts[1:]:
        total = total + part.astype(F32)
    return total.astype(BF)


def after(*arrays):
    return lax.optimization_barrier(arrays)


def body(dp, fsdp, *args):
    (
        points, centers, neighbours, mask, targets,
        embed_in, embed_in_m, embed_in_v, embed_out, embed_out_m, embed_out_v,
        qkv_w, qkv_m, qkv_v, proj_w, proj_m, proj_v, fc1_w, fc1_m, fc1_v, fc2_w, fc2_m, fc2_v,
        gains, gains_m, gains_v, special, special_m, special_v, head, head_m, head_v,
    ) = args
    rank = lax.axis_index("fsdp").astype(I32)
    group = lax.axis_index("dp").astype(I32)
    where = jnp.stack([rank, group % SPLIT])

    def swap(x, axis, bit):
        size = dp if axis == "dp" else fsdp
        return lax.ppermute(x, axis, [(i, i ^ bit) for i in range(size)])

    def higher(total):
        bit = SPLIT
        while bit < dp:
            total = add(total, swap(total, "dp", bit))
            bit *= 2
        return total

    embed_in, embed_in_m, embed_in_v = (
        jnp.transpose(array, (1, 0, 2)) for array in (embed_in, embed_in_m, embed_in_v)
    )
    e_own, l_own, l_send = pack(
        embed_in, embed_out, gains, special, mask, targets, qkv_w, proj_w, fc1_w, fc2_w
    )
    e_far = swap(e_own, "fsdp", 2)
    e_near = swap(e_own, "fsdp", 1)
    h_own, h_core, h_far = pack_head(where, head)
    e_far, l_send, h_own = after(e_far, l_send, h_own)
    l_far = swap(l_send, "fsdp", 2)
    e_all = jnp.stack([e_own, e_near, e_far, swap(e_far, "fsdp", 1)])
    xa, big, *kept_a = point_forward(where, points, centers, neighbours, mask, e_all, 0, 2)
    l_far, xa, e_all, l_own, h_far = after(l_far, xa, e_all, l_own, h_far)
    l_far_b = swap(l_far, "dp", 1)
    l_near = swap(l_own, "fsdp", 1)
    l_last = swap(l_far, "fsdp", 1)
    h_got = swap(h_far, "fsdp", 2)
    xb, big, *kept_b = point_forward(where, points, centers, neighbours, mask, e_all, 1, 2, big)
    l_far_b, xb, e_late = after(l_far_b, xb, e_all)
    codes, pick, small = choose(where, e_late)
    l_last_b = swap(l_far_b, "fsdp", 1)
    h_near = swap(h_core, "fsdp", 1)
    shards = (l_own, l_near, l_far, l_far_b, l_last, l_last_b)
    *kept, f_own, w_main, w_two = layer_forward(where, (xa, xb), small, pick, shards)
    m, xo, y, qkv, a, o, z, act, slope = kept
    f_far = swap(f_own, "fsdp", 2)
    f_near = swap(f_own, "fsdp", 1)
    h_got, f_near = after(h_got, f_near)
    pieces = (h_own, h_near, h_got, swap(h_got[1], "fsdp", 1))
    e01, stat01, table = head_scores(where, (f_own, f_near), pieces, codes)
    f_far, stat01, e01 = after(f_far, stat01, e01)
    f_last = swap(f_far, "fsdp", 1)
    near01, far01, last01 = (swap(stat01, "fsdp", pos) for pos in (1, 2, 3))
    e23, stat23 = head_scores(where, (f_far, f_last), (table,), codes)
    rows = (f_own, f_near, f_far, f_last)
    near23, far23, last23 = (swap(stat23, "fsdp", pos) for pos in (1, 2, 3))
    d23, keep23, send23 = head_back(where, 2, e23, (stat23, near23, far01, last01), codes, table)
    keep23, send23, far23, last23 = after(keep23, send23, far23, last23)
    got23 = swap(send23, "fsdp", 1)
    passed, far23 = after(add(keep23, got23), far23)
    got_far = swap(passed, "fsdp", 2)
    d01, keep, send, loss = head_back(where, 0, e01, (stat01, near01, far23, last23), codes, table)
    got = swap(send, "fsdp", 1)
    a_keep, a_send, b_keep, b_send = head_grad(where, rows, d01, d23)

    a_send, b_send, got_far, got = after(a_send, b_send, got_far, got)
    a_1 = swap(a_send, "dp", 1)
    b_1 = swap(b_send, "dp", 2)
    f_keep, f_send, dm, sgf = ffn_backward(
        where, keep, got, got_far, pick, xo, m, small, z, act, slope, w_main, w_two
    )
    a_1, b_1, f_send, dm = after(a_1, b_1, f_send, dm)
    a_2 = swap(add(a_keep[2:], a_1[2:]), "dp", 2)
    b_2 = swap(add(b_keep[2:], b_1[2:]), "dp", 4)
    f_core = swap(f_send, "fsdp", 1)
    f_core, dm = after(f_core, dm)
    f_x = swap(add(f_keep[1], f_core[1]), "fsdp", 2)
    t_keep, t_send, dx, sg = attention_backward(
        where, dm, sgf, xa, xb, small, y, qkv, a, o, kept_a[-1], kept_b[-1], w_main
    )
    a_2, b_2, f_x, t_send, dx = after(a_2, b_2, f_x, t_send, dx)
    t_core = swap(t_send, "fsdp", 1)
    f_low = add(f_keep[0], f_core[0], f_x)
    f_y = swap(f_low[1], "dp", 1)
    a_low = add(a_keep[:2], a_1[:2])
    b_low = add(b_keep[:2], b_1[:2])
    a_3 = swap(add(a_low[1], a_2[1]), "dp", 4)
    b_3 = swap(add(b_low[1], b_2[1]), "dp", 1)
    t_core, dx = after(t_core, dx)
    t_x = swap(add(t_keep[1], t_core[1]), "fsdp", 2)
    part = point_backward(where, dx, (big, *kept_a), e_all, 0, 3)
    a_3, b_3, t_x, part = after(a_3, b_3, t_x, part)
    ab_sum = higher(
        jnp.concatenate([add(a_low[0], a_2[0], a_3), add(b_low[0], b_2[0], b_3)], 0)
    )
    h_got = [swap(ab_sum[pos], "fsdp", pos) for pos in (1, 2, 3)]
    t_low = add(t_keep[0], t_core[0], t_x)
    t_y = swap(t_low[1], "dp", 1)
    part = point_backward(where, dx, (big, *kept_a), e_all, 3, 1, part)
    *h_got, f_y, t_y, part = after(*h_got, f_y, t_y, part)
    h_mine = jnp.stack([ab_sum[0], *h_got])
    h_two = swap(h_mine, "dp", 4)
    ft_low = jnp.concatenate([add(f_low[0], f_y), add(t_low[0], t_y)], 1)
    ft_z1 = swap(ft_low[2:], "dp", 2)
    e_grad = point_backward(where, dx, (big, *kept_b), e_all, 4, 4, part, (sg, loss, mask))
    h_two, ft_z1, e_grad = after(h_two, ft_z1, e_grad)
    e_core = swap(e_grad[2:], "fsdp", 1)
    h_both = jnp.stack([h_mine, h_two])
    a_both, b_both = h_both[:, 0:2], h_both[:, 2:4]
    a_pair = swap(a_both, "dp", 2)
    b_pair = swap(b_both, "dp", 1)
    ft_z2 = swap(add(ft_low[1], ft_z1[1]), "dp", 4)
    e_x = swap(e_grad[1] + e_core[1], "fsdp", 2)
    e_x, ft_z2, a_pair, b_pair = after(e_x, ft_z2, a_pair, b_pair)
    ft_sum = higher(add(ft_low[0], ft_z1[0], ft_z2))
    ft_two = swap(ft_sum, "dp", 4)
    a_four = jnp.concatenate([a_both, a_pair], 0)
    b_four = jnp.concatenate([b_both, b_pair], 0)
    b_end = swap(b_four, "dp", 2)
    a_end = swap(a_four, "dp", 1)
    e_sum = e_grad[0] + e_core[0] + e_x
    e_y = swap(e_sum, "dp", 1)
    e_y, ft_two = after(e_y, ft_two)
    ft_both = jnp.stack([ft_sum, ft_two])
    f_both, t_both = ft_both[:, :F_PIECE], ft_both[:, F_PIECE:]
    f_pair = swap(f_both, "dp", 2)
    t_pair = swap(t_both, "dp", 1)
    e_sum = e_sum + e_y
    e_z2 = swap(e_sum, "dp", 4)
    e_z2, f_pair, t_pair, a_end, b_end = after(e_z2, f_pair, t_pair, a_end, b_end)
    f_four = jnp.concatenate([f_both, f_pair], 0)
    t_four = jnp.concatenate([t_both, t_pair], 0)
    f_end = swap(f_four, "dp", 1)
    t_end = swap(t_four, "dp", 2)
    e_sum = e_sum + e_z2
    e_sum = e_sum + swap(e_sum, "dp", 2)
    bit = SPLIT
    while bit < dp:
        e_sum = e_sum + swap(e_sum, "dp", bit)
        bit *= 2
    grads = (f_four, f_end, t_four, t_end, a_four, a_end, b_four, b_end)

    sums = squares(*grads, e_sum)
    sums = sums + swap(sums, "fsdp", 1)
    sums = (sums, swap(sums, "fsdp", 2))
    states = (
        embed_in, embed_in_m, embed_in_v, embed_out, embed_out_m, embed_out_v,
        qkv_w, qkv_m, qkv_v, proj_w, proj_m, proj_v, fc1_w, fc1_m, fc1_v, fc2_w, fc2_m, fc2_v,
        gains, gains_m, gains_v, special, special_m, special_v, head, head_m, head_v,
    )
    *news, scalars = step_all(where, sums, e_sum, grads, states)
    news[:3] = [jnp.transpose(array, (1, 0, 2)) for array in news[:3]]
    return (*news, scalars[0, 0], scalars[1, 0], scalars[2, 0])


def solution(mesh):
    in_specs = (
        P(None, ("dp", "fsdp"), None),
        *[P(("dp", "fsdp"), None)] * 4,
        *[P(None, None, "fsdp")] * 3,
        *[P(None, "fsdp", None)] * 15,
        *[P(None, "fsdp")] * 6,
        *[P("fsdp", None)] * 3,
    )
    out_specs = in_specs[5:] + (P(), P(), P())
    step = functools.partial(body, mesh.shape["dp"], mesh.shape["fsdp"])
    return jax.shard_map(
        step, mesh=mesh, in_specs=in_specs, out_specs=out_specs, check_vma=False
    )
```
